256 devices in a mesh: role: 4 (over z_hi), slab: 64 (over z_lo, y, x, core).
Axes of the slice: x: 4, y: 4, z: 8 (z_hi: 4, z_lo: 2; z = z_hi * 2 + z_lo), core: 2. Of those that a mesh axis runs over, the one named last changes fastest.
Arguments:
- velocity: float32 [3, 32, 4096, 128], P(None, 'role', 'slab'), may hold values from -6 to 6
- anchors: int32 [64, 2], P('slab'), may hold values from 0 to 32
- slot_table: int32 [64, 2], P('slab'), may hold values from -1 to 63, as said below
- lift: float32 [3, 64], replicated, may hold values from -3.5 to 3.5
- mix: float32 [64, 64], replicated, may hold values from -0.75 to 0.75
- proj: float32 [3, 64], replicated, may hold values from -0.75 to 0.75
- spectral: float32 [4096, 64, 64], P(('role', 'slab')), may hold values from -0.75 to 0.75
Outputs:
- advanced: float32 [3, 32, 4096, 128], P(None, 'role', 'slab')
- patch_loss: float32 [64, 2], P('slab')
- grad_lift: float32 [3, 64], replicated
- grad_mix: float32 [64, 64], replicated
- grad_proj: float32 [3, 64], replicated
- grad_spectral: float32 [4096, 64, 64], P(('role', 'slab'))
The draws below stay inside these ranges and needn't reach their ends.
Inputs may be any that keep to these rules, and one draw needn't show every extreme that they name: anchors[g] gives the x and y offsets of patch g inside the slab of device g. `slot_table`: row t lists the patches that trainer t takes, -1 marking an empty slot; every patch index from 0 to 63 stands exactly once in the table, and at least one row is full.
All inputs are finite; a program needn't handle non-finite values.
Results may differ from the reference program's by a relative error of at most 0.0025.
Values may be sent and summed in bfloat16 or wider, within the bound.
A program may use at most 128 MiB of HBM per device.

```python
import math
import jax
import jax.numpy as jnp
from jax import lax

C = 64
MODES = 16
PATCH = 32
CX = 64
YW = 128
PS = 1
PMAX = 2
NX = 4096
N_PATCH = 64
N_SLAB = 64


def draw_slot_table(key, part):
    key = jax.random.fold_in(key, 7)
    total_slots = N_SLAB * PMAX
    shuffled = jax.random.permutation(key, jnp.arange(total_slots, dtype=jnp.int32))
    busiest = shuffled[0] // PMAX
    ranking = jnp.arange(total_slots, dtype=jnp.int32)
    scores = jnp.where(shuffled // PMAX == busiest, -1, ranking)
    chosen = shuffled[jnp.argsort(scores, stable=True)][:N_PATCH]
    table = jnp.full((total_slots,), -1, jnp.int32).at[chosen].set(jnp.arange(N_PATCH, dtype=jnp.int32))
    return table.reshape(N_SLAB, PMAX)


def place_ends(entries, own_key, smallest, largest):
    extent = entries.shape
    place = [jax.random.randint(jax.random.fold_in(own_key, axis), (), 0, extent[axis]) for axis in range(len(extent))]
    entries = entries.at[tuple(place)].set(smallest)
    longest = extent.index(max(extent))
    place[longest] = (place[longest] + 1) % extent[longest]
    return entries.at[tuple(place)].set(largest)


def shard_levels(rng, shape, shards, low, high):
    gain, own = 1.0, jax.random.fold_in(rng, 6)
    for axis_at, parts in shards:
        heights = jnp.exp(jax.random.uniform(jax.random.fold_in(own, axis_at), (parts,), jnp.float32, low / len(shards), high / len(shards)))
        gain = gain * jnp.repeat(heights, shape[axis_at] // parts).reshape([-1 if axis == axis_at else 1 for axis in range(len(shape))])
    return gain


def gaussian(stream_key, shape, spread, limit, split=(), kind=jnp.bfloat16):
    array = spread * jax.random.normal(stream_key, shape, jnp.float32)
    if split:
        array = array * shard_levels(stream_key, shape, split, -0.22, 0.18)
    return jnp.clip(array, -limit, limit).astype(kind)


def setup_inputs(seed: int = 0) -> dict:
    splits = jax.random.split(jax.random.key(seed), 8)
    velocity = gaussian(splits[0], (3, PATCH, NX, YW), 1.0, 6.0, ((1, 4), (2, 64)), jnp.float32)
    anchors = place_ends(jax.random.randint(splits[1], (N_PATCH, 2), 0, CX - PATCH + 1), jax.random.fold_in(splits[1], 1), 0, CX - PATCH).astype(jnp.int32)
    slot_table = draw_slot_table(jax.random.fold_in(splits[7], 71), 0)
    lift = gaussian(splits[3], (3, C), 3 ** -0.5, 3.5, (), jnp.float32)
    mix = gaussian(splits[4], (C, C), C ** -0.5, 0.75, (), jnp.float32)
    proj = gaussian(splits[5], (3, C), C ** -0.5, 0.75, (), jnp.float32)
    spectral = gaussian(splits[6], (MODES**3, C, C), C ** -0.5, 0.75, ((0, 256),), jnp.float32)
    return {"velocity": velocity, "anchors": anchors, "slot_table": slot_table, "lift": lift, "mix": mix, "proj": proj, "spectral": spectral}


time_step = 0.1
viscosity = 1.5
tiny_eps = 1e-06
exact = lax.Precision.HIGHEST

def stencil(extended):
    padded = jnp.pad(extended, ((0, 0), (0, 0), (0, 0), (1, 1)))
    centre = padded[:, 1:-1, 1:-1, 1:-1]
    z_next = padded[:, 2:, 1:-1, 1:-1]
    z_prev = padded[:, :-2, 1:-1, 1:-1]
    x_next = padded[:, 1:-1, 2:, 1:-1]
    x_prev = padded[:, 1:-1, :-2, 1:-1]
    y_next = padded[:, 1:-1, 1:-1, 2:]
    y_prev = padded[:, 1:-1, 1:-1, :-2]
    laplace = z_next + z_prev + x_next + x_prev + y_next + y_prev - 6.0 * centre
    carried = 0.5 * (centre[0] * (z_next - z_prev) + centre[1] * (x_next - x_prev) + centre[2] * (y_next - y_prev))
    return centre + time_step * (viscosity * laplace - carried)

def fourier_basis(count, length):
    order = lax.broadcasted_iota(jnp.int32, (count, length), 0)
    points = lax.broadcasted_iota(jnp.int32, (count, length), 1)
    freq = ((order + 1) // 2).astype(jnp.float32)
    angles = 2.0 * math.pi * freq * points.astype(jnp.float32) / length
    waves = jnp.where((order % 2 == 1) | (order == 0), jnp.cos(angles), jnp.sin(angles))
    return waves * jnp.where(order == 0, math.sqrt(1.0 / length), math.sqrt(2.0 / length))

def plane_basis(count, length):
    single = fourier_basis(count, length)
    return (single[:, None, :, None] * single[None, :, None, :]).reshape(count * count, length * length)

def advance(field):
    wrapped = jnp.concatenate([field[:, :, -1:], field, field[:, :, :1]], axis=2)
    return stencil(jnp.pad(wrapped, ((0, 0), (1, 1), (0, 0), (0, 0))))

def patch_error(lift, mix, proj, spectral, samples, answers):
    basis_z = fourier_basis(MODES, PATCH)
    basis_xy = plane_basis(MODES, PATCH)
    hidden = jnp.einsum('ic,zip->zcp', lift, samples, precision=exact)
    plane_coef = jnp.einsum('kp,zcp->zck', basis_xy, hidden, precision=exact)
    coeffs = jnp.einsum('qz,zck->qck', basis_z, plane_coef, precision=exact)
    flat = jnp.transpose(coeffs, (1, 0, 2)).reshape(hidden.shape[1], MODES ** 3)
    mixed_modes = jnp.einsum('im,mio->om', flat, spectral, precision=exact)
    back_modes = jnp.transpose(mixed_modes.reshape(hidden.shape[1], MODES, MODES * MODES), (1, 0, 2))
    plane_back = jnp.einsum('qz,qck->zck', basis_z, back_modes, precision=exact)
    spectral_part = jnp.einsum('kp,zck->zcp', basis_xy, plane_back, precision=exact)
    pre = spectral_part + jnp.einsum('co,zcp->zop', mix, hidden, precision=exact)
    output = jnp.einsum('jc,zcp->zjp', proj, jax.nn.gelu(pre), precision=exact)
    error = samples + output - answers
    return jnp.sum(error * error)

def reference(velocity, anchors, slot_table, lift, mix, proj, spectral):
    first = advance(velocity)
    advanced = advance(first)
    area = PATCH * PATCH

    def cut(field, which):
        x_start = (which // PS * CX + anchors[which, 0]).astype(jnp.int32)
        y_start = anchors[which, 1].astype(jnp.int32)
        piece = lax.dynamic_slice(field, (jnp.int32(0), jnp.int32(0), x_start, y_start), (3, PATCH, PATCH, PATCH))
        return jnp.transpose(piece.reshape(3, PATCH, area), (1, 0, 2)).astype(jnp.bfloat16)
    patch_ids = jnp.arange(N_PATCH, dtype=jnp.int32)
    inputs = lax.map(lambda which: cut(first, which), patch_ids)
    targets = lax.map(lambda which: cut(advanced, which), patch_ids)

    def accumulate(carry, pair):
        samples = pair[0].astype(jnp.float32)
        answers = pair[1].astype(jnp.float32)
        sse, pullback = jax.vjp(lambda w_one, w_two, w_three, w_four: patch_error(w_one, w_two, w_three, w_four, samples, answers), lift, mix, proj, spectral)
        grads = pullback(jnp.ones_like(sse))
        return (tuple((total + grad for total, grad in zip(carry, grads))), sse)
    start = (jnp.zeros_like(lift), jnp.zeros_like(mix), jnp.zeros_like(proj), jnp.zeros_like(spectral))
    raw_grads, sse_all = lax.scan(accumulate, start, (inputs, targets))
    normed = tuple((grad / jnp.sqrt(jnp.mean(grad * grad) + tiny_eps) for grad in raw_grads))
    cells = 3.0 * PATCH ** 3
    safe_ids = jnp.maximum(slot_table, 0)
    patch_loss = jnp.where(slot_table >= 0, sse_all[safe_ids] / cells, 0.0)
    return (advanced, patch_loss, normed[0], normed[1], normed[2], normed[3])
```

```python
import math

import jax
import jax.numpy as jnp
import numpy as np
from jax import lax
from jax.sharding import PartitionSpec as P

MODES = 16
PATCH = 32
AREA = PATCH * PATCH
PLANE_MODES = MODES * MODES

time_step = 0.1
viscosity = 1.5
tiny_eps = 1e-06
exact = lax.Precision.HIGHEST


def padded_2(value, sides, width):
    for axis, dim in sides:
        peers, length = (lax.axis_size(axis), value.shape[dim])
        up = [(i, (i + 1) % peers) for i in range(peers)]
        down = [(j, i) for i, j in up]
        last = lax.slice_in_dim(value, length - width, length, axis=dim)
        first = lax.slice_in_dim(value, 0, width, axis=dim)
        before = lax.ppermute(last, axis, up)
        after = lax.ppermute(first, axis, down)
        value = jnp.concatenate([before, value, after], axis=dim)
    return value


def stencil(extended):
    padded = jnp.pad(extended, ((0, 0), (0, 0), (0, 0), (1, 1)))
    centre = padded[:, 1:-1, 1:-1, 1:-1]
    z_next = padded[:, 2:, 1:-1, 1:-1]
    z_prev = padded[:, :-2, 1:-1, 1:-1]
    x_next = padded[:, 1:-1, 2:, 1:-1]
    x_prev = padded[:, 1:-1, :-2, 1:-1]
    y_next = padded[:, 1:-1, 1:-1, 2:]
    y_prev = padded[:, 1:-1, 1:-1, :-2]
    laplace = z_next + z_prev + x_next + x_prev + y_next + y_prev - 6.0 * centre
    carried = 0.5 * (
        centre[0] * (z_next - z_prev)
        + centre[1] * (x_next - x_prev)
        + centre[2] * (y_next - y_prev)
    )
    return centre + time_step * (viscosity * laplace - carried)


def fourier_table():
    order = np.arange(MODES)[:, None]
    points = np.arange(PATCH)[None, :]
    angles = 2.0 * math.pi * ((order + 1) // 2) * points / PATCH
    waves = np.where((order % 2 == 1) | (order == 0), np.cos(angles), np.sin(angles))
    return waves * np.where(order == 0, math.sqrt(1.0 / PATCH), math.sqrt(2.0 / PATCH))


PHI64 = fourier_table()
PHI = PHI64.astype(np.float32)
PLANE = np.einsum("ax,by->abxy", PHI64, PHI64).reshape(PLANE_MODES, AREA).astype(np.float32)


def normalise(grad, total_squares, count):
    return grad / jnp.sqrt(total_squares / count + tiny_eps)


def on_device(velocity, anchors, slot_table, lift, mix, proj, spectral):
    roles = lax.axis_size("role")
    slabs = lax.axis_size("slab")
    band = lax.axis_index("role")
    slab = lax.axis_index("slab")
    planes = velocity.shape[1]
    width = spectral.shape[1]
    part = width // roles
    highs = slabs // MODES

    def rim_mask(extended, rim):
        length = extended.shape[1]
        layer = lax.broadcasted_iota(jnp.int32, (1, length, 1, 1), 1)
        lower = (layer < rim) & (band == 0)
        upper = (layer >= length - rim) & (band == roles - 1)
        return jnp.where(lower | upper, 0.0, extended)

    def one_step(field):
        widened = padded_2(field, (("role", 1), ("slab", 2)), 1)
        return stencil(rim_mask(widened, 1))

    seen = jnp.einsum("ic,mco->imo", lift, spectral, precision=exact)
    seen = seen.reshape(3, MODES, roles, part).transpose(2, 0, 1, 3)
    seen = lax.all_to_all(seen, "role", split_axis=0, concat_axis=0, tiled=True)
    seen = seen.transpose(1, 2, 0, 3).reshape(3, MODES, roles * part)
    seen = lax.all_gather(seen, "slab", axis=0, tiled=False)
    seen = seen.reshape(highs, MODES, 3, MODES, roles, part).transpose(2, 1, 3, 4, 0, 5)
    seen = seen.reshape(3, PLANE_MODES, MODES, part)

    first = one_step(velocity)
    second = one_step(first)

    def cut(field):
        piece = lax.dynamic_slice(
            field,
            (jnp.int32(0), jnp.int32(0), anchors[0, 0], anchors[0, 1]),
            (3, planes, PATCH, PATCH),
        )
        return piece.reshape(3, planes, AREA).astype(jnp.bfloat16).astype(jnp.float32)

    given = cut(first)
    wanted = cut(second)

    plane_coef = jnp.einsum("izp,kp->izk", given, PLANE, precision=exact)
    plane_coef = lax.all_gather(plane_coef, "role", axis=1, tiled=True)
    coef = jnp.einsum("izk,qz->ikq", plane_coef, PHI, precision=exact)
    mixed = jnp.sum(coef[:, :, :, None] * seen, axis=0)
    back = jnp.einsum("kqc,qz->zkc", mixed, PHI, precision=exact)
    back = lax.all_to_all(back, "role", split_axis=0, concat_axis=2, tiled=True)
    lift_mix = jnp.einsum("ic,co->io", lift, mix, precision=exact)
    pre = jnp.einsum("kp,zko->zpo", PLANE, back, precision=exact) + jnp.einsum(
        "izp,io->zpo", given, lift_mix, precision=exact
    )
    activated, gelu_back = jax.vjp(jax.nn.gelu, pre)
    output = jnp.einsum("jc,zpc->jzp", proj, activated, precision=exact)
    error = given + output - wanted
    sse = jnp.sum(error * error)
    twice = 2.0 * error
    proj_part = jnp.einsum("jzp,zpc->jc", twice, activated, precision=exact)
    act_grad = jnp.einsum("jc,jzp->zpc", proj, twice, precision=exact)
    (pre_grad,) = gelu_back(act_grad)
    cross = jnp.einsum("izp,zpo->io", given, pre_grad, precision=exact)
    grad_plane = jnp.einsum("kp,zpc->zkc", PLANE, pre_grad, precision=exact)
    grad_plane = lax.all_to_all(grad_plane, "role", split_axis=2, concat_axis=0, tiled=True)
    grad_coef = jnp.einsum("zkc,qz->kqc", grad_plane, PHI, precision=exact)

    def to_owner(value):
        depth, tail = value.shape[0], value.shape[3]
        value = value.reshape(depth, MODES, MODES, roles, highs, tail).transpose(4, 1, 0, 2, 3, 5)
        value = value.reshape(slabs, depth * MODES * roles * tail)
        value = lax.all_to_all(value, "slab", split_axis=0, concat_axis=0, tiled=True)
        return value.reshape(slabs, depth, MODES, roles, tail)

    coef_owner = to_owner(coef[:, :, :, None])[..., 0]
    grad_owner = to_owner(grad_coef[None])[:, 0]
    crossed = jnp.einsum("piyr,pyrc->riyc", coef_owner, grad_owner, precision=exact)
    crossed = lax.all_to_all(crossed, "role", split_axis=0, concat_axis=0, tiled=True)
    crossed = crossed.transpose(1, 2, 0, 3).reshape(3, MODES, width)
    spectral_grad = jnp.einsum("ic,iyo->yco", lift, crossed, precision=exact)
    lift_part = jnp.einsum("yco,iyo->ic", spectral, crossed, precision=exact)
    squares = jnp.sum(spectral_grad * spectral_grad)
    own = lax.broadcasted_iota(jnp.int32, (slabs,), 0) == slab
    packed = jnp.concatenate(
        [
            cross.reshape(-1),
            proj_part.reshape(-1),
            lift_part.reshape(-1),
            jnp.where(own, sse, 0.0),
            jnp.broadcast_to(squares, (64,)),
        ]
    )
    packed = lax.psum(packed, ("role", "slab"))
    size = 3 * width
    cross = packed[:size].reshape(3, width)
    proj_total = packed[size : 2 * size].reshape(3, width)
    lift_total = packed[2 * size : 3 * size].reshape(3, width)
    sse_all = packed[3 * size : 3 * size + slabs]
    squares_total = packed[3 * size + slabs]
    lift_total = lift_total + jnp.einsum("co,io->ic", mix, cross, precision=exact)
    mix_total = jnp.einsum("ic,io->co", lift, cross, precision=exact)

    table = slot_table[0]
    chosen = table[:, None] == lax.broadcasted_iota(jnp.int32, (table.shape[0], slabs), 1)
    patch_loss = jnp.sum(jnp.where(chosen, sse_all[None, :], 0.0), axis=1) / (3.0 * PATCH**3)
    grad_lift = normalise(lift_total, jnp.sum(lift_total * lift_total), lift_total.size)
    grad_mix = normalise(mix_total, jnp.sum(mix_total * mix_total), mix_total.size)
    grad_proj = normalise(proj_total, jnp.sum(proj_total * proj_total), proj_total.size)
    grad_spectral = normalise(spectral_grad, squares_total, MODES**3 * width * width)
    return (second, patch_loss[None, :], grad_lift, grad_mix, grad_proj, grad_spectral)


def solution(mesh):
    return jax.shard_map(
        on_device,
        mesh=mesh,
        in_specs=(
            P(None, "role", "slab", None),
            P("slab", None),
            P("slab", None),
            P(),
            P(),
            P(),
            P(("role", "slab"), None, None),
        ),
        out_specs=(
            P(None, "role", "slab", None),
            P("slab", None),
            P(),
            P(),
            P(),
            P(("role", "slab"), None, None),
        ),
        check_vma=False,
    )
```

```python
import math

import jax
import jax.numpy as jnp
import numpy as np
from jax import lax
from jax.experimental import pallas as pl
from jax.experimental.pallas import tpu as pltpu
from jax.sharding import PartitionSpec as P

MODES = 16
PATCH = 32
AREA = PATCH * PATCH
ROLES = 4
SLABS = 64
LOW = 8
HIGH = 8
PLANES = 8
WIDTH = 64
PART = WIDTH // ROLES
SH = 4
TILE = 128
PAIRS = 3 * PLANES

time_step = 0.1
viscosity = 1.5
tiny_eps = 1e-06
exact = lax.Precision.HIGHEST
MESH = pl.DeviceIdType.MESH
NN = (((1,), (0,)), ((), ()))
NT = (((1,), (1,)), ((), ()))
TN = (((0,), (0,)), ((), ()))


def dot(a, b, dims=NN):
    return lax.dot_general(a, b, dims, precision=exact, preferred_element_type=jnp.float32)


def fourier_table():
    order = np.arange(MODES)[:, None]
    points = np.arange(PATCH)[None, :]
    angles = 2.0 * math.pi * ((order + 1) // 2) * points / PATCH
    waves = np.where((order % 2 == 1) | (order == 0), np.cos(angles), np.sin(angles))
    return waves * np.where(order == 0, math.sqrt(1.0 / PATCH), math.sqrt(2.0 / PATCH))


def tables():
    phi = fourier_table()
    plane = np.einsum("ax,hby->habxy", phi, phi.reshape(2, 8, PATCH)).reshape(256, AREA)
    phi_z = phi.reshape(ROLES, SH, ROLES, PLANES)
    eye2, eye3, eye16 = np.eye(2), np.eye(3), np.eye(PART)
    ones = np.ones(PART)
    spread = np.einsum("hg,rsbz,ij,c->hbzijsgrc", eye2, phi_z, eye3, ones).reshape(2 * ROLES * PAIRS, 3 * SH * TILE)
    inverse = np.einsum("hg,rsbz,cd->bhzcsgrd", eye2, phi_z, eye16).reshape(ROLES, 256, SH * TILE)
    channel = np.einsum("qp,z,cd->qzcpd", np.eye(ROLES), np.ones(PLANES), eye16).reshape(512, WIDTH)
    same = np.einsum("q,zy,c,i->qzcyi", np.ones(ROLES), np.eye(PLANES), ones, np.ones(3)).reshape(512, PAIRS)
    repeat = np.einsum("z,ij->izj", np.ones(PLANES), eye3).reshape(3, PAIRS)
    return [t.astype(np.float32) for t in (plane, spread, inverse, channel, same, repeat)]


def others(role, slab):
    low, high = slab % LOW, slab // LOW
    found = [("role", d, (role + d) % ROLES, slab) for d in range(1, ROLES)]
    found += [("high", d, role, (high + d) % HIGH * LOW + low) for d in range(1, HIGH)]
    found += [("low", d, role, high * LOW + (low + d) % LOW) for d in range(1, LOW)]
    return found


def send(src, dst, sems, at, role, slab):
    copy = pltpu.make_async_remote_copy(
        src_ref=src,
        dst_ref=dst,
        send_sem=sems.at[0, at],
        recv_sem=sems.at[1, at],
        device_id=(role, slab),
        device_id_type=MESH,
    )
    copy.start()
    return copy


ROWS = 96


def flow_kernel(vel, own_w, first_out, second_out, w_out, ext, mid, w_in, w_all, local_sem, z_sem, x_sem, c_sem, r_sem, h_sem, l_sem):
    role, slab = lax.axis_index("role"), lax.axis_index("slab")
    low, high = slab % LOW, slab // LOW
    sh, kxh = high // 2, high % 2
    after, before = (slab + 1) % SLABS, (slab + SLABS - 1) % SLABS

    own = pltpu.make_async_copy(vel, ext.at[:, pl.ds(2, PLANES), pl.ds(16, 64)], local_sem)
    own.start()

    barrier = pltpu.get_barrier_semaphore()

    def greet(to_role, to_slab):
        pl.semaphore_signal(barrier, inc=1, device_id=(to_role, to_slab), device_id_type=MESH)

    for _, _, to_role, to_slab in others(role, slab):
        greet(to_role, to_slab)
    greet(role, after)
    greet(role, before)

    @pl.when(role > 0)
    def _():
        greet(role - 1, after)
        greet(role - 1, before)

    @pl.when(role < ROLES - 1)
    def _():
        greet(role + 1, after)
        greet(role + 1, before)

    @pl.when((role == 0) | (role == ROLES - 1))
    def _():
        pl.semaphore_wait(barrier, 21)

    @pl.when((role > 0) & (role < ROLES - 1))
    def _():
        pl.semaphore_wait(barrier, 23)

    def remote(src, dst, sems, at, to_role, to_slab):
        return pltpu.make_async_remote_copy(
            src_ref=src,
            dst_ref=dst,
            send_sem=sems.at[0, at],
            recv_sem=sems.at[1, at],
            device_id=(to_role, to_slab),
            device_id_type=MESH,
        )

    def to_below(k):
        return remote(
            vel.at[:, pl.ds(k, 1)], ext.at[:, pl.ds(10 + k, 1), pl.ds(16, 64)], z_sem, k, role - 1, slab
        )

    def to_above(k):
        return remote(
            vel.at[:, pl.ds(7 - k, 1)], ext.at[:, pl.ds(1 - k, 1), pl.ds(16, 64)], z_sem, 2 + k, role + 1, slab
        )

    to_after = remote(
        vel.at[:, :, pl.ds(56, 8)], ext.at[:, pl.ds(2, PLANES), pl.ds(8, 8)], x_sem, 0, role, after
    )
    to_before = remote(
        vel.at[:, :, pl.ds(0, 8)], ext.at[:, pl.ds(2, PLANES), pl.ds(80, 8)], x_sem, 1, role, before
    )

    def corner(up, right, at):
        plane, slot = (7, 1) if up else (0, 10)
        row, place = (56, 8) if right else (0, 80)
        return remote(
            vel.at[:, pl.ds(plane, 1), pl.ds(row, 8)],
            ext.at[:, pl.ds(slot, 1), pl.ds(place, 8)],
            c_sem,
            at,
            role + 1 if up else role - 1,
            after if right else before,
        )

    @pl.when(role > 0)
    def _():
        to_below(0).start()
        corner(False, True, 0).start()
        corner(False, False, 1).start()

    @pl.when(role < ROLES - 1)
    def _():
        to_above(0).start()
        corner(True, True, 2).start()
        corner(True, False, 3).start()

    to_after.start()
    to_before.start()

    w_copies = [
        send(own_w.at[to_role], w_in.at[d], r_sem, d, to_role, slab)
        for kind, d, to_role, _ in others(role, slab)
        if kind == "role"
    ]

    @pl.when(role > 0)
    def _():
        to_below(1).start()

    @pl.when(role < ROLES - 1)
    def _():
        to_above(1).start()

    @pl.when(role == 0)
    def _():
        ext[:, pl.ds(0, 2)] = jnp.zeros((3, 2, ROWS, TILE), jnp.float32)

    @pl.when(role == ROLES - 1)
    def _():
        ext[:, pl.ds(10, 2)] = jnp.zeros((3, 2, ROWS, TILE), jnp.float32)

    mine = own_w[role]
    for copy in w_copies:
        copy.wait_recv()
    mine = mine + (w_in[1] + (w_in[2] + w_in[3]))
    w_all[:, sh, kxh, low] = mine
    h_copies = [
        send(w_all.at[:, sh, kxh, low], w_all.at[:, sh, kxh, low], h_sem, d, role, to_slab)
        for kind, d, _, to_slab in others(role, slab)
        if kind == "high"
    ]

    lane_80 = lax.broadcasted_iota(jnp.int32, (80, TILE), 1)
    lane_64 = lax.broadcasted_iota(jnp.int32, (64, TILE), 1)

    def advance(field, z, row, count, lane):
        centre = [field[c, z, pl.ds(row, count)] for c in range(3)]
        out = []
        for c in range(3):
            here = centre[c]
            z_next, z_prev = field[c, z + 1, pl.ds(row, count)], field[c, z - 1, pl.ds(row, count)]
            x_next, x_prev = field[c, z, pl.ds(row + 1, count)], field[c, z, pl.ds(row - 1, count)]
            y_next = jnp.where(lane == TILE - 1, 0.0, pltpu.roll(here, TILE - 1, 1))
            y_prev = jnp.where(lane == 0, 0.0, pltpu.roll(here, 1, 1))
            laplace = z_next + z_prev + x_next + x_prev + y_next + y_prev - 6.0 * here
            carried = 0.5 * (
                centre[0] * (z_next - z_prev) + centre[1] * (x_next - x_prev) + centre[2] * (y_next - y_prev)
            )
            out.append(here + time_step * (viscosity * laplace - carried))
        return out

    own.wait()
    to_after.wait_recv()
    to_before.wait_recv()

    def inner(z, carry):
        out = advance(ext, z, 8, 80, lane_80)
        for c in range(3):
            mid[c, z, pl.ds(8, 80)] = out[c]
        return carry

    lax.fori_loop(3, 9, inner, 0)

    @pl.when(role > 0)
    def _():
        to_above(0).wait_recv()
        corner(True, True, 2).wait_recv()
        corner(True, False, 3).wait_recv()

    @pl.when(role < ROLES - 1)
    def _():
        to_below(0).wait_recv()
        corner(False, True, 0).wait_recv()
        corner(False, False, 1).wait_recv()

    inner(2, 0)
    inner(9, 0)
    for z in range(PLANES):
        for c in range(3):
            first_out[c, z] = mid[c, z + 2, pl.ds(16, 64)]

    for copy in h_copies:
        copy.wait_recv()
    l_copies = [
        send(w_all.at[:, :, :, low], w_all.at[:, :, :, low], l_sem, d, role, to_slab)
        for kind, d, _, to_slab in others(role, slab)
        if kind == "low"
    ]

    @pl.when(role > 0)
    def _():
        to_above(1).wait_recv()
        out = advance(ext, 1, 16, 64, lane_64)
        for c in range(3):
            mid[c, 1, pl.ds(16, 64)] = out[c]

    @pl.when(role < ROLES - 1)
    def _():
        to_below(1).wait_recv()
        out = advance(ext, 10, 16, 64, lane_64)
        for c in range(3):
            mid[c, 10, pl.ds(16, 64)] = out[c]

    @pl.when(role == 0)
    def _():
        mid[:, 1, pl.ds(16, 64)] = jnp.zeros((3, 64, TILE), jnp.float32)

    @pl.when(role == ROLES - 1)
    def _():
        mid[:, 10, pl.ds(16, 64)] = jnp.zeros((3, 64, TILE), jnp.float32)

    def outer(z, carry):
        out = advance(mid, z, 16, 64, lane_64)
        for c in range(3):
            second_out[c, z - 2] = out[c]
        return carry

    lax.fori_loop(2, 10, outer, 0)

    for copy in l_copies:
        copy.wait_recv()
    w_out[...] = w_all[...]
    for copy in w_copies + h_copies + l_copies:
        copy.wait_send()
    to_after.wait_send()
    to_before.wait_send()

    @pl.when(role > 0)
    def _():
        to_below(0).wait_send()
        to_below(1).wait_send()
        corner(False, True, 0).wait_send()
        corner(False, False, 1).wait_send()

    @pl.when(role < ROLES - 1)
    def _():
        to_above(0).wait_send()
        to_above(1).wait_send()
        corner(True, True, 2).wait_send()
        corner(True, False, 3).wait_send()


def flow(vel, own_w):
    vmem = pl.BlockSpec(memory_space=pltpu.VMEM)
    anywhere = pl.BlockSpec(memory_space=pl.ANY)
    dma = pltpu.SemaphoreType.DMA
    return pl.pallas_call(
        flow_kernel,
        out_shape=(
            jax.ShapeDtypeStruct((3, PLANES, 64, TILE), jnp.float32),
            jax.ShapeDtypeStruct((3, PLANES, 64, TILE), jnp.float32),
            jax.ShapeDtypeStruct((3, SH, 2, LOW, 8, TILE), jnp.float32),
        ),
        in_specs=[anywhere, vmem],
        out_specs=(vmem, vmem, vmem),
        scratch_shapes=[
            pltpu.VMEM((3, 12, ROWS, TILE), jnp.float32),
            pltpu.VMEM((3, 12, ROWS, TILE), jnp.float32),
            pltpu.VMEM((ROLES, 3, 8, TILE), jnp.float32),
            pltpu.VMEM((3, SH, 2, LOW, 8, TILE), jnp.float32),
            dma,
            dma((2, 4)),
            dma((2, 2)),
            dma((2, 4)),
            dma((2, ROLES)),
            dma((2, HIGH)),
            dma((2, LOW)),
        ],
        compiler_params=pltpu.CompilerParams(
            collective_id=0, has_side_effects=True, vmem_limit_bytes=32 * 2**20
        ),
    )(vel, own_w)


root = math.sqrt(2.0 / math.pi)


def operator_kernel(
    given, wanted, weights, spectral, lift, lift_t, mix, proj, table, plane, spread, inverse, channel, same, repeat,
    loss_out, lift_out, mix_out, proj_out, spec_out,
    bands, a_send, a_mid, a_got, y_send, y_got, act, slope, g_send, g_got, m_send, m_mid, m_got, r_got, raw, s_role, s_high, s_low, point, out_w,
    band_sem, y_sem, g_sem, al_sem, ah_sem, ml_sem, mh_sem, r_sem, s_sem, sh_sem, sl_sem,
):
    role, slab = lax.axis_index("role"), lax.axis_index("slab")
    low, high = slab % LOW, slab // LOW
    sh, kxh = high // 2, high % 2
    group = others(role, slab)
    roles = [(d, to) for kind, d, to, _ in group if kind == "role"]
    highs = [(d, (high + d) % HIGH, to) for kind, d, _, to in group if kind == "high"]
    lows = [(d, (low + d) % LOW, to) for kind, d, _, to in group if kind == "low"]
    pending = []

    barrier = pltpu.get_barrier_semaphore()
    for _, _, to_role, to_slab in group:
        pl.semaphore_signal(barrier, inc=1, device_id=(to_role, to_slab), device_id_type=MESH)

    a = given[...]
    bands[role] = dot(a, plane[...], NT)
    pl.semaphore_wait(barrier, len(group))
    copies = [send(bands.at[role], bands.at[role], band_sem, d, to, slab) for d, to in roles]
    pending += copies

    seen = dot(lift[...], mix[...])
    point_rows = dot(dot(channel[...], seen, NT), repeat[...]) * same[...]
    out_rows = dot(dot(channel[...], proj[...], NT), repeat[...]) * same[...]

    for copy in copies:
        copy.wait_recv()
    every = jnp.concatenate([bands[b] for b in range(ROLES)], axis=0)
    halves = jnp.concatenate([every[:, :TILE], every[:, TILE:]], axis=0)
    coef = dot(halves, spread[...], TN)
    mixed = []
    for s in range(SH):
        total = None
        for i in range(3):
            at = (i * SH + s) * TILE
            part = coef[:, at : at + TILE]
            a_send[i, s] = part.reshape(2, LOW, 8, TILE)
            term = part * weights[i, s].reshape(TILE, TILE)
            total = term if total is None else total + term
        mixed.append(total)
    mixed = jnp.concatenate(mixed, axis=1)

    def back(to):
        y_send[to] = dot(inverse[to], mixed, NT)

    y_copies = []
    for d, to in roles:
        back(to)
        y_copies.append(send(y_send.at[to], y_got.at[role], y_sem, d, to, slab))
    pending += y_copies

    al_copies = [send(a_send.at[:, :, :, at], a_mid.at[low], al_sem, d, role, to) for d, at, to in lows]
    pending += al_copies
    a_mid[low] = a_send[:, :, :, low]
    back(role)
    y_got[role] = y_send[role]

    point[...] = point_rows.reshape(ROLES, TILE, PAIRS)
    out_w[...] = out_rows.reshape(ROLES, TILE, PAIRS)

    def forward(q):
        rows = jnp.concatenate([y_got[q, :TILE], y_got[q, TILE:]], axis=1)
        slope[q] = dot(rows, plane[...]) + dot(point[q], a)

        def gelu(k, carry):
            at = pl.ds(pl.multiple_of(k * 8, 8), 8)
            x = slope[q, at]
            square = x * x
            t = jnp.tanh(x * (root + (root * 0.044715) * square))
            half = 0.5 + 0.5 * t
            act[q, at] = x * half
            slope[q, at] = half + x * (half * (1.0 - t)) * (root + (root * 3.0 * 0.044715) * square)
            return carry

        lax.fori_loop(0, TILE // 8, gelu, 0)
        return dot(out_w[q], act[q], TN)

    out = forward(role)
    for (d, _), copy in zip(roles, y_copies):
        copy.wait_recv()
        out = out + forward((role + ROLES - d) % ROLES)

    for copy in al_copies:
        copy.wait_recv()
    ah_copies = [
        send(a_mid.at[:, :, at // 2, at % 2], a_got.at[high], ah_sem, d, role, to) for d, at, to in highs
    ]
    pending += ah_copies

    error = a + out - wanted[...]
    twice = 2.0 * error

    def backward(q):
        g = dot(out_w[q], twice) * slope[q]
        slope[q] = g
        g_send[q] = dot(g, plane[...], NT)

    g_copies = []
    for d, to in roles:
        backward(to)
        g_copies.append(send(g_send.at[to], g_got.at[role], g_sem, d, to, slab))
    pending += g_copies
    backward(role)
    g_got[role] = g_send[role]

    a_got[high] = a_mid[:, :, sh, kxh]

    def cells(left, right):
        total = jnp.concatenate([dot(right[q], left, NT) for q in range(ROLES)], axis=0) * same[...]
        return dot(dot(repeat[...], total, NT), channel[...])

    cross = cells(a, slope)
    proj_part = cells(twice, act)
    sse = jnp.sum(error * error, keepdims=True)

    for copy in g_copies:
        copy.wait_recv()
    stacked = jnp.concatenate([g_got[b][:, h * TILE : (h + 1) * TILE] for b in range(ROLES) for h in range(2)], axis=0)
    grad = dot(stacked, inverse[...].reshape(ROLES * 256, SH * TILE), TN)
    for s in range(SH):
        m_send[s] = grad[:, s * TILE : (s + 1) * TILE].reshape(2, LOW, 8, TILE)
    ml_copies = [send(m_send.at[:, :, at], m_mid.at[low], ml_sem, d, role, to) for d, at, to in lows]
    m_mid[low] = m_send[:, :, low]
    for copy in ml_copies:
        copy.wait_recv()
    mh_copies = [
        send(m_mid.at[:, at // 2, at % 2], m_got.at[high], mh_sem, d, role, to) for d, at, to in highs
    ]
    pending += ml_copies + mh_copies
    m_got[high] = m_mid[:, sh, kxh]
    for copy in ah_copies + mh_copies:
        copy.wait_recv()

    def patch(k, carry):
        g = m_got[k // LOW, k % LOW]
        return tuple(carry[i] + a_got[k // LOW, k % LOW, i] * g for i in range(3))

    zero = jnp.zeros((8, TILE), jnp.float32)
    crossed = lax.fori_loop(0, SLABS, patch, (zero, zero, zero))
    for i in range(3):
        r_got[role, i] = crossed[i]
    r_copies = [send(r_got.at[role], r_got.at[role], r_sem, d, to, slab) for d, to in roles]
    pending += r_copies
    source = lax.broadcasted_iota(jnp.int32, (ROLES * TILE, TILE), 0)
    target = lax.broadcasted_iota(jnp.int32, (ROLES * TILE, TILE), 1)
    pick = (
        (source // TILE == target % WIDTH // PART)
        & (source % TILE // WIDTH == target // WIDTH)
        & (source % WIDTH // PART == role)
        & (source % PART == target % PART)
    )
    pick = jnp.where(pick, 1.0, 0.0)
    for copy in r_copies:
        copy.wait_recv()
    joined = jnp.concatenate([r_got[q].reshape(PAIRS, TILE) for q in range(ROLES)], axis=1)
    joined = dot(joined, pick)

    squares = jnp.zeros((WIDTH, TILE), jnp.float32)
    columns = lift_t[...]
    lift_sum = [jnp.zeros((WIDTH, WIDTH), jnp.float32)] * 3
    for k in range(8):
        rows = [joined[i * 8 + k : i * 8 + k + 1] for i in range(3)]
        value = columns[:, 0:1] * rows[0] + columns[:, 1:2] * rows[1] + columns[:, 2:3] * rows[2]
        raw[k] = value
        squares = squares + value * value
        for i in range(3):
            lift_sum[i] = lift_sum[i] + (
                spectral[k] * rows[i][:, :WIDTH] + spectral[8 + k] * rows[i][:, WIDTH:]
            )
    row = lax.broadcasted_iota(jnp.int32, (8, WIDTH), 0)
    lift_rows = zero[:, :WIDTH]
    for i in range(3):
        lift_rows = lift_rows + dot(jnp.where(row == 3 + i, 1.0, 0.0), lift_sum[i], NT)
    full = lax.broadcasted_iota(jnp.int32, (8, TILE), 0)
    lane = lax.broadcasted_iota(jnp.int32, (8, TILE), 1)
    blank = jnp.zeros((5, WIDTH), jnp.float32)
    left = jnp.concatenate([cross, blank], axis=0) + lift_rows
    right = jnp.concatenate([proj_part, blank], axis=0)
    tile = jnp.concatenate([left, right], axis=1)
    tile = tile + jnp.where((full == 6) & (lane == slab), sse, 0.0)
    tile = tile + jnp.where(full == 7, jnp.sum(squares, keepdims=True), 0.0)

    s_role[role] = tile
    copies = [send(s_role.at[role], s_role.at[role], s_sem, d, to, slab) for d, to in roles]
    pending += copies
    for copy in copies:
        copy.wait_recv()
    s_high[high] = (s_role[0] + s_role[1]) + (s_role[2] + s_role[3])
    copies = [send(s_high.at[high], s_high.at[high], sh_sem, d, role, to) for d, _, to in highs]
    pending += copies
    for copy in copies:
        copy.wait_recv()
    s_low[low] = jnp.sum(s_high[...], axis=0)
    copies = [send(s_low.at[low], s_low.at[low], sl_sem, d, role, to) for d, _, to in lows]
    pending += copies
    for copy in copies:
        copy.wait_recv()
    tile = jnp.sum(s_low[...], axis=0)

    def normal(total):
        mean = jnp.sum(total * total, keepdims=True) / total.size
        return total / jnp.sqrt(mean + tiny_eps)

    cross = tile[0:3, :WIDTH]
    proj_out[...] = normal(tile[0:3, WIDTH:])
    lift_out[...] = normal(tile[3:6, :WIDTH] + dot(cross, mix[...], NT))
    mix_out[...] = normal(dot(lift[...], cross, TN))
    scale = jnp.sqrt(tile[7:8, 0:1] / (MODES**3 * WIDTH * WIDTH) + tiny_eps)
    for k in range(8):
        value = raw[k] / scale
        spec_out[k] = value[:, :WIDTH]
        spec_out[8 + k] = value[:, WIDTH:]
    losses = tile[6:7, :] / (3.0 * PATCH**3)
    lanes = lax.broadcasted_iota(jnp.int32, (1, TILE), 1)
    found = [jnp.sum(jnp.where(lanes == table[0:1, k : k + 1], losses, 0.0), axis=1, keepdims=True) for k in range(2)]
    loss_out[...] = jnp.concatenate(found, axis=1)
    for copy in pending:
        copy.wait_send()


def operator(given, wanted, weights, spectral, lift, mix, proj, table):
    vmem = pl.BlockSpec(memory_space=pltpu.VMEM)
    dma = pltpu.SemaphoreType.DMA

    def room(*shape):
        return pltpu.VMEM(shape, jnp.float32)

    def result(*shape):
        return jax.ShapeDtypeStruct(shape, jnp.float32)

    return pl.pallas_call(
        operator_kernel,
        out_shape=(
            result(1, 2),
            result(3, WIDTH),
            result(WIDTH, WIDTH),
            result(3, WIDTH),
            result(MODES, WIDTH, WIDTH),
        ),
        in_specs=[vmem] * 15,
        out_specs=(vmem,) * 5,
        scratch_shapes=[
            room(ROLES, PAIRS, 256),
            room(3, SH, 2, LOW, 8, TILE),
            room(LOW, 3, SH, 2, 8, TILE),
            room(HIGH, LOW, 3, 8, TILE),
            room(ROLES, 256, TILE),
            room(ROLES, 256, TILE),
            room(ROLES, TILE, AREA),
            room(ROLES, TILE, AREA),
            room(ROLES, TILE, 256),
            room(ROLES, TILE, 256),
            room(SH, 2, LOW, 8, TILE),
            room(LOW, SH, 2, 8, TILE),
            room(HIGH, LOW, 8, TILE),
            room(ROLES, 3, 8, TILE),
            room(8, WIDTH, TILE),
            room(ROLES, 8, TILE),
            room(HIGH, 8, TILE),
            room(LOW, 8, TILE),
            room(ROLES, TILE, PAIRS),
            room(ROLES, TILE, PAIRS),
            dma((2, ROLES)),
            dma((2, ROLES)),
            dma((2, ROLES)),
            dma((2, LOW)),
            dma((2, HIGH)),
            dma((2, LOW)),
            dma((2, HIGH)),
            dma((2, ROLES)),
            dma((2, ROLES)),
            dma((2, HIGH)),
            dma((2, LOW)),
        ],
        compiler_params=pltpu.CompilerParams(
            collective_id=1, has_side_effects=True, vmem_limit_bytes=48 * 2**20
        ),
    )(given, wanted, weights, spectral, lift, lift.T, mix, proj, table, *(jnp.asarray(t) for t in tables()))


def on_device(velocity, anchors, slot_table, lift, mix, proj, spectral):
    seen = jnp.einsum("ic,mco->imo", lift, spectral, precision=exact)
    seen = seen.reshape(3, 2, 8, ROLES, PART).transpose(3, 0, 2, 1, 4)[:, :, :, :, None, :]
    place = lax.broadcasted_iota(jnp.int32, (1, 1, 1, 1, ROLES, 1), 4) == lax.axis_index("role")
    seen = jnp.where(place, seen, 0.0).reshape(ROLES, 3, 8, TILE)
    first, second, weights = flow(velocity, seen)

    def cut(field):
        piece = lax.dynamic_slice(
            field,
            (jnp.int32(0), jnp.int32(0), anchors[0, 0], anchors[0, 1]),
            (3, PLANES, PATCH, PATCH),
        )
        piece = piece.astype(jnp.bfloat16).astype(jnp.float32)
        return jnp.transpose(piece.reshape(3, PLANES, AREA), (1, 0, 2)).reshape(PAIRS, AREA)

    grads = operator(cut(first), cut(second), weights, spectral, lift, mix, proj, slot_table)
    return (second, *grads)


def solution(mesh):
    return jax.shard_map(
        on_device,
        mesh=mesh,
        in_specs=(
            P(None, "role", "slab", None),
            P("slab", None),
            P("slab", None),
            P(),
            P(),
            P(),
            P(("role", "slab"), None, None),
        ),
        out_specs=(
            P(None, "role", "slab", None),
            P("slab", None),
            P(),
            P(),
            P(),
            P(("role", "slab"), None, None),
        ),
        check_vma=False,
    )
```

```python
import math

import jax
import jax.numpy as jnp
import numpy as np
from jax import lax
from jax.experimental import pallas as pl
from jax.experimental.pallas import tpu as pltpu
from jax.sharding import PartitionSpec as P

MODES = 16
PATCH = 32
AREA = PATCH * PATCH
ROLES = 4
SLABS = 64
YX = 16
CREW = 16
PLANES = 8
WIDTH = 64
PART = WIDTH // ROLES
SH = 4
TILE = 128
PAIRS = 3 * PLANES

time_step = 0.1
viscosity = 1.5
tiny_eps = 1e-06
exact = lax.Precision.HIGHEST
MESH = pl.DeviceIdType.MESH
root = math.sqrt(2.0 / math.pi)
NN = (((1,), (0,)), ((), ()))
NT = (((1,), (1,)), ((), ()))
TN = (((0,), (0,)), ((), ()))


def dot(a, b, dims=NN):
    return lax.dot_general(a, b, dims, precision=exact, preferred_element_type=jnp.float32)


def split(value):
    high = value.astype(jnp.bfloat16)
    return high, (value - high.astype(jnp.float32)).astype(jnp.bfloat16)


def pass_(a, b, dims):
    return lax.dot_general(a, b, dims, preferred_element_type=jnp.float32)


def dot3(a, b, dims=NN):
    return pass_(a[0], b[0], dims) + (pass_(a[0], b[1], dims) + pass_(a[1], b[0], dims))


def dot2(a, exact_b, dims=NN):
    return pass_(a[0], exact_b, dims) + pass_(a[1], exact_b, dims)


def fourier_table():
    order = np.arange(MODES)[:, None]
    points = np.arange(PATCH)[None, :]
    angles = 2.0 * math.pi * ((order + 1) // 2) * points / PATCH
    waves = np.where((order % 2 == 1) | (order == 0), np.cos(angles), np.sin(angles))
    return waves * np.where(order == 0, math.sqrt(1.0 / PATCH), math.sqrt(2.0 / PATCH))


def pair(table):
    table = table.astype(np.float32)
    high = table.astype(jnp.bfloat16)
    return jnp.asarray(np.stack([high, (table - high.astype(np.float32)).astype(jnp.bfloat16)]))


def tables():
    phi = fourier_table()
    over_x = phi.reshape(2, 4, 2, 4, 8)
    over_y = phi.reshape(2, 8, PATCH)
    plane = np.einsum("axchl,gky->gcaxklhy", over_x, over_y).reshape(256, AREA)
    phi_z = phi.reshape(ROLES, SH, ROLES, PLANES)
    eye2, eye3, eye4, eye16 = np.eye(2), np.eye(3), np.eye(ROLES), np.eye(PART)
    ones = np.ones(PART)
    spread = np.einsum("hg,rsbz,ij,c->hbzijsgrc", eye2, phi_z, eye3, ones).reshape(2 * ROLES * PAIRS, 3 * SH * TILE)
    short = np.einsum("hg,rsbz,ij->hbzisjgr", eye2, phi_z, eye3).reshape(2 * ROLES * PAIRS, SH, 24)
    short = np.pad(short, ((0, 0), (0, 0), (0, TILE - 24))).reshape(-1, SH * TILE)
    inverse = np.einsum("hg,rsbz,cd->bhzcsgrd", eye2, phi_z, eye16).reshape(ROLES * 256, SH * TILE)
    expand = np.einsum("ij,hg,rs,c->ihrjgsc", eye3, eye2, eye4, ones).reshape(24, 3 * TILE)
    expand = np.pad(expand, ((0, TILE - 24), (0, 0)))
    sort = np.einsum("ij,hg,rs,cd->ihrcsjgd", eye3, eye2, eye4, eye16).reshape(3 * TILE, ROLES, 96)
    sort = np.pad(sort, ((0, 0), (0, 0), (0, TILE - 96))).reshape(3 * TILE, ROLES * TILE)
    return [pair(plane), pair(np.concatenate([spread, short], axis=1)), pair(inverse), jnp.asarray(expand, jnp.bfloat16), jnp.asarray(sort, jnp.bfloat16)]


def place(team, slab):
    return team // 2 * 32 + slab % 32 // 2 * 2 + team % 2


ROWS = 96


def step_kernel(
    anchors, vel, spectral_in, lift_in, mix_in, proj_in, plane_in, spread_in, inverse_in, expand_in, sort_in,
    second_out, raw_out, tile_out,
    ext, mid, after_two, spectral, lift, mix, proj, plane, spread, inverse, expand, sort,
    w_send, w_in, w_all, cut_out, cut_in, a_rows, t_rows, bands, a_send, a_got, a_wide, y_send, y_got,
    seen_wide, proj_wide, act, slope, g_high, g_low, out_sum, twice, g_send, g_got, m_send, m_got, r_send, r_got, raw,
    s_crew, s_yx,
    local_sem, z_sem, x_sem, c_sem, cross_sem, swap_sem, wy_sem, band_sem, y_sem, g_sem, a_sem, m_sem, back_sem,
    sc_sem, sy_sem,
):
    role, slab = lax.axis_index("role"), lax.axis_index("slab")
    yx = slab % 32 // 2
    team = slab // 32 * 2 + slab % 2
    patch = role // 2 * 32 + yx * 2 + role % 2
    after, before = (slab + 1) % SLABS, (slab + SLABS - 1) % SLABS
    teams = [(d, (team + d) % ROLES) for d in range(1, ROLES)]
    crew = [(d, (role * ROLES + team + d) % CREW) for d in range(1, CREW)]
    spots = [(d, (yx + d) % YX) for d in range(1, YX)]
    home = role == team
    pending = []

    def remote(src, dst, send_sem, recv_sem, to_role, to_slab):
        return pltpu.make_async_remote_copy(
            src_ref=src, dst_ref=dst, send_sem=send_sem, recv_sem=recv_sem,
            device_id=(to_role, to_slab), device_id_type=MESH,
        )

    def to_spot(at):
        return slab // 32 * 32 + at * 2 + slab % 2

    def send(src, dst, sems, d, to_role, to_slab):
        copy = remote(src, dst, sems.at[0, d], sems.at[1, d], to_role, to_slab)
        copy.start()
        pending.append(copy)
        return copy

    def fetch(at, src, dst):
        copy = pltpu.make_async_copy(src, dst, local_sem.at[at])
        copy.start()
        return copy

    own = fetch(0, vel, ext.at[:, pl.ds(2, PLANES), pl.ds(16, 64)])
    fetched = [fetch(1, spectral_in, spectral), fetch(2, lift_in, lift), fetch(3, mix_in, mix), fetch(4, proj_in, proj)]
    later = [
        fetch(5, plane_in, plane), fetch(6, spread_in, spread), fetch(7, inverse_in, inverse), fetch(8, expand_in, expand),
        fetch(9, sort_in, sort),
    ]

    barrier = pltpu.get_barrier_semaphore()

    def greet(to_role, to_slab):
        pl.semaphore_signal(barrier, inc=1, device_id=(to_role, to_slab), device_id_type=MESH)

    greet(role, after)
    greet(role, before)

    @pl.when(role > 0)
    def _():
        greet(role - 1, after)
        greet(role - 1, before)

    @pl.when(role < ROLES - 1)
    def _():
        greet(role + 1, after)
        greet(role + 1, before)

    for _, to in crew:
        greet(to // ROLES, place(to % ROLES, slab))
    for _, to in spots:
        greet(role, to_spot(to))

    source = lax.broadcasted_iota(jnp.int32, (ROLES * TILE, TILE), 0)
    target = lax.broadcasted_iota(jnp.int32, (ROLES * TILE, TILE), 1)
    pick = (
        (source // TILE == target % WIDTH // PART)
        & (source % TILE // WIDTH == target // WIDTH)
        & (source % WIDTH // PART == role)
        & (source % PART == target % PART)
    )
    pick = jnp.where(pick, 1.0, 0.0).astype(jnp.bfloat16)
    for copy in fetched:
        copy.wait()
    row_ky = lax.broadcasted_iota(jnp.int32, (MODES, MODES * WIDTH), 0)
    lane_ky = lax.broadcasted_iota(jnp.int32, (MODES, MODES * WIDTH), 1) // WIDTH
    twin = jnp.concatenate([lift[...], lift[...]], axis=1)
    long = jnp.concatenate([twin] * (MODES // 2), axis=1)
    blocks = [jnp.where(row_ky == lane_ky, long[i : i + 1], 0.0) for i in range(3)]
    lifted = dot3(
        split(jnp.concatenate(blocks, axis=0)), split(spectral[...].reshape(MODES * WIDTH, WIDTH))
    )
    lifted = lifted.reshape(3, 2, 8, WIDTH)
    lifted = jnp.concatenate([lifted[:, 0].reshape(24, WIDTH), lifted[:, 1].reshape(24, WIDTH)], axis=1)
    lifted = dot2(split(lifted), pick, NT)
    for k in range(ROLES):
        w_send[k] = lifted[:, k * TILE : (k + 1) * TILE].reshape(3, 8, TILE)

    pl.semaphore_wait(barrier, 34 + 2 * ((role + 1) // 2 % 2))

    def to_below(k):
        return remote(
            vel.at[:, pl.ds(k, 1)], ext.at[:, pl.ds(10 + k, 1), pl.ds(16, 64)],
            z_sem.at[0, k], z_sem.at[1, k], role - 1, slab,
        )

    def to_above(k):
        return remote(
            vel.at[:, pl.ds(7 - k, 1)], ext.at[:, pl.ds(1 - k, 1), pl.ds(16, 64)],
            z_sem.at[0, 2 + k], z_sem.at[1, 2 + k], role + 1, slab,
        )

    def corner(up, right, at):
        plane_at, slot = (7, 1) if up else (0, 10)
        row, spot = (56, 8) if right else (0, 80)
        return remote(
            vel.at[:, pl.ds(plane_at, 1), pl.ds(row, 8)], ext.at[:, pl.ds(slot, 1), pl.ds(spot, 8)],
            c_sem.at[0, at], c_sem.at[1, at], role + 1 if up else role - 1, after if right else before,
        )

    to_after = remote(
        vel.at[:, :, pl.ds(56, 8)], ext.at[:, pl.ds(2, PLANES), pl.ds(8, 8)],
        x_sem.at[0, 0], x_sem.at[1, 0], role, after,
    )
    to_before = remote(
        vel.at[:, :, pl.ds(0, 8)], ext.at[:, pl.ds(2, PLANES), pl.ds(80, 8)],
        x_sem.at[0, 1], x_sem.at[1, 1], role, before,
    )

    @pl.when(role > 0)
    def _():
        to_below(0).start()
        corner(False, True, 0).start()
        corner(False, False, 1).start()

    @pl.when(role < ROLES - 1)
    def _():
        to_above(0).start()
        corner(True, True, 2).start()
        corner(True, False, 3).start()

    to_after.start()
    to_before.start()

    o_copies = [
        send(w_send.at[to % ROLES], w_in.at[team, role], cross_sem, d, to // ROLES, place(to % ROLES, slab))
        for d, to in crew
    ]
    w_in[team, role] = w_send[team]

    @pl.when(role > 0)
    def _():
        to_below(1).start()

    @pl.when(role < ROLES - 1)
    def _():
        to_above(1).start()

    @pl.when(role == 0)
    def _():
        ext[:, pl.ds(0, 2)] = jnp.zeros((3, 2, ROWS, TILE), jnp.float32)

    @pl.when(role == ROLES - 1)
    def _():
        ext[:, pl.ds(10, 2)] = jnp.zeros((3, 2, ROWS, TILE), jnp.float32)

    seen = dot(mix[...], lift[...], (((0,), (1,)), ((), ())))
    unit = jnp.where(
        lax.broadcasted_iota(jnp.int32, (3, 3), 0) == lax.broadcasted_iota(jnp.int32, (3, 3), 1), 1.0, 0.0
    )
    proj_t = dot(proj[...], unit, TN)
    lift_t = dot(lift[...], unit, TN)
    for i in range(3):
        seen_wide[i] = jnp.broadcast_to(seen[:, i : i + 1], (WIDTH, TILE))
        proj_wide[i] = jnp.broadcast_to(proj_t[:, i : i + 1], (WIDTH, TILE))

    lane_80 = lax.broadcasted_iota(jnp.int32, (80, TILE), 1)
    lane_64 = lax.broadcasted_iota(jnp.int32, (64, TILE), 1)

    def advance(field, z, row, count, lane):
        centre = [field[c, z, pl.ds(row, count)] for c in range(3)]
        out = []
        for c in range(3):
            here = centre[c]
            z_next, z_prev = field[c, z + 1, pl.ds(row, count)], field[c, z - 1, pl.ds(row, count)]
            x_next, x_prev = field[c, z, pl.ds(row + 1, count)], field[c, z, pl.ds(row - 1, count)]
            y_next = jnp.where(lane == TILE - 1, 0.0, pltpu.roll(here, TILE - 1, 1))
            y_prev = jnp.where(lane == 0, 0.0, pltpu.roll(here, 1, 1))
            laplace = z_next + z_prev + x_next + x_prev + y_next + y_prev - 6.0 * here
            carried = 0.5 * (
                centre[0] * (z_next - z_prev) + centre[1] * (x_next - x_prev) + centre[2] * (y_next - y_prev)
            )
            out.append(here + time_step * (viscosity * laplace - carried))
        return out

    own.wait()
    to_after.wait_recv()
    to_before.wait_recv()

    def inner(z, carry):
        out = advance(ext, z, 8, 80, lane_80)
        for c in range(3):
            mid[c, z, pl.ds(8, 80)] = out[c]
        return carry

    lax.fori_loop(3, 9, inner, 0)

    @pl.when(role > 0)
    def _():
        to_above(0).wait_recv()
        corner(True, True, 2).wait_recv()
        corner(True, False, 3).wait_recv()

    @pl.when(role < ROLES - 1)
    def _():
        to_below(0).wait_recv()
        corner(False, True, 0).wait_recv()
        corner(False, False, 1).wait_recv()

    inner(2, 0)
    inner(9, 0)

    x_at, y_at = anchors[0, 0], anchors[0, 1]
    from_lane = lax.broadcasted_iota(jnp.int32, (TILE, TILE), 0)
    to_lane = lax.broadcasted_iota(jnp.int32, (TILE, TILE), 1)
    chosen = [
        jnp.where((from_lane == to_lane % PATCH + y_at) & (to_lane // PATCH == k), 1.0, 0.0).astype(jnp.bfloat16)
        for k in range(4)
    ]

    def cut(field, first_row, first_plane, at):
        total = None
        for k in range(4):
            rows = [
                field[c, z + first_plane, pl.ds(first_row + x_at + 8 * k, 8), :]
                for z in range(PLANES)
                for c in range(3)
            ]
            part = pass_(jnp.concatenate(rows, axis=0).astype(jnp.bfloat16), chosen[k], NN)
            total = part if total is None else total + part
        cut_out[at] = total.astype(jnp.bfloat16).reshape(12, 16, TILE)

    def swap(at):
        return remote(
            cut_out.at[at], cut_in.at[at], swap_sem.at[0, at], swap_sem.at[1, at], team, place(role, slab)
        )

    def swap_start(at):
        @pl.when(jnp.logical_not(home))
        def _():
            swap(at).start()

        @pl.when(home)
        def _():
            cut_in[at] = cut_out[at]

    def swap_arrival(at, rows):
        @pl.when(jnp.logical_not(home))
        def _():
            swap(at).wait_recv()

        rows[...] = cut_in[at].astype(jnp.float32).reshape(PAIRS, 8, TILE)
        return jnp.concatenate([rows[:, k] for k in range(8)], axis=1)

    cut(mid, 16, 2, 0)
    swap_start(0)

    for copy in o_copies:
        copy.wait_recv()
    for k in range(ROLES):
        w_all[k, yx] = (w_in[k, 0] + w_in[k, 1]) + (w_in[k, 2] + w_in[k, 3])
    w_copies = [send(w_all.at[:, yx], w_all.at[:, yx], wy_sem, d, role, to_spot(to)) for d, to in spots]

    @pl.when(role > 0)
    def _():
        to_above(1).wait_recv()
        out = advance(ext, 1, 16, 64, lane_64)
        for c in range(3):
            mid[c, 1, pl.ds(16, 64)] = out[c]

    @pl.when(role < ROLES - 1)
    def _():
        to_below(1).wait_recv()
        out = advance(ext, 10, 16, 64, lane_64)
        for c in range(3):
            mid[c, 10, pl.ds(16, 64)] = out[c]

    @pl.when(role == 0)
    def _():
        mid[:, 1, pl.ds(16, 64)] = jnp.zeros((3, 64, TILE), jnp.float32)

    @pl.when(role == ROLES - 1)
    def _():
        mid[:, 10, pl.ds(16, 64)] = jnp.zeros((3, 64, TILE), jnp.float32)

    def outer(z, carry):
        out = advance(mid, z, 16, 64, lane_64)
        for c in range(3):
            after_two[c, z - 2] = out[c]
        return carry

    lax.fori_loop(2, 6, outer, 0)
    for copy in later:
        copy.wait()

    a = swap_arrival(0, a_rows)
    a_low = a.astype(jnp.bfloat16)
    bands[team] = pass_(a_low, plane[0], NT) + pass_(a_low, plane[1], NT)
    copies = [send(bands.at[team], bands.at[team], band_sem, d, role, place(to, slab)) for d, to in teams]

    lax.fori_loop(6, 10, outer, 0)
    second_copy = fetch(0, after_two, second_out)
    cut(after_two, 0, 0, 1)
    swap_start(1)

    for copy in copies:
        copy.wait_recv()
    every = jnp.concatenate([bands[b] for b in range(ROLES)], axis=0)
    halves = jnp.concatenate([every[:, :TILE], every[:, TILE:]], axis=0)
    coef = dot3(split(halves), (spread[0], spread[1]), TN)
    for copy in w_copies:
        copy.wait_recv()

    def blocks_out(ref, s, part):
        part = part.reshape(2, 8, 8, TILE)
        for core in range(2):
            ref[s // 2 * 2 + core, pl.ds(s % 2 * 8, 8)] = part[core]

    mixed = []
    for s in range(SH):
        at = (3 * SH + s) * TILE
        blocks_out(a_send, s, coef[:, at : at + TILE])
        total = None
        for i in range(3):
            at = (i * SH + s) * TILE
            weights = jnp.concatenate(
                [w_all[s // 2 * 2 + core, pl.ds(s % 2 * 8, 8), i].reshape(64, TILE) for core in range(2)], axis=0
            )
            term = coef[:, at : at + TILE] * weights
            total = term if total is None else total + term
        mixed.append(total)
    mixed = split(jnp.concatenate(mixed, axis=1))

    def back(to):
        rows = pl.ds(pl.multiple_of(to * 256, 256), 256)
        y_send[to] = dot3((inverse[0, rows], inverse[1, rows]), mixed, NT)

    y_copies = []
    for d, to in (teams[1], teams[0], teams[2]):
        back(to)
        y_copies.append((d, send(y_send.at[to], y_got.at[team], y_sem, d, role, place(to, slab))))
    back(team)
    y_got[team] = y_send[team]
    for k in range(PAIRS):
        out_sum[k] = jnp.zeros((8, AREA), jnp.float32)

    def forward(q):
        rows = jnp.concatenate([y_got[q, :TILE], y_got[q, TILE:]], axis=1)
        slope[q] = dot3(split(rows), (plane[0], plane[1]))
        channels = pl.ds(pl.multiple_of(q * PART, PART), PART)
        by_seen = [seen_wide[i, channels] for i in range(3)]
        by_proj = [proj_wide[j, channels] for j in range(3)]

        def gelu(z, carry):
            at = pl.ds(pl.multiple_of(z * PART, PART), PART)
            for k in range(8):
                lanes = slice(k * TILE, (k + 1) * TILE)
                x = slope[q, at, lanes]
                for i in range(3):
                    x = x + by_seen[i] * a_rows[z * 3 + i, k : k + 1]
                square = x * x
                t = jnp.tanh(x * (root + (root * 0.044715) * square))
                half = 0.5 + 0.5 * t
                value = x * half
                act[q, at, lanes] = value
                slope[q, at, lanes] = half + value * (1.0 - t) * (root + (root * 3.0 * 0.044715) * square)
                for j in range(3):
                    term = by_proj[j] * value
                    out_sum[z * 3 + j, :, lanes] += term[:8] + term[8:]
            return carry

        lax.fori_loop(0, PLANES, gelu, 0)

    forward(team)
    for n, (d, copy) in enumerate(y_copies):
        copy.wait_recv()
        if n == 1:
            a_copies = [send(a_send.at[:, to], a_got.at[yx], a_sem, d, role, to_spot(to)) for d, to in spots]
            a_got[yx] = a_send[:, yx]
        forward((team + ROLES - d) % ROLES)

    wanted = swap_arrival(1, t_rows)
    out = jnp.concatenate([jnp.sum(out_sum[k], axis=0, keepdims=True) for k in range(PAIRS)], axis=0)
    error = a + out - wanted
    doubled = 2.0 * error
    for k in range(8):
        twice[:, k] = doubled[:, k * TILE : (k + 1) * TILE]

    def backward(q):
        channels = pl.ds(pl.multiple_of(q * PART, PART), PART)
        by_proj = [proj_wide[j, channels] for j in range(3)]

        def chain(z, carry):
            at = pl.ds(pl.multiple_of(z * PART, PART), PART)
            for k in range(8):
                lanes = slice(k * TILE, (k + 1) * TILE)
                g = by_proj[0] * twice[z * 3, k : k + 1]
                for j in range(1, 3):
                    g = g + by_proj[j] * twice[z * 3 + j, k : k + 1]
                g = g * slope[q, at, lanes]
                slope[q, at, lanes] = g
                g_high[at, lanes], g_low[at, lanes] = split(g)
            return carry

        lax.fori_loop(0, PLANES, chain, 0)
        g_send[q] = dot3((g_high[...], g_low[...]), (plane[0], plane[1]), NT)

    g_copies = []
    for d, to in (teams[1], teams[0], teams[2]):
        backward(to)
        g_copies.append(send(g_send.at[to], g_got.at[team], g_sem, d, role, place(to, slab)))
    backward(team)
    g_got[team] = g_send[team]

    row_8 = lax.broadcasted_iota(jnp.int32, (8, TILE), 0)
    lane = lax.broadcasted_iota(jnp.int32, (8, TILE), 1)
    zero = jnp.zeros((8, TILE), jnp.float32)
    wide = jnp.zeros((PART, TILE), jnp.float32)

    def cells(q, carry):
        def over(z, sums):
            at = pl.ds(pl.multiple_of(z * PART, PART), PART)
            sums = list(sums)
            for k in range(8):
                lanes = slice(k * TILE, (k + 1) * TILE)
                g, value = slope[q, at, lanes], act[q, at, lanes]
                for i in range(3):
                    sums[i] = sums[i] + g * a_rows[z * 3 + i, k : k + 1]
                    sums[3 + i] = sums[3 + i] + value * twice[z * 3 + i, k : k + 1]
            return tuple(sums)

        return lax.fori_loop(0, PLANES, over, (wide,) * 6)

    by_quarter = [cells(q, 0) for q in range(ROLES)]

    def channel_rows(k, row):
        column = jnp.concatenate([sums[k] for sums in by_quarter], axis=0)
        return dot(jnp.where(row_8 == row, 1.0, 0.0), column, NT)

    cross_rows = sum(channel_rows(i, i) for i in range(3))
    proj_rows = sum(channel_rows(3 + j, j) for j in range(3))
    sse = jnp.sum(error * error, keepdims=True)

    for copy in g_copies:
        copy.wait_recv()
    stacked = jnp.concatenate([g_got[b][:, h * TILE : (h + 1) * TILE] for b in range(ROLES) for h in range(2)], axis=0)
    grad = dot3(split(stacked), (inverse[0], inverse[1]), TN)
    for s in range(SH):
        blocks_out(m_send, s, grad[:, s * TILE : (s + 1) * TILE])
    m_copies = [send(m_send.at[:, to], m_got.at[yx], m_sem, d, role, to_spot(to)) for d, to in spots]
    m_got[yx] = m_send[:, yx]
    for copy in a_copies:
        copy.wait_recv()
    a_all = split(a_got[...].reshape(SLABS * 8, TILE))
    a_all = dot2(a_all, expand[...])
    for i in range(3):
        a_wide[i] = a_all[:, i * TILE : (i + 1) * TILE].reshape(YX, ROLES, 8, TILE)
    for copy in m_copies:
        copy.wait_recv()

    crossed = []
    for b in range(ROLES):
        sums = [zero, zero, zero]
        for k in range(YX):
            g = m_got[k, b]
            sums = [sums[i] + a_wide[i, k, b] * g for i in range(3)]
        crossed.append(jnp.concatenate(sums, axis=1))
    crossed = dot2(split(jnp.concatenate(crossed, axis=0)), sort[...])
    for b in range(ROLES):
        for k in range(ROLES):
            r_send[k, b] = crossed[b * 8 : b * 8 + 8, k * TILE : (k + 1) * TILE]
    r_copies = [
        send(r_send.at[to // ROLES, to % ROLES], r_got.at[role, team], back_sem, d, to // ROLES, place(to % ROLES, slab))
        for d, to in crew
    ]
    r_got[role, team] = r_send[role, team]
    for copy in r_copies:
        copy.wait_recv()
    joined = [(r_got[0, q] + r_got[1, q]) + (r_got[2, q] + r_got[3, q]) for q in range(ROLES)]
    joined = dot2(split(jnp.concatenate(joined, axis=1)), sort[...], NT)
    squares = jnp.zeros((WIDTH, TILE), jnp.float32)
    lift_sum = [jnp.zeros((WIDTH, WIDTH), jnp.float32)] * 3
    for k in range(8):
        rows = [joined[k : k + 1, i * TILE : (i + 1) * TILE] for i in range(3)]
        value = lift_t[:, 0:1] * rows[0] + lift_t[:, 1:2] * rows[1] + lift_t[:, 2:3] * rows[2]
        raw[k] = value
        squares = squares + value * value
        for i in range(3):
            lift_sum[i] = lift_sum[i] + (
                spectral[k] * rows[i][:, :WIDTH] + spectral[8 + k] * rows[i][:, WIDTH:]
            )
    raw_copy = fetch(1, raw, raw_out)
    left = cross_rows
    for i in range(3):
        left = left + dot(jnp.where(row_8[:, :WIDTH] == 3 + i, 1.0, 0.0), lift_sum[i], NT)
    tile = jnp.concatenate([left, proj_rows], axis=1)
    tile = tile + jnp.where((row_8 == 6) & (lane == patch), sse, 0.0)
    tile = tile + jnp.where(row_8 == 7, jnp.sum(squares, keepdims=True), 0.0)

    s_crew[role, team] = tile
    copies = [
        send(s_crew.at[role, team], s_crew.at[role, team], sc_sem, d, to // ROLES, place(to % ROLES, slab))
        for d, to in crew
    ]
    for copy in copies:
        copy.wait_recv()
    s_yx[yx] = jnp.sum(s_crew[...], axis=(0, 1))
    copies = [send(s_yx.at[yx], s_yx.at[yx], sy_sem, d, role, to_spot(to)) for d, to in spots]
    for copy in copies:
        copy.wait_recv()
    tile_out[...] = jnp.sum(s_yx[...], axis=0)

    for copy in pending:
        copy.wait_send()
    second_copy.wait()
    raw_copy.wait()
    to_after.wait_send()
    to_before.wait_send()

    @pl.when(role > 0)
    def _():
        to_below(0).wait_send()
        to_below(1).wait_send()
        corner(False, True, 0).wait_send()
        corner(False, False, 1).wait_send()

    @pl.when(role < ROLES - 1)
    def _():
        to_above(0).wait_send()
        to_above(1).wait_send()
        corner(True, True, 2).wait_send()
        corner(True, False, 3).wait_send()

    @pl.when(jnp.logical_not(home))
    def _():
        swap(0).wait_send()
        swap(1).wait_send()


def result(*shape):
    return jax.ShapeDtypeStruct(shape, jnp.float32)


def step(anchors, velocity, spectral, lift, mix, proj):
    vmem = pl.BlockSpec(memory_space=pltpu.VMEM)
    anywhere = pl.BlockSpec(memory_space=pltpu.HBM)
    dma = pltpu.SemaphoreType.DMA

    def room(*shape):
        return pltpu.VMEM(shape, jnp.float32)

    def narrow(*shape):
        return pltpu.VMEM(shape, jnp.bfloat16)

    return pl.pallas_call(
        step_kernel,
        out_shape=(result(3, PLANES, 64, TILE), result(8, WIDTH, TILE), result(8, TILE)),
        in_specs=[pl.BlockSpec(memory_space=pltpu.SMEM)] + [anywhere] * 10,
        out_specs=(anywhere, anywhere, vmem),
        scratch_shapes=[
            room(3, 12, ROWS, TILE),
            room(3, 12, ROWS, TILE),
            room(3, PLANES, 64, TILE),
            room(MODES, WIDTH, WIDTH),
            room(3, WIDTH),
            room(WIDTH, WIDTH),
            room(3, WIDTH),
            narrow(2, 256, AREA),
            narrow(2, 2 * ROLES * PAIRS, 4 * SH * TILE),
            narrow(2, ROLES * 256, SH * TILE),
            narrow(TILE, 3 * TILE),
            narrow(3 * TILE, ROLES * TILE),
            room(ROLES, 3, 8, TILE),
            room(ROLES, ROLES, 3, 8, TILE),
            room(ROLES, YX, 3, 8, TILE),
            narrow(2, 12, 16, TILE),
            narrow(2, 12, 16, TILE),
            room(PAIRS, 8, TILE),
            room(PAIRS, 8, TILE),
            room(ROLES, PAIRS, 256),
            room(ROLES, YX, 8, TILE),
            room(YX, ROLES, 8, TILE),
            room(3, YX, ROLES, 8, TILE),
            room(ROLES, 256, TILE),
            room(ROLES, 256, TILE),
            room(3, WIDTH, TILE),
            room(3, WIDTH, TILE),
            room(ROLES, TILE, AREA),
            room(ROLES, TILE, AREA),
            narrow(TILE, AREA),
            narrow(TILE, AREA),
            room(PAIRS, 8, AREA),
            room(PAIRS, 8, TILE),
            room(ROLES, TILE, 256),
            room(ROLES, TILE, 256),
            room(ROLES, YX, 8, TILE),
            room(YX, ROLES, 8, TILE),
            room(ROLES, ROLES, 8, TILE),
            room(ROLES, ROLES, 8, TILE),
            room(8, WIDTH, TILE),
            room(ROLES, ROLES, 8, TILE),
            room(YX, 8, TILE),
            dma((10,)),
            dma((2, 4)),
            dma((2, 2)),
            dma((2, 4)),
            dma((2, CREW)),
            dma((2, 2)),
            dma((2, YX)),
            dma((2, ROLES)),
            dma((2, ROLES)),
            dma((2, ROLES)),
            dma((2, YX)),
            dma((2, YX)),
            dma((2, CREW)),
            dma((2, CREW)),
            dma((2, YX)),
        ],
        compiler_params=pltpu.CompilerParams(
            collective_id=0, has_side_effects=True, vmem_limit_bytes=63 * 2**20
        ),
    )(anchors, velocity, spectral, lift, mix, proj, *tables())


def finish_kernel(
    second, raw, tile, lift, mix, table, second_out, loss_out, lift_out, mix_out, proj_out, spec_out, held, copy_sem
):
    fetches = [pltpu.make_async_copy(second.at[c], held.at[c], copy_sem.at[0, c]) for c in range(3)]
    stores = [pltpu.make_async_copy(held.at[c], second_out.at[c], copy_sem.at[1, c]) for c in range(3)]
    for copy in fetches:
        copy.start()

    for get, put in zip(fetches, stores):
        get.wait()
        put.start()

    def normal(total):
        mean = jnp.sum(total * total, keepdims=True) / total.size
        return total / jnp.sqrt(mean + tiny_eps)

    cross = tile[0:3, :WIDTH]
    proj_out[...] = normal(tile[0:3, WIDTH:])
    lift_out[...] = normal(tile[3:6, :WIDTH] + dot(cross, mix[...], NT))
    mix_out[...] = normal(dot(lift[...], cross, TN))
    scale = 1.0 / jnp.sqrt(tile[7:8, 0:1] / (MODES**3 * WIDTH * WIDTH) + tiny_eps)
    for k in range(8):
        value = raw[k] * scale
        spec_out[k] = value[:, :WIDTH]
        spec_out[8 + k] = value[:, WIDTH:]
    losses = tile[6:7, :] / (3.0 * PATCH**3)
    lanes = lax.broadcasted_iota(jnp.int32, (1, TILE), 1)
    found = [jnp.sum(jnp.where(lanes == table[0:1, k : k + 1], losses, 0.0), axis=1, keepdims=True) for k in range(2)]
    loss_out[...] = jnp.concatenate(found, axis=1)
    for copy in stores:
        copy.wait()


def finish(second, raw, tile, lift, mix, table):
    vmem = pl.BlockSpec(memory_space=pltpu.VMEM)
    anywhere = pl.BlockSpec(memory_space=pltpu.HBM)
    return pl.pallas_call(
        finish_kernel,
        out_shape=(
            result(3, PLANES, 64, TILE),
            result(1, 2),
            result(3, WIDTH),
            result(WIDTH, WIDTH),
            result(3, WIDTH),
            result(MODES, WIDTH, WIDTH),
        ),
        in_specs=[anywhere] + [vmem] * 5,
        out_specs=(anywhere,) + (vmem,) * 5,
        scratch_shapes=[pltpu.VMEM((3, PLANES, 64, TILE), jnp.float32), pltpu.SemaphoreType.DMA((2, 3))],
    )(second, raw, tile, lift, mix, table)


def on_device(velocity, anchors, slot_table, lift, mix, proj, spectral):
    second, raw, tile = step(anchors, velocity, spectral, lift, mix, proj)
    return finish(second, raw, tile, lift, mix, slot_table)


def solution(mesh):
    return jax.shard_map(
        on_device,
        mesh=mesh,
        in_specs=(
            P(None, "role", "slab", None),
            P("slab", None),
            P("slab", None),
            P(),
            P(),
            P(),
            P(("role", "slab"), None, None),
        ),
        out_specs=(
            P(None, "role", "slab", None),
            P("slab", None),
            P(),
            P(),
            P(),
            P(("role", "slab"), None, None),
        ),
        check_vma=False,
    )
```

```python
import math

import jax
import jax.numpy as jnp
import numpy as np
from jax import lax
from jax.experimental import pallas as pl
from jax.experimental.pallas import tpu as pltpu
from jax.sharding import PartitionSpec as P

MODES = 16
PATCH = 32
AREA = PATCH * PATCH
ROLES = 4
SLABS = 64
YX = 16
CREW = 16
PLANES = 8
WIDTH = 64
PART = WIDTH // ROLES
SH = 4
TILE = 128
PAIRS = 3 * PLANES

time_step = 0.1
viscosity = 1.5
tiny_eps = 1e-06
exact = lax.Precision.HIGHEST
MESH = pl.DeviceIdType.MESH
root = math.sqrt(2.0 / math.pi)
NN = (((1,), (0,)), ((), ()))
NT = (((1,), (1,)), ((), ()))
TN = (((0,), (0,)), ((), ()))


def dot(a, b, dims=NN):
    return lax.dot_general(a, b, dims, precision=exact, preferred_element_type=jnp.float32)


def split(value):
    high = value.astype(jnp.bfloat16)
    return high, (value - high.astype(jnp.float32)).astype(jnp.bfloat16)


def pass_(a, b, dims):
    return lax.dot_general(a, b, dims, preferred_element_type=jnp.float32)


def dot3(a, b, dims=NN):
    return pass_(a[0], b[0], dims) + (pass_(a[0], b[1], dims) + pass_(a[1], b[0], dims))


def dot2(a, exact_b, dims=NN):
    return pass_(a[0], exact_b, dims) + pass_(a[1], exact_b, dims)


def fourier_table():
    order = np.arange(MODES)[:, None]
    points = np.arange(PATCH)[None, :]
    angles = 2.0 * math.pi * ((order + 1) // 2) * points / PATCH
    waves = np.where((order % 2 == 1) | (order == 0), np.cos(angles), np.sin(angles))
    return waves * np.where(order == 0, math.sqrt(1.0 / PATCH), math.sqrt(2.0 / PATCH))


def pair(table):
    table = table.astype(np.float32)
    high = table.astype(jnp.bfloat16)
    return jnp.asarray(np.stack([high, (table - high.astype(np.float32)).astype(jnp.bfloat16)]))


def tables():
    phi = fourier_table()
    over_x = phi.reshape(2, 4, 2, 4, 8)
    over_y = phi.reshape(2, 8, PATCH)
    plane = np.einsum("axchl,gky->gcaxklhy", over_x, over_y).reshape(256, AREA)
    phi_z = phi.reshape(ROLES, SH, ROLES, PLANES)
    eye2, eye3, eye4, eye16 = np.eye(2), np.eye(3), np.eye(ROLES), np.eye(PART)
    ones = np.ones(PART)
    spread = np.einsum("hg,rsbz,ij,c->hbzijsgrc", eye2, phi_z, eye3, ones).reshape(2 * ROLES * PAIRS, 3 * SH * TILE)
    short = np.einsum("hg,rsbz,ij->hbzisjgr", eye2, phi_z, eye3).reshape(2 * ROLES * PAIRS, SH, 24)
    short = np.pad(short, ((0, 0), (0, 0), (0, TILE - 24))).reshape(-1, SH * TILE)
    inverse = np.einsum("hg,rsbz,cd->bhzcsgrd", eye2, phi_z, eye16).reshape(ROLES * 256, SH * TILE)
    expand = np.einsum("ij,hg,rs,c->ihrjgsc", eye3, eye2, eye4, ones).reshape(24, 3 * TILE)
    expand = np.pad(expand, ((0, TILE - 24), (0, 0)))
    sort = np.einsum("ij,hg,rs,cd->ihrcsjgd", eye3, eye2, eye4, eye16).reshape(3 * TILE, ROLES, 96)
    sort = np.pad(sort, ((0, 0), (0, 0), (0, TILE - 96))).reshape(3 * TILE, ROLES * TILE)
    return [pair(plane), pair(np.concatenate([spread, short], axis=1)), pair(inverse), jnp.asarray(expand, jnp.bfloat16), jnp.asarray(sort, jnp.bfloat16)]


def place(team, slab):
    return team // 2 * 32 + slab % 32 // 2 * 2 + team % 2


ROWS = 96


def step_kernel(
    anchors, vel, spectral_in, lift_in, mix_in, proj_in, plane_in, spread_in, inverse_in, expand_in, sort_in,
    second_out, raw_out, tile_out,
    ext, mid, after_two, spectral, lift, mix, proj, plane, spread, inverse, expand, sort,
    w_send, w_in, w_all, cut_out, cut_in, a_rows, t_rows, band, bands, a_send, a_got, a_wide, y_send, y_got,
    seen_wide, proj_wide, act, slope, g_high, g_low, out_sum, twice, g_send, g_got, m_send, m_got, r_send, r_got, raw,
    s_crew, s_yx,
    local_sem, z_sem, x_sem, c_sem, cross_sem, swap_sem, wy_sem, band_sem, y_sem, g_sem, a_sem, m_sem, back_sem,
    sc_sem, sy_sem,
):
    role, slab = lax.axis_index("role"), lax.axis_index("slab")
    yx = slab % 32 // 2
    team = slab // 32 * 2 + slab % 2
    patch = role // 2 * 32 + yx * 2 + role % 2
    after, before = (slab + 1) % SLABS, (slab + SLABS - 1) % SLABS
    teams = [(d, (team + d) % ROLES) for d in range(1, ROLES)]
    crew = [(d, (role * ROLES + team + d) % CREW) for d in range(1, CREW)]
    spots = [(d, (yx + d) % YX) for d in range(1, YX)]
    home = role == team
    pending = []

    def remote(src, dst, send_sem, recv_sem, to_role, to_slab):
        return pltpu.make_async_remote_copy(
            src_ref=src, dst_ref=dst, send_sem=send_sem, recv_sem=recv_sem,
            device_id=(to_role, to_slab), device_id_type=MESH,
        )

    def to_spot(at):
        return slab // 32 * 32 + at * 2 + slab % 2

    def send(src, dst, sems, d, to_role, to_slab):
        copy = remote(src, dst, sems.at[0, d], sems.at[1, d], to_role, to_slab)
        copy.start()
        pending.append(copy)
        return copy

    def fetch(at, src, dst):
        copy = pltpu.make_async_copy(src, dst, local_sem.at[at])
        copy.start()
        return copy

    own = fetch(0, vel, ext.at[:, pl.ds(2, PLANES), pl.ds(16, 64)])
    fetched = [
        fetch(1, spectral_in, spectral), fetch(2, lift_in, lift), fetch(3, mix_in, mix), fetch(4, proj_in, proj),
        fetch(9, sort_in, sort),
    ]
    later = [
        fetch(5, plane_in, plane), fetch(6, spread_in, spread), fetch(7, inverse_in, inverse), fetch(8, expand_in, expand)
    ]

    barrier = pltpu.get_barrier_semaphore()

    def greet(to_role, to_slab):
        pl.semaphore_signal(barrier, inc=1, device_id=(to_role, to_slab), device_id_type=MESH)

    greet(role, after)
    greet(role, before)

    @pl.when(role > 0)
    def _():
        greet(role - 1, after)
        greet(role - 1, before)

    @pl.when(role < ROLES - 1)
    def _():
        greet(role + 1, after)
        greet(role + 1, before)

    for _, to in crew:
        greet(to // ROLES, place(to % ROLES, slab))
    for _, to in spots:
        greet(role, to_spot(to))

    for copy in fetched:
        copy.wait()
    row_ky = lax.broadcasted_iota(jnp.int32, (MODES, MODES * WIDTH), 0)
    lane_ky = lax.broadcasted_iota(jnp.int32, (MODES, MODES * WIDTH), 1) // WIDTH
    twin = jnp.concatenate([lift[...], lift[...]], axis=1)
    long = jnp.concatenate([twin] * (MODES // 2), axis=1)
    blocks = [jnp.where(row_ky == lane_ky, long[i : i + 1], 0.0) for i in range(3)]
    lifted = dot3(
        split(jnp.concatenate(blocks, axis=0)), split(spectral[...].reshape(MODES * WIDTH, WIDTH))
    )
    lifted = lifted.reshape(3, 2, 8, WIDTH)
    lifted = jnp.concatenate([lifted[i, h] for i in range(3) for h in range(2)], axis=1)
    lifted = dot2(split(lifted), sort[...])
    for k in range(ROLES):
        w_send[k] = lifted[:, k * TILE : (k + 1) * TILE]

    pl.semaphore_wait(barrier, 34 + 2 * ((role + 1) // 2 % 2))

    def to_below(k):
        return remote(
            vel.at[:, pl.ds(k, 1)], ext.at[:, pl.ds(10 + k, 1), pl.ds(16, 64)],
            z_sem.at[0, k], z_sem.at[1, k], role - 1, slab,
        )

    def to_above(k):
        return remote(
            vel.at[:, pl.ds(7 - k, 1)], ext.at[:, pl.ds(1 - k, 1), pl.ds(16, 64)],
            z_sem.at[0, 2 + k], z_sem.at[1, 2 + k], role + 1, slab,
        )

    def corner(up, right, at):
        plane_at, slot = (7, 1) if up else (0, 10)
        row, spot = (56, 8) if right else (0, 80)
        return remote(
            vel.at[:, pl.ds(plane_at, 1), pl.ds(row, 8)], ext.at[:, pl.ds(slot, 1), pl.ds(spot, 8)],
            c_sem.at[0, at], c_sem.at[1, at], role + 1 if up else role - 1, after if right else before,
        )

    to_after = remote(
        vel.at[:, :, pl.ds(56, 8)], ext.at[:, pl.ds(2, PLANES), pl.ds(8, 8)],
        x_sem.at[0, 0], x_sem.at[1, 0], role, after,
    )
    to_before = remote(
        vel.at[:, :, pl.ds(0, 8)], ext.at[:, pl.ds(2, PLANES), pl.ds(80, 8)],
        x_sem.at[0, 1], x_sem.at[1, 1], role, before,
    )

    @pl.when(role > 0)
    def _():
        to_below(0).start()

    @pl.when(role < ROLES - 1)
    def _():
        to_above(0).start()

    to_after.start()
    to_before.start()

    o_copies = [
        send(w_send.at[to % ROLES], w_in.at[team, role], cross_sem, d, to // ROLES, place(to % ROLES, slab))
        for d, to in crew
    ]
    w_in[team, role] = w_send[team]

    @pl.when(role > 0)
    def _():
        to_below(1).start()
        corner(False, True, 0).start()
        corner(False, False, 1).start()

    @pl.when(role < ROLES - 1)
    def _():
        to_above(1).start()
        corner(True, True, 2).start()
        corner(True, False, 3).start()

    @pl.when(role == 0)
    def _():
        ext[:, pl.ds(0, 2)] = jnp.zeros((3, 2, ROWS, TILE), jnp.float32)

    @pl.when(role == ROLES - 1)
    def _():
        ext[:, pl.ds(10, 2)] = jnp.zeros((3, 2, ROWS, TILE), jnp.float32)

    seen = dot(mix[...], lift[...], (((0,), (1,)), ((), ())))
    unit = jnp.where(
        lax.broadcasted_iota(jnp.int32, (3, 3), 0) == lax.broadcasted_iota(jnp.int32, (3, 3), 1), 1.0, 0.0
    )
    proj_t = dot(proj[...], unit, TN)
    lift_t = dot(lift[...], unit, TN)
    for i in range(3):
        seen_wide[i] = jnp.broadcast_to(seen[:, i : i + 1], (WIDTH, TILE))
        proj_wide[i] = jnp.broadcast_to(proj_t[:, i : i + 1], (WIDTH, TILE))

    lane_80 = lax.broadcasted_iota(jnp.int32, (80, TILE), 1)
    lane_64 = lax.broadcasted_iota(jnp.int32, (64, TILE), 1)
    lane_8 = lax.broadcasted_iota(jnp.int32, (8, TILE), 1)

    def advance(field, z, row, count, lane):
        centre = [field[c, z, pl.ds(row, count)] for c in range(3)]
        out = []
        for c in range(3):
            here = centre[c]
            z_next, z_prev = field[c, z + 1, pl.ds(row, count)], field[c, z - 1, pl.ds(row, count)]
            x_next, x_prev = field[c, z, pl.ds(row + 1, count)], field[c, z, pl.ds(row - 1, count)]
            y_next = jnp.where(lane == TILE - 1, 0.0, pltpu.roll(here, TILE - 1, 1))
            y_prev = jnp.where(lane == 0, 0.0, pltpu.roll(here, 1, 1))
            laplace = z_next + z_prev + x_next + x_prev + y_next + y_prev - 6.0 * here
            carried = 0.5 * (
                centre[0] * (z_next - z_prev) + centre[1] * (x_next - x_prev) + centre[2] * (y_next - y_prev)
            )
            out.append(here + time_step * (viscosity * laplace - carried))
        return out

    own.wait()
    to_after.wait_recv()
    to_before.wait_recv()

    def inner(z, carry):
        out = advance(ext, z, 8, 80, lane_80)
        for c in range(3):
            mid[c, z, pl.ds(8, 80)] = out[c]
        return carry

    lax.fori_loop(3, 9, inner, 0)

    for copy in o_copies:
        copy.wait_recv()
    lifted = [jnp.concatenate([w_in[k, r] for r in range(ROLES)], axis=1) for k in range(ROLES)]
    lifted = dot2(split(jnp.concatenate(lifted, axis=0)), sort[...], NT)
    for k in range(ROLES):
        for i in range(3):
            w_all[k, yx, i] = lifted[k * 8 : k * 8 + 8, i * TILE : (i + 1) * TILE]
    w_copies = [send(w_all.at[:, yx], w_all.at[:, yx], wy_sem, d, role, to_spot(to)) for d, to in spots]

    @pl.when(role > 0)
    def _():
        to_above(0).wait_recv()

    @pl.when(role < ROLES - 1)
    def _():
        to_below(0).wait_recv()

    for z in (2, 9):
        out = advance(ext, z, 16, 64, lane_64)
        for c in range(3):
            mid[c, z, pl.ds(16, 64)] = out[c]


    x_at, y_at = anchors[0, 0], anchors[0, 1]
    from_lane = lax.broadcasted_iota(jnp.int32, (TILE, TILE), 0)
    to_lane = lax.broadcasted_iota(jnp.int32, (TILE, TILE), 1)
    chosen = [
        jnp.where((from_lane == to_lane % PATCH + y_at) & (to_lane // PATCH == k), 1.0, 0.0).astype(jnp.bfloat16)
        for k in range(4)
    ]

    def cut(field, first_row, first_plane, at):
        total = None
        for k in range(4):
            rows = [
                field[c, z + first_plane, pl.ds(first_row + x_at + 8 * k, 8), :]
                for z in range(PLANES)
                for c in range(3)
            ]
            part = pass_(jnp.concatenate(rows, axis=0).astype(jnp.bfloat16), chosen[k], NN)
            total = part if total is None else total + part
        cut_out[at] = total.astype(jnp.bfloat16).reshape(12, 16, TILE)

    def swap(at):
        return remote(
            cut_out.at[at], cut_in.at[at], swap_sem.at[0, at], swap_sem.at[1, at], team, place(role, slab)
        )

    def swap_start(at):
        @pl.when(jnp.logical_not(home))
        def _():
            swap(at).start()

        @pl.when(home)
        def _():
            cut_in[at] = cut_out[at]

    def swap_arrival(at, rows):
        @pl.when(jnp.logical_not(home))
        def _():
            swap(at).wait_recv()

        rows[...] = cut_in[at].astype(jnp.float32).reshape(PAIRS, 8, TILE)
        return jnp.concatenate([rows[:, k] for k in range(8)], axis=1)

    cut(mid, 16, 2, 0)

    t_rows[...] = cut_out[0].astype(jnp.float32).reshape(PAIRS, 8, TILE)
    cells_here = jnp.concatenate([t_rows[:, k] for k in range(8)], axis=1).astype(jnp.bfloat16)
    for copy in later:
        copy.wait()
    band[...] = pass_(cells_here, plane[0], NT) + pass_(cells_here, plane[1], NT)

    def band_copy(k):
        return remote(band, bands.at[role], band_sem.at[0, k], band_sem.at[1, role], team, place(k, slab))

    def band_arrival(k):
        return remote(band, bands.at[k], band_sem.at[0, k], band_sem.at[1, k], team, place(k, slab))

    for k in range(ROLES):

        @pl.when(jnp.logical_not(home & (k == role)))
        def _():
            band_copy(k).start()

    @pl.when(home)
    def _():
        bands[role] = band[...]

    swap_start(0)

    @pl.when(role > 0)
    def _():
        to_above(1).wait_recv()
        corner(True, True, 2).wait_recv()
        corner(True, False, 3).wait_recv()
        out = advance(ext, 1, 16, 64, lane_64)
        for c in range(3):
            mid[c, 1, pl.ds(16, 64)] = out[c]

    @pl.when(role < ROLES - 1)
    def _():
        to_below(1).wait_recv()
        corner(False, True, 0).wait_recv()
        corner(False, False, 1).wait_recv()
        out = advance(ext, 10, 16, 64, lane_64)
        for c in range(3):
            mid[c, 10, pl.ds(16, 64)] = out[c]

    for z in (2, 9):
        for row in (8, 80):
            out = advance(ext, z, row, 8, lane_8)
            for c in range(3):
                mid[c, z, pl.ds(row, 8)] = out[c]

    @pl.when(role == 0)
    def _():
        mid[:, 1, pl.ds(16, 64)] = jnp.zeros((3, 64, TILE), jnp.float32)

    @pl.when(role == ROLES - 1)
    def _():
        mid[:, 10, pl.ds(16, 64)] = jnp.zeros((3, 64, TILE), jnp.float32)

    def outer(z, carry):
        out = advance(mid, z, 16, 64, lane_64)
        for c in range(3):
            after_two[c, z - 2] = out[c]
        return carry

    lax.fori_loop(2, 6, outer, 0)
    lax.fori_loop(6, 10, outer, 0)
    second_copy = fetch(0, after_two, second_out)
    cut(after_two, 0, 0, 1)
    swap_start(1)

    for k in range(ROLES):

        @pl.when(jnp.logical_not(home & (k == role)))
        def _():
            band_arrival(k).wait_recv()

    every = jnp.concatenate([bands[b] for b in range(ROLES)], axis=0)
    halves = jnp.concatenate([every[:, :TILE], every[:, TILE:]], axis=0)
    coef = dot3(split(halves), (spread[0], spread[1]), TN)
    for copy in w_copies:
        copy.wait_recv()

    def blocks_out(ref, s, part):
        part = part.reshape(2, 8, 8, TILE)
        for core in range(2):
            ref[s // 2 * 2 + core, pl.ds(s % 2 * 8, 8)] = part[core]

    mixed = []
    for s in range(SH):
        at = (3 * SH + s) * TILE
        blocks_out(a_send, s, coef[:, at : at + TILE])
        total = None
        for i in range(3):
            at = (i * SH + s) * TILE
            weights = jnp.concatenate(
                [w_all[s // 2 * 2 + core, pl.ds(s % 2 * 8, 8), i].reshape(64, TILE) for core in range(2)], axis=0
            )
            term = coef[:, at : at + TILE] * weights
            total = term if total is None else total + term
        mixed.append(total)
    mixed = split(jnp.concatenate(mixed, axis=1))

    def back(to):
        rows = pl.ds(pl.multiple_of(to * 256, 256), 256)
        y_send[to] = dot3((inverse[0, rows], inverse[1, rows]), mixed, NT)

    y_copies = []
    for d, to in (teams[1], teams[0], teams[2]):
        back(to)
        y_copies.append((d, send(y_send.at[to], y_got.at[team], y_sem, d, role, place(to, slab))))
    back(team)
    y_got[team] = y_send[team]
    a = swap_arrival(0, a_rows)
    for k in range(PAIRS):
        out_sum[k] = jnp.zeros((8, AREA), jnp.float32)

    def forward(q):
        rows = jnp.concatenate([y_got[q, :TILE], y_got[q, TILE:]], axis=1)
        slope[q] = dot3(split(rows), (plane[0], plane[1]))
        channels = pl.ds(pl.multiple_of(q * PART, PART), PART)
        by_seen = [seen_wide[i, channels] for i in range(3)]
        by_proj = [proj_wide[j, channels] for j in range(3)]

        def gelu(z, carry):
            at = pl.ds(pl.multiple_of(z * PART, PART), PART)
            for k in range(8):
                lanes = slice(k * TILE, (k + 1) * TILE)
                x = slope[q, at, lanes]
                for i in range(3):
                    x = x + by_seen[i] * a_rows[z * 3 + i, k : k + 1]
                square = x * x
                t = jnp.tanh(x * (root + (root * 0.044715) * square))
                half = 0.5 + 0.5 * t
                value = x * half
                act[q, at, lanes] = value
                slope[q, at, lanes] = half + value * (1.0 - t) * (root + (root * 3.0 * 0.044715) * square)
                for j in range(3):
                    term = by_proj[j] * value
                    out_sum[z * 3 + j, :, lanes] += term[:8] + term[8:]
            return carry

        lax.fori_loop(0, PLANES, gelu, 0)

    forward(team)
    for n, (d, copy) in enumerate(y_copies):
        copy.wait_recv()
        if n == 1:
            a_copies = [send(a_send.at[:, to], a_got.at[yx], a_sem, d, role, to_spot(to)) for d, to in spots]
            a_got[yx] = a_send[:, yx]
        forward((team + ROLES - d) % ROLES)

    wanted = swap_arrival(1, t_rows)
    out = jnp.concatenate([jnp.sum(out_sum[k], axis=0, keepdims=True) for k in range(PAIRS)], axis=0)
    error = a + out - wanted
    doubled = 2.0 * error
    for k in range(8):
        twice[:, k] = doubled[:, k * TILE : (k + 1) * TILE]

    def backward(q):
        channels = pl.ds(pl.multiple_of(q * PART, PART), PART)
        by_proj = [proj_wide[j, channels] for j in range(3)]

        def chain(z, carry):
            at = pl.ds(pl.multiple_of(z * PART, PART), PART)
            for k in range(8):
                lanes = slice(k * TILE, (k + 1) * TILE)
                g = by_proj[0] * twice[z * 3, k : k + 1]
                for j in range(1, 3):
                    g = g + by_proj[j] * twice[z * 3 + j, k : k + 1]
                g = g * slope[q, at, lanes]
                slope[q, at, lanes] = g
                g_high[at, lanes], g_low[at, lanes] = split(g)
            return carry

        lax.fori_loop(0, PLANES, chain, 0)
        g_send[q] = dot3((g_high[...], g_low[...]), (plane[0], plane[1]), NT)

    g_copies = []
    for d, to in (teams[1], teams[0], teams[2]):
        backward(to)
        g_copies.append(send(g_send.at[to], g_got.at[team], g_sem, d, role, place(to, slab)))
    backward(team)
    g_got[team] = g_send[team]

    row_8 = lax.broadcasted_iota(jnp.int32, (8, TILE), 0)
    lane = lax.broadcasted_iota(jnp.int32, (8, TILE), 1)
    zero = jnp.zeros((8, TILE), jnp.float32)
    wide = jnp.zeros((PART, TILE), jnp.float32)

    def cells(q, carry):
        def over(z, sums):
            at = pl.ds(pl.multiple_of(z * PART, PART), PART)
            sums = list(sums)
            for k in range(8):
                lanes = slice(k * TILE, (k + 1) * TILE)
                g, value = slope[q, at, lanes], act[q, at, lanes]
                for i in range(3):
                    sums[i] = sums[i] + g * a_rows[z * 3 + i, k : k + 1]
                    sums[3 + i] = sums[3 + i] + value * twice[z * 3 + i, k : k + 1]
            return tuple(sums)

        return lax.fori_loop(0, PLANES, over, (wide,) * 6)

    by_quarter = [cells(q, 0) for q in range(ROLES)]

    def channel_rows(k, row):
        column = jnp.concatenate([sums[k] for sums in by_quarter], axis=0)
        return dot(jnp.where(row_8 == row, 1.0, 0.0), column, NT)

    cross_rows = sum(channel_rows(i, i) for i in range(3))
    proj_rows = sum(channel_rows(3 + j, j) for j in range(3))
    sse = jnp.sum(error * error, keepdims=True)

    for copy in g_copies:
        copy.wait_recv()
    stacked = jnp.concatenate([g_got[b][:, h * TILE : (h + 1) * TILE] for b in range(ROLES) for h in range(2)], axis=0)
    grad = dot3(split(stacked), (inverse[0], inverse[1]), TN)
    for s in range(SH):
        blocks_out(m_send, s, grad[:, s * TILE : (s + 1) * TILE])
    m_copies = [send(m_send.at[:, to], m_got.at[yx], m_sem, d, role, to_spot(to)) for d, to in spots]
    m_got[yx] = m_send[:, yx]
    for copy in a_copies:
        copy.wait_recv()
    a_all = split(a_got[...].reshape(SLABS * 8, TILE))
    a_all = dot2(a_all, expand[...])
    for i in range(3):
        a_wide[i] = a_all[:, i * TILE : (i + 1) * TILE].reshape(YX, ROLES, 8, TILE)
    for copy in m_copies:
        copy.wait_recv()

    crossed = []
    for b in range(ROLES):
        sums = [zero, zero, zero]
        for k in range(YX):
            g = m_got[k, b]
            sums = [sums[i] + a_wide[i, k, b] * g for i in range(3)]
        crossed.append(jnp.concatenate(sums, axis=1))
    crossed = dot2(split(jnp.concatenate(crossed, axis=0)), sort[...])
    for b in range(ROLES):
        for k in range(ROLES):
            r_send[k, b] = crossed[b * 8 : b * 8 + 8, k * TILE : (k + 1) * TILE]
    r_copies = [
        send(r_send.at[to // ROLES, to % ROLES], r_got.at[role, team], back_sem, d, to // ROLES, place(to % ROLES, slab))
        for d, to in crew
    ]
    r_got[role, team] = r_send[role, team]
    for copy in r_copies:
        copy.wait_recv()
    joined = [(r_got[0, q] + r_got[1, q]) + (r_got[2, q] + r_got[3, q]) for q in range(ROLES)]
    joined = dot2(split(jnp.concatenate(joined, axis=1)), sort[...], NT)
    squares = jnp.zeros((WIDTH, TILE), jnp.float32)
    lift_sum = [jnp.zeros((WIDTH, WIDTH), jnp.float32)] * 3
    for k in range(8):
        rows = [joined[k : k + 1, i * TILE : (i + 1) * TILE] for i in range(3)]
        value = lift_t[:, 0:1] * rows[0] + lift_t[:, 1:2] * rows[1] + lift_t[:, 2:3] * rows[2]
        raw[k] = value
        squares = squares + value * value
        for i in range(3):
            lift_sum[i] = lift_sum[i] + (
                spectral[k] * rows[i][:, :WIDTH] + spectral[8 + k] * rows[i][:, WIDTH:]
            )
    raw_copy = fetch(1, raw, raw_out)
    left = cross_rows
    for i in range(3):
        left = left + dot(jnp.where(row_8[:, :WIDTH] == 3 + i, 1.0, 0.0), lift_sum[i], NT)
    tile = jnp.concatenate([left, proj_rows], axis=1)
    tile = tile + jnp.where((row_8 == 6) & (lane == patch), sse, 0.0)
    tile = tile + jnp.where(row_8 == 7, jnp.sum(squares, keepdims=True), 0.0)

    s_crew[role, team] = tile
    copies = [
        send(s_crew.at[role, team], s_crew.at[role, team], sc_sem, d, to // ROLES, place(to % ROLES, slab))
        for d, to in crew
    ]
    for copy in copies:
        copy.wait_recv()
    s_yx[yx] = jnp.sum(s_crew[...], axis=(0, 1))
    copies = [send(s_yx.at[yx], s_yx.at[yx], sy_sem, d, role, to_spot(to)) for d, to in spots]
    for copy in copies:
        copy.wait_recv()
    tile_out[...] = jnp.sum(s_yx[...], axis=0)

    for copy in pending:
        copy.wait_send()
    second_copy.wait()
    raw_copy.wait()
    to_after.wait_send()
    to_before.wait_send()

    @pl.when(role > 0)
    def _():
        to_below(0).wait_send()
        to_below(1).wait_send()
        corner(False, True, 0).wait_send()
        corner(False, False, 1).wait_send()

    @pl.when(role < ROLES - 1)
    def _():
        to_above(0).wait_send()
        to_above(1).wait_send()
        corner(True, True, 2).wait_send()
        corner(True, False, 3).wait_send()

    for k in range(ROLES):

        @pl.when(jnp.logical_not(home & (k == role)))
        def _():
            band_copy(k).wait_send()

    @pl.when(jnp.logical_not(home))
    def _():
        swap(0).wait_send()
        swap(1).wait_send()


def result(*shape):
    return jax.ShapeDtypeStruct(shape, jnp.float32)


def step(anchors, velocity, spectral, lift, mix, proj):
    vmem = pl.BlockSpec(memory_space=pltpu.VMEM)
    anywhere = pl.BlockSpec(memory_space=pltpu.HBM)
    dma = pltpu.SemaphoreType.DMA

    def room(*shape):
        return pltpu.VMEM(shape, jnp.float32)

    def narrow(*shape):
        return pltpu.VMEM(shape, jnp.bfloat16)

    return pl.pallas_call(
        step_kernel,
        out_shape=(result(3, PLANES, 64, TILE), result(8, WIDTH, TILE), result(8, TILE)),
        in_specs=[pl.BlockSpec(memory_space=pltpu.SMEM)] + [anywhere] * 10,
        out_specs=(anywhere, anywhere, vmem),
        scratch_shapes=[
            room(3, 12, ROWS, TILE),
            room(3, 12, ROWS, TILE),
            room(3, PLANES, 64, TILE),
            room(MODES, WIDTH, WIDTH),
            room(3, WIDTH),
            room(WIDTH, WIDTH),
            room(3, WIDTH),
            narrow(2, 256, AREA),
            narrow(2, 2 * ROLES * PAIRS, 4 * SH * TILE),
            narrow(2, ROLES * 256, SH * TILE),
            narrow(TILE, 3 * TILE),
            narrow(3 * TILE, ROLES * TILE),
            room(ROLES, 8, TILE),
            room(ROLES, ROLES, 8, TILE),
            room(ROLES, YX, 3, 8, TILE),
            narrow(2, 12, 16, TILE),
            narrow(2, 12, 16, TILE),
            room(PAIRS, 8, TILE),
            room(PAIRS, 8, TILE),
            room(PAIRS, 256),
            room(ROLES, PAIRS, 256),
            room(ROLES, YX, 8, TILE),
            room(YX, ROLES, 8, TILE),
            room(3, YX, ROLES, 8, TILE),
            room(ROLES, 256, TILE),
            room(ROLES, 256, TILE),
            room(3, WIDTH, TILE),
            room(3, WIDTH, TILE),
            room(ROLES, TILE, AREA),
            room(ROLES, TILE, AREA),
            narrow(TILE, AREA),
            narrow(TILE, AREA),
            room(PAIRS, 8, AREA),
            room(PAIRS, 8, TILE),
            room(ROLES, TILE, 256),
            room(ROLES, TILE, 256),
            room(ROLES, YX, 8, TILE),
            room(YX, ROLES, 8, TILE),
            room(ROLES, ROLES, 8, TILE),
            room(ROLES, ROLES, 8, TILE),
            room(8, WIDTH, TILE),
            room(ROLES, ROLES, 8, TILE),
            room(YX, 8, TILE),
            dma((10,)),
            dma((2, 4)),
            dma((2, 2)),
            dma((2, 4)),
            dma((2, CREW)),
            dma((2, 2)),
            dma((2, YX)),
            dma((2, ROLES)),
            dma((2, ROLES)),
            dma((2, ROLES)),
            dma((2, YX)),
            dma((2, YX)),
            dma((2, CREW)),
            dma((2, CREW)),
            dma((2, YX)),
        ],
        compiler_params=pltpu.CompilerParams(
            collective_id=0, has_side_effects=True, vmem_limit_bytes=63 * 2**20
        ),
    )(anchors, velocity, spectral, lift, mix, proj, *tables())


def finish_kernel(
    second, raw, tile, lift, mix, table, second_out, loss_out, lift_out, mix_out, proj_out, spec_out, held, copy_sem
):
    fetches = [pltpu.make_async_copy(second.at[c], held.at[c], copy_sem.at[0, c]) for c in range(3)]
    stores = [pltpu.make_async_copy(held.at[c], second_out.at[c], copy_sem.at[1, c]) for c in range(3)]
    for copy in fetches:
        copy.start()

    for get, put in zip(fetches, stores):
        get.wait()
        put.start()

    def normal(total):
        mean = jnp.sum(total * total, keepdims=True) / total.size
        return total / jnp.sqrt(mean + tiny_eps)

    cross = tile[0:3, :WIDTH]
    proj_out[...] = normal(tile[0:3, WIDTH:])
    lift_out[...] = normal(tile[3:6, :WIDTH] + dot(cross, mix[...], NT))
    mix_out[...] = normal(dot(lift[...], cross, TN))
    scale = 1.0 / jnp.sqrt(tile[7:8, 0:1] / (MODES**3 * WIDTH * WIDTH) + tiny_eps)
    for k in range(8):
        value = raw[k] * scale
        spec_out[k] = value[:, :WIDTH]
        spec_out[8 + k] = value[:, WIDTH:]
    losses = tile[6:7, :] / (3.0 * PATCH**3)
    lanes = lax.broadcasted_iota(jnp.int32, (1, TILE), 1)
    found = [jnp.sum(jnp.where(lanes == table[0:1, k : k + 1], losses, 0.0), axis=1, keepdims=True) for k in range(2)]
    loss_out[...] = jnp.concatenate(found, axis=1)
    for copy in stores:
        copy.wait()


def finish(second, raw, tile, lift, mix, table):
    vmem = pl.BlockSpec(memory_space=pltpu.VMEM)
    anywhere = pl.BlockSpec(memory_space=pltpu.HBM)
    return pl.pallas_call(
        finish_kernel,
        out_shape=(
            result(3, PLANES, 64, TILE),
            result(1, 2),
            result(3, WIDTH),
            result(WIDTH, WIDTH),
            result(3, WIDTH),
            result(MODES, WIDTH, WIDTH),
        ),
        in_specs=[anywhere] + [vmem] * 5,
        out_specs=(anywhere,) + (vmem,) * 5,
        scratch_shapes=[pltpu.VMEM((3, PLANES, 64, TILE), jnp.float32), pltpu.SemaphoreType.DMA((2, 3))],
    )(second, raw, tile, lift, mix, table)


def on_device(velocity, anchors, slot_table, lift, mix, proj, spectral):
    second, raw, tile = step(anchors, velocity, spectral, lift, mix, proj)
    return finish(second, raw, tile, lift, mix, slot_table)


def solution(mesh):
    return jax.shard_map(
        on_device,
        mesh=mesh,
        in_specs=(
            P(None, "role", "slab", None),
            P("slab", None),
            P("slab", None),
            P(),
            P(),
            P(),
            P(("role", "slab"), None, None),
        ),
        out_specs=(
            P(None, "role", "slab", None),
            P("slab", None),
            P(),
            P(),
            P(),
            P(("role", "slab"), None, None),
        ),
        check_vma=False,
    )
```

```python
import math

import jax
import jax.numpy as jnp
import numpy as np
from jax import lax
from jax.experimental import pallas as pl
from jax.experimental.pallas import tpu as pltpu
from jax.sharding import PartitionSpec as P

MODES = 16
PATCH = 32
AREA = PATCH * PATCH
ROLES = 4
SLABS = 64
YX = 16
CREW = 16
PLANES = 8
WIDTH = 64
PART = WIDTH // ROLES
SH = 4
TILE = 128
PAIRS = 3 * PLANES

time_step = 0.1
viscosity = 1.5
tiny_eps = 1e-06
exact = lax.Precision.HIGHEST
MESH = pl.DeviceIdType.MESH
root = math.sqrt(2.0 / math.pi)
NN = (((1,), (0,)), ((), ()))
NT = (((1,), (1,)), ((), ()))
TN = (((0,), (0,)), ((), ()))


def dot(a, b, dims=NN):
    return lax.dot_general(a, b, dims, precision=exact, preferred_element_type=jnp.float32)


def split(value):
    high = value.astype(jnp.bfloat16)
    return high, (value - high.astype(jnp.float32)).astype(jnp.bfloat16)


def pass_(a, b, dims):
    return lax.dot_general(a, b, dims, preferred_element_type=jnp.float32)


def dot3(a, b, dims=NN):
    return pass_(a[0], b[0], dims) + (pass_(a[0], b[1], dims) + pass_(a[1], b[0], dims))


def dot2(a, exact_b, dims=NN):
    return pass_(a[0], exact_b, dims) + pass_(a[1], exact_b, dims)


def fourier_table():
    order = np.arange(MODES)[:, None]
    points = np.arange(PATCH)[None, :]
    angles = 2.0 * math.pi * ((order + 1) // 2) * points / PATCH
    waves = np.where((order % 2 == 1) | (order == 0), np.cos(angles), np.sin(angles))
    return waves * np.where(order == 0, math.sqrt(1.0 / PATCH), math.sqrt(2.0 / PATCH))


def pair(table):
    table = table.astype(np.float32)
    high = table.astype(jnp.bfloat16)
    return jnp.asarray(np.stack([high, (table - high.astype(np.float32)).astype(jnp.bfloat16)]))


def tables():
    phi = fourier_table()
    over_x = phi.reshape(2, 4, 2, 4, 8)
    over_y = phi.reshape(2, 8, PATCH)
    plane = np.einsum("axchl,gky->gcaxklhy", over_x, over_y).reshape(256, AREA)
    phi_z = phi.reshape(ROLES, SH, ROLES, PLANES)
    eye2, eye3, eye4, eye16 = np.eye(2), np.eye(3), np.eye(ROLES), np.eye(PART)
    ones = np.ones(PART)
    spread = np.einsum("hg,rsbz,ij,c->hbzijsgrc", eye2, phi_z, eye3, ones).reshape(2 * ROLES * PAIRS, 3 * SH * TILE)
    short = np.einsum("hg,rsbz,ij->hbzisjgr", eye2, phi_z, eye3).reshape(2 * ROLES * PAIRS, SH, 24)
    short = np.pad(short, ((0, 0), (0, 0), (0, TILE - 24))).reshape(-1, SH * TILE)
    inverse = np.einsum("hg,rsbz,cd->bhzcsgrd", eye2, phi_z, eye16).reshape(ROLES * 256, SH * TILE)
    expand = np.einsum("ij,hg,rs,c->ihrjgsc", eye3, eye2, eye4, ones).reshape(24, 3 * TILE)
    expand = np.pad(expand, ((0, TILE - 24), (0, 0)))
    sort = np.einsum("ij,hg,rs,cd->ihrcsjgd", eye3, eye2, eye4, eye16).reshape(3 * TILE, ROLES, 96)
    sort = np.pad(sort, ((0, 0), (0, 0), (0, TILE - 96))).reshape(3 * TILE, ROLES * TILE)
    return [pair(plane), pair(plane.T), pair(np.concatenate([spread, short], axis=1)), pair(inverse), jnp.asarray(expand, jnp.bfloat16), jnp.asarray(sort, jnp.bfloat16)]


def place(team, slab):
    return team // 2 * 32 + slab % 32 // 2 * 2 + team % 2


ROWS = 96


def step_kernel(
    anchors, vel, spectral_in, lift_in, mix_in, proj_in, plane_in, across_in, spread_in, inverse_in, expand_in, sort_in,
    second_out, raw_out, tile_out,
    ext, mid, after_two, spectral, lift, mix, proj, plane, across, spread, inverse, expand, sort,
    w_send, w_in, w_all, cut_out, cut_in, a_rows, t_rows, band, bands, a_send, a_got, a_wide, y_send, y_got,
    seen_wide, proj_wide, act, slope, g_high, g_low, out_sum, twice, g_send, g_got, m_send, m_got, r_send, r_got, raw,
    s_crew, s_yx,
    local_sem, z_sem, x_sem, c_sem, cross_sem, swap_sem, wy_sem, band_sem, y_sem, g_sem, a_sem, m_sem, back_sem,
    sc_sem, sy_sem,
):
    role, slab = lax.axis_index("role"), lax.axis_index("slab")
    yx = slab % 32 // 2
    team = slab // 32 * 2 + slab % 2
    patch = role // 2 * 32 + yx * 2 + role % 2
    after, before = (slab + 1) % SLABS, (slab + SLABS - 1) % SLABS
    teams = [(d, (team + d) % ROLES) for d in range(1, ROLES)]
    crew = [(d, (role * ROLES + team + d) % CREW) for d in range(1, CREW)]
    spots = [(d, (yx + d) % YX) for d in range(1, YX)]
    home = role == team
    pending = []

    def remote(src, dst, send_sem, recv_sem, to_role, to_slab):
        return pltpu.make_async_remote_copy(
            src_ref=src, dst_ref=dst, send_sem=send_sem, recv_sem=recv_sem,
            device_id=(to_role, to_slab), device_id_type=MESH,
        )

    def to_spot(at):
        return slab // 32 * 32 + at * 2 + slab % 2

    def send(src, dst, sems, d, to_role, to_slab):
        copy = remote(src, dst, sems.at[0, d], sems.at[1, d], to_role, to_slab)
        copy.start()
        pending.append(copy)
        return copy

    def fetch(at, src, dst):
        copy = pltpu.make_async_copy(src, dst, local_sem.at[at])
        copy.start()
        return copy

    own = fetch(0, vel, ext.at[:, pl.ds(2, PLANES), pl.ds(16, 64)])
    fetched = [
        fetch(1, spectral_in, spectral), fetch(2, lift_in, lift), fetch(3, mix_in, mix), fetch(4, proj_in, proj),
        fetch(9, sort_in, sort),
    ]
    later = [
        fetch(5, plane_in, plane), fetch(10, across_in, across), fetch(6, spread_in, spread), fetch(7, inverse_in, inverse), fetch(8, expand_in, expand)
    ]

    barrier = pltpu.get_barrier_semaphore()

    def greet(to_role, to_slab):
        pl.semaphore_signal(barrier, inc=1, device_id=(to_role, to_slab), device_id_type=MESH)

    greet(role, after)
    greet(role, before)

    @pl.when(role > 0)
    def _():
        greet(role - 1, after)
        greet(role - 1, before)

    @pl.when(role < ROLES - 1)
    def _():
        greet(role + 1, after)
        greet(role + 1, before)

    for _, to in crew:
        greet(to // ROLES, place(to % ROLES, slab))
    for _, to in spots:
        greet(role, to_spot(to))

    for copy in fetched:
        copy.wait()
    row_ky = lax.broadcasted_iota(jnp.int32, (MODES, MODES * WIDTH), 0)
    lane_ky = lax.broadcasted_iota(jnp.int32, (MODES, MODES * WIDTH), 1) // WIDTH
    twin = jnp.concatenate([lift[...], lift[...]], axis=1)
    long = jnp.concatenate([twin] * (MODES // 2), axis=1)
    blocks = [jnp.where(row_ky == lane_ky, long[i : i + 1], 0.0) for i in range(3)]
    lifted = dot3(
        split(jnp.concatenate(blocks, axis=0)), split(spectral[...].reshape(MODES * WIDTH, WIDTH))
    )
    lifted = lifted.reshape(3, 2, 8, WIDTH)
    lifted = jnp.concatenate([lifted[i, h] for i in range(3) for h in range(2)], axis=1)
    lifted = dot2(split(lifted), sort[...])
    for k in range(ROLES):
        w_send[k] = lifted[:, k * TILE : (k + 1) * TILE]

    pl.semaphore_wait(barrier, 34 + 2 * ((role + 1) // 2 % 2))

    o_copies = [
        send(w_send.at[to % ROLES], w_in.at[team, role], cross_sem, d, to // ROLES, place(to % ROLES, slab))
        for d, to in crew
    ]
    w_in[team, role] = w_send[team]

    def to_below(k):
        return remote(
            vel.at[:, pl.ds(k, 1)], ext.at[:, pl.ds(10 + k, 1), pl.ds(16, 64)],
            z_sem.at[0, k], z_sem.at[1, k], role - 1, slab,
        )

    def to_above(k):
        return remote(
            vel.at[:, pl.ds(7 - k, 1)], ext.at[:, pl.ds(1 - k, 1), pl.ds(16, 64)],
            z_sem.at[0, 2 + k], z_sem.at[1, 2 + k], role + 1, slab,
        )

    def corner(up, right, at):
        plane_at, slot = (7, 1) if up else (0, 10)
        row, spot = (56, 8) if right else (0, 80)
        return remote(
            vel.at[:, pl.ds(plane_at, 1), pl.ds(row, 8)], ext.at[:, pl.ds(slot, 1), pl.ds(spot, 8)],
            c_sem.at[0, at], c_sem.at[1, at], role + 1 if up else role - 1, after if right else before,
        )

    to_after = remote(
        vel.at[:, :, pl.ds(56, 8)], ext.at[:, pl.ds(2, PLANES), pl.ds(8, 8)],
        x_sem.at[0, 0], x_sem.at[1, 0], role, after,
    )
    to_before = remote(
        vel.at[:, :, pl.ds(0, 8)], ext.at[:, pl.ds(2, PLANES), pl.ds(80, 8)],
        x_sem.at[0, 1], x_sem.at[1, 1], role, before,
    )

    @pl.when(role > 0)
    def _():
        to_below(0).start()

    @pl.when(role < ROLES - 1)
    def _():
        to_above(0).start()

    to_after.start()
    to_before.start()

    @pl.when(role > 0)
    def _():
        to_below(1).start()
        corner(False, True, 0).start()
        corner(False, False, 1).start()

    @pl.when(role < ROLES - 1)
    def _():
        to_above(1).start()
        corner(True, True, 2).start()
        corner(True, False, 3).start()

    @pl.when(role == 0)
    def _():
        ext[:, pl.ds(0, 2)] = jnp.zeros((3, 2, ROWS, TILE), jnp.float32)

    @pl.when(role == ROLES - 1)
    def _():
        ext[:, pl.ds(10, 2)] = jnp.zeros((3, 2, ROWS, TILE), jnp.float32)

    seen = dot(mix[...], lift[...], (((0,), (1,)), ((), ())))
    unit = jnp.where(
        lax.broadcasted_iota(jnp.int32, (3, 3), 0) == lax.broadcasted_iota(jnp.int32, (3, 3), 1), 1.0, 0.0
    )
    proj_t = dot(proj[...], unit, TN)
    lift_t = dot(lift[...], unit, TN)
    for i in range(3):
        seen_wide[i] = jnp.broadcast_to(seen[:, i : i + 1], (WIDTH, TILE))
        proj_wide[i] = jnp.broadcast_to(proj_t[:, i : i + 1], (WIDTH, TILE))

    lane_80 = lax.broadcasted_iota(jnp.int32, (80, TILE), 1)
    lane_64 = lax.broadcasted_iota(jnp.int32, (64, TILE), 1)
    lane_8 = lax.broadcasted_iota(jnp.int32, (8, TILE), 1)

    def advance(field, z, row, count, lane):
        centre = [field[c, z, pl.ds(row, count)] for c in range(3)]
        out = []
        for c in range(3):
            here = centre[c]
            z_next, z_prev = field[c, z + 1, pl.ds(row, count)], field[c, z - 1, pl.ds(row, count)]
            x_next, x_prev = field[c, z, pl.ds(row + 1, count)], field[c, z, pl.ds(row - 1, count)]
            y_next = jnp.where(lane == TILE - 1, 0.0, pltpu.roll(here, TILE - 1, 1))
            y_prev = jnp.where(lane == 0, 0.0, pltpu.roll(here, 1, 1))
            laplace = z_next + z_prev + x_next + x_prev + y_next + y_prev - 6.0 * here
            carried = 0.5 * (
                centre[0] * (z_next - z_prev) + centre[1] * (x_next - x_prev) + centre[2] * (y_next - y_prev)
            )
            out.append(here + time_step * (viscosity * laplace - carried))
        return out

    own.wait()
    to_after.wait_recv()
    to_before.wait_recv()

    def inner(z, carry):
        out = advance(ext, z, 8, 80, lane_80)
        for c in range(3):
            mid[c, z, pl.ds(8, 80)] = out[c]
        return carry

    lax.fori_loop(3, 9, inner, 0)

    for copy in o_copies:
        copy.wait_recv()
    lifted = [jnp.concatenate([w_in[k, r] for r in range(ROLES)], axis=1) for k in range(ROLES)]
    lifted = dot2(split(jnp.concatenate(lifted, axis=0)), sort[...], NT)
    for k in range(ROLES):
        for i in range(3):
            w_all[k, yx, i] = lifted[k * 8 : k * 8 + 8, i * TILE : (i + 1) * TILE]
    w_copies = [send(w_all.at[:, yx], w_all.at[:, yx], wy_sem, d, role, to_spot(to)) for d, to in spots]

    @pl.when(role > 0)
    def _():
        to_above(0).wait_recv()

    @pl.when(role < ROLES - 1)
    def _():
        to_below(0).wait_recv()

    for z in (2, 9):
        out = advance(ext, z, 16, 64, lane_64)
        for c in range(3):
            mid[c, z, pl.ds(16, 64)] = out[c]


    x_at, y_at = anchors[0, 0], anchors[0, 1]
    from_lane = lax.broadcasted_iota(jnp.int32, (TILE, TILE), 0)
    to_lane = lax.broadcasted_iota(jnp.int32, (TILE, TILE), 1)
    chosen = [
        jnp.where((from_lane == to_lane % PATCH + y_at) & (to_lane // PATCH == k), 1.0, 0.0).astype(jnp.bfloat16)
        for k in range(4)
    ]

    def cut(field, first_row, first_plane, at):
        total = None
        for k in range(4):
            rows = [
                field[c, z + first_plane, pl.ds(first_row + x_at + 8 * k, 8), :]
                for z in range(PLANES)
                for c in range(3)
            ]
            part = pass_(jnp.concatenate(rows, axis=0).astype(jnp.bfloat16), chosen[k], NN)
            total = part if total is None else total + part
        cut_out[at] = total.astype(jnp.bfloat16).reshape(12, 16, TILE)

    def swap(at):
        return remote(
            cut_out.at[at], cut_in.at[at], swap_sem.at[0, at], swap_sem.at[1, at], team, place(role, slab)
        )

    def swap_start(at):
        @pl.when(jnp.logical_not(home))
        def _():
            swap(at).start()

        @pl.when(home)
        def _():
            cut_in[at] = cut_out[at]

    def swap_arrival(at, rows):
        @pl.when(jnp.logical_not(home))
        def _():
            swap(at).wait_recv()

        rows[...] = cut_in[at].astype(jnp.float32).reshape(PAIRS, 8, TILE)
        return jnp.concatenate([rows[:, k] for k in range(8)], axis=1)

    cut(mid, 16, 2, 0)

    t_rows[...] = cut_out[0].astype(jnp.float32).reshape(PAIRS, 8, TILE)
    cells_here = jnp.concatenate([t_rows[:, k] for k in range(8)], axis=1).astype(jnp.bfloat16)
    for copy in later:
        copy.wait()
    band[...] = pass_(cells_here, across[0], NN) + pass_(cells_here, across[1], NN)

    def band_copy(k):
        return remote(band, bands.at[role], band_sem.at[0, k], band_sem.at[1, role], team, place(k, slab))

    def band_arrival(k):
        return remote(band, bands.at[k], band_sem.at[0, k], band_sem.at[1, k], team, place(k, slab))

    for k in range(ROLES):

        @pl.when(jnp.logical_not(home & (k == role)))
        def _():
            band_copy(k).start()

    @pl.when(home)
    def _():
        bands[role] = band[...]

    swap_start(0)

    @pl.when(role > 0)
    def _():
        to_above(1).wait_recv()
        corner(True, True, 2).wait_recv()
        corner(True, False, 3).wait_recv()
        out = advance(ext, 1, 16, 64, lane_64)
        for c in range(3):
            mid[c, 1, pl.ds(16, 64)] = out[c]

    @pl.when(role < ROLES - 1)
    def _():
        to_below(1).wait_recv()
        corner(False, True, 0).wait_recv()
        corner(False, False, 1).wait_recv()
        out = advance(ext, 10, 16, 64, lane_64)
        for c in range(3):
            mid[c, 10, pl.ds(16, 64)] = out[c]

    for z in (2, 9):
        for row in (8, 80):
            out = advance(ext, z, row, 8, lane_8)
            for c in range(3):
                mid[c, z, pl.ds(row, 8)] = out[c]

    @pl.when(role == 0)
    def _():
        mid[:, 1, pl.ds(16, 64)] = jnp.zeros((3, 64, TILE), jnp.float32)

    @pl.when(role == ROLES - 1)
    def _():
        mid[:, 10, pl.ds(16, 64)] = jnp.zeros((3, 64, TILE), jnp.float32)

    def outer(z, carry):
        out = advance(mid, z, 16, 64, lane_64)
        for c in range(3):
            after_two[c, z - 2] = out[c]
        return carry

    lax.fori_loop(2, 6, outer, 0)
    lax.fori_loop(6, 10, outer, 0)
    second_copy = fetch(0, after_two, second_out)
    cut(after_two, 0, 0, 1)
    swap_start(1)

    for k in range(ROLES):

        @pl.when(jnp.logical_not(home & (k == role)))
        def _():
            band_arrival(k).wait_recv()

    every = jnp.concatenate([bands[b] for b in range(ROLES)], axis=0)
    halves = jnp.concatenate([every[:, :TILE], every[:, TILE:]], axis=0)
    coef = dot3(split(halves), (spread[0], spread[1]), TN)
    for copy in w_copies:
        copy.wait_recv()

    def blocks_out(ref, s, part):
        part = part.reshape(2, 8, 8, TILE)
        for core in range(2):
            ref[s // 2 * 2 + core, pl.ds(s % 2 * 8, 8)] = part[core]

    mixed = []
    for s in range(SH):
        at = (3 * SH + s) * TILE
        blocks_out(a_send, s, coef[:, at : at + TILE])
        total = None
        for i in range(3):
            at = (i * SH + s) * TILE
            weights = jnp.concatenate(
                [w_all[s // 2 * 2 + core, pl.ds(s % 2 * 8, 8), i].reshape(64, TILE) for core in range(2)], axis=0
            )
            term = coef[:, at : at + TILE] * weights
            total = term if total is None else total + term
        mixed.append(total)
    mixed = split(jnp.concatenate([part.T for part in mixed], axis=0))

    def back(to):
        rows = pl.ds(pl.multiple_of(to * 256, 256), 256)
        y_send[to] = dot3((inverse[0, rows], inverse[1, rows]), mixed)

    y_copies = []
    for d, to in (teams[1], teams[0], teams[2]):
        back(to)
        y_copies.append((d, send(y_send.at[to], y_got.at[team], y_sem, d, role, place(to, slab))))
    back(team)
    y_got[team] = y_send[team]
    a = swap_arrival(0, a_rows)
    for k in range(PAIRS):
        out_sum[k] = jnp.zeros((8, AREA), jnp.float32)

    def forward(q):
        rows = jnp.concatenate([y_got[q, :TILE], y_got[q, TILE:]], axis=1)
        slope[q] = dot3(split(rows), (plane[0], plane[1]))
        channels = pl.ds(pl.multiple_of(q * PART, PART), PART)
        by_seen = [seen_wide[i, channels] for i in range(3)]
        by_proj = [proj_wide[j, channels] for j in range(3)]

        def gelu(z, carry):
            at = pl.ds(pl.multiple_of(z * PART, PART), PART)
            for k in range(8):
                lanes = slice(k * TILE, (k + 1) * TILE)
                x = slope[q, at, lanes]
                for i in range(3):
                    x = x + by_seen[i] * a_rows[z * 3 + i, k : k + 1]
                square = x * x
                t = jnp.tanh(x * (root + (root * 0.044715) * square))
                half = 0.5 + 0.5 * t
                value = x * half
                act[q, at, lanes] = value
                slope[q, at, lanes] = half + value * (1.0 - t) * (root + (root * 3.0 * 0.044715) * square)
                for j in range(3):
                    term = by_proj[j] * value
                    out_sum[z * 3 + j, :, lanes] += term[:8] + term[8:]
            return carry

        lax.fori_loop(0, PLANES, gelu, 0)

    forward(team)
    for n, (d, copy) in enumerate(y_copies):
        copy.wait_recv()
        if n == 1:
            a_copies = [send(a_send.at[:, to], a_got.at[yx], a_sem, d, role, to_spot(to)) for d, to in spots]
            a_got[yx] = a_send[:, yx]
        forward((team + ROLES - d) % ROLES)

    wanted = swap_arrival(1, t_rows)
    out = jnp.concatenate([jnp.sum(out_sum[k], axis=0, keepdims=True) for k in range(PAIRS)], axis=0)
    error = a + out - wanted
    doubled = 2.0 * error
    for k in range(8):
        twice[:, k] = doubled[:, k * TILE : (k + 1) * TILE]

    def backward(q):
        channels = pl.ds(pl.multiple_of(q * PART, PART), PART)
        by_proj = [proj_wide[j, channels] for j in range(3)]

        def chain(z, carry):
            at = pl.ds(pl.multiple_of(z * PART, PART), PART)
            for k in range(8):
                lanes = slice(k * TILE, (k + 1) * TILE)
                g = by_proj[0] * twice[z * 3, k : k + 1]
                for j in range(1, 3):
                    g = g + by_proj[j] * twice[z * 3 + j, k : k + 1]
                g = g * slope[q, at, lanes]
                slope[q, at, lanes] = g
                g_high[at, lanes], g_low[at, lanes] = split(g)
            return carry

        lax.fori_loop(0, PLANES, chain, 0)
        g_send[q] = dot3((g_high[...], g_low[...]), (across[0], across[1]))

    g_copies = []
    for d, to in (teams[1], teams[0], teams[2]):
        backward(to)
        g_copies.append(send(g_send.at[to], g_got.at[team], g_sem, d, role, place(to, slab)))
    backward(team)
    g_got[team] = g_send[team]

    row_8 = lax.broadcasted_iota(jnp.int32, (8, TILE), 0)
    lane = lax.broadcasted_iota(jnp.int32, (8, TILE), 1)
    zero = jnp.zeros((8, TILE), jnp.float32)
    wide = jnp.zeros((PART, TILE), jnp.float32)

    def cells(q, carry):
        def over(z, sums):
            at = pl.ds(pl.multiple_of(z * PART, PART), PART)
            sums = list(sums)
            for k in range(8):
                lanes = slice(k * TILE, (k + 1) * TILE)
                g, value = slope[q, at, lanes], act[q, at, lanes]
                for i in range(3):
                    sums[i] = sums[i] + g * a_rows[z * 3 + i, k : k + 1]
                    sums[3 + i] = sums[3 + i] + value * twice[z * 3 + i, k : k + 1]
            return tuple(sums)

        return lax.fori_loop(0, PLANES, over, (wide,) * 6)

    by_quarter = [cells(q, 0) for q in range(ROLES)]

    def channel_rows(k, row):
        column = jnp.concatenate([sums[k] for sums in by_quarter], axis=0)
        return dot(jnp.where(row_8 == row, 1.0, 0.0), column, NT)

    cross_rows = sum(channel_rows(i, i) for i in range(3))
    proj_rows = sum(channel_rows(3 + j, j) for j in range(3))
    sse = jnp.sum(error * error, keepdims=True)

    for copy in g_copies:
        copy.wait_recv()
    stacked = jnp.concatenate([g_got[b][:, h * TILE : (h + 1) * TILE] for b in range(ROLES) for h in range(2)], axis=0)
    grad = dot3(split(stacked), (inverse[0], inverse[1]), TN)
    for s in range(SH):
        blocks_out(m_send, s, grad[:, s * TILE : (s + 1) * TILE])
    m_copies = [send(m_send.at[:, to], m_got.at[yx], m_sem, d, role, to_spot(to)) for d, to in spots]
    m_got[yx] = m_send[:, yx]
    for copy in a_copies:
        copy.wait_recv()
    a_all = split(a_got[...].reshape(SLABS * 8, TILE))
    a_all = dot2(a_all, expand[...])
    for i in range(3):
        a_wide[i] = a_all[:, i * TILE : (i + 1) * TILE].reshape(YX, ROLES, 8, TILE)
    for copy in m_copies:
        copy.wait_recv()

    crossed = []
    for b in range(ROLES):
        sums = [zero, zero, zero]
        for k in range(YX):
            g = m_got[k, b]
            sums = [sums[i] + a_wide[i, k, b] * g for i in range(3)]
        crossed.append(jnp.concatenate(sums, axis=1))
    crossed = dot2(split(jnp.concatenate(crossed, axis=0)), sort[...])
    for b in range(ROLES):
        for k in range(ROLES):
            r_send[k, b] = crossed[b * 8 : b * 8 + 8, k * TILE : (k + 1) * TILE]
    r_copies = [
        send(r_send.at[to // ROLES, to % ROLES], r_got.at[role, team], back_sem, d, to // ROLES, place(to % ROLES, slab))
        for d, to in crew
    ]
    r_got[role, team] = r_send[role, team]
    for copy in r_copies:
        copy.wait_recv()
    joined = [(r_got[0, q] + r_got[1, q]) + (r_got[2, q] + r_got[3, q]) for q in range(ROLES)]
    joined = dot2(split(jnp.concatenate(joined, axis=1)), sort[...], NT)
    squares = jnp.zeros((WIDTH, TILE), jnp.float32)
    lift_sum = [jnp.zeros((WIDTH, WIDTH), jnp.float32)] * 3
    for k in range(8):
        rows = [joined[k : k + 1, i * TILE : (i + 1) * TILE] for i in range(3)]
        value = lift_t[:, 0:1] * rows[0] + lift_t[:, 1:2] * rows[1] + lift_t[:, 2:3] * rows[2]
        raw[k] = value
        squares = squares + value * value
        for i in range(3):
            lift_sum[i] = lift_sum[i] + (
                spectral[k] * rows[i][:, :WIDTH] + spectral[8 + k] * rows[i][:, WIDTH:]
            )
    raw_copy = fetch(1, raw, raw_out)
    left = cross_rows
    for i in range(3):
        left = left + dot(jnp.where(row_8[:, :WIDTH] == 3 + i, 1.0, 0.0), lift_sum[i], NT)
    tile = jnp.concatenate([left, proj_rows], axis=1)
    tile = tile + jnp.where((row_8 == 6) & (lane == patch), sse, 0.0)
    tile = tile + jnp.where(row_8 == 7, jnp.sum(squares, keepdims=True), 0.0)

    s_crew[role, team] = tile
    copies = [
        send(s_crew.at[role, team], s_crew.at[role, team], sc_sem, d, to // ROLES, place(to % ROLES, slab))
        for d, to in crew
    ]
    for copy in copies:
        copy.wait_recv()
    s_yx[yx] = jnp.sum(s_crew[...], axis=(0, 1))
    copies = [send(s_yx.at[yx], s_yx.at[yx], sy_sem, d, role, to_spot(to)) for d, to in spots]
    for copy in copies:
        copy.wait_recv()
    tile_out[...] = jnp.sum(s_yx[...], axis=0)

    for copy in pending:
        copy.wait_send()
    second_copy.wait()
    raw_copy.wait()
    to_after.wait_send()
    to_before.wait_send()

    @pl.when(role > 0)
    def _():
        to_below(0).wait_send()
        to_below(1).wait_send()
        corner(False, True, 0).wait_send()
        corner(False, False, 1).wait_send()

    @pl.when(role < ROLES - 1)
    def _():
        to_above(0).wait_send()
        to_above(1).wait_send()
        corner(True, True, 2).wait_send()
        corner(True, False, 3).wait_send()

    for k in range(ROLES):

        @pl.when(jnp.logical_not(home & (k == role)))
        def _():
            band_copy(k).wait_send()

    @pl.when(jnp.logical_not(home))
    def _():
        swap(0).wait_send()
        swap(1).wait_send()


def result(*shape):
    return jax.ShapeDtypeStruct(shape, jnp.float32)


def step(anchors, velocity, spectral, lift, mix, proj):
    vmem = pl.BlockSpec(memory_space=pltpu.VMEM)
    anywhere = pl.BlockSpec(memory_space=pltpu.HBM)
    dma = pltpu.SemaphoreType.DMA

    def room(*shape):
        return pltpu.VMEM(shape, jnp.float32)

    def narrow(*shape):
        return pltpu.VMEM(shape, jnp.bfloat16)

    return pl.pallas_call(
        step_kernel,
        out_shape=(result(3, PLANES, 64, TILE), result(8, WIDTH, TILE), result(8, TILE)),
        in_specs=[pl.BlockSpec(memory_space=pltpu.SMEM)] + [anywhere] * 11,
        out_specs=(anywhere, anywhere, vmem),
        scratch_shapes=[
            room(3, 12, ROWS, TILE),
            room(3, 12, ROWS, TILE),
            room(3, PLANES, 64, TILE),
            room(MODES, WIDTH, WIDTH),
            room(3, WIDTH),
            room(WIDTH, WIDTH),
            room(3, WIDTH),
            narrow(2, 256, AREA),
            narrow(2, AREA, 256),
            narrow(2, 2 * ROLES * PAIRS, 4 * SH * TILE),
            narrow(2, ROLES * 256, SH * TILE),
            narrow(TILE, 3 * TILE),
            narrow(3 * TILE, ROLES * TILE),
            room(ROLES, 8, TILE),
            room(ROLES, ROLES, 8, TILE),
            room(ROLES, YX, 3, 8, TILE),
            narrow(2, 12, 16, TILE),
            narrow(2, 12, 16, TILE),
            room(PAIRS, 8, TILE),
            room(PAIRS, 8, TILE),
            room(PAIRS, 256),
            room(ROLES, PAIRS, 256),
            room(ROLES, YX, 8, TILE),
            room(YX, ROLES, 8, TILE),
            room(3, YX, ROLES, 8, TILE),
            room(ROLES, 256, TILE),
            room(ROLES, 256, TILE),
            room(3, WIDTH, TILE),
            room(3, WIDTH, TILE),
            room(ROLES, TILE, AREA),
            room(ROLES, TILE, AREA),
            narrow(TILE, AREA),
            narrow(TILE, AREA),
            room(PAIRS, 8, AREA),
            room(PAIRS, 8, TILE),
            room(ROLES, TILE, 256),
            room(ROLES, TILE, 256),
            room(ROLES, YX, 8, TILE),
            room(YX, ROLES, 8, TILE),
            room(ROLES, ROLES, 8, TILE),
            room(ROLES, ROLES, 8, TILE),
            room(8, WIDTH, TILE),
            room(ROLES, ROLES, 8, TILE),
            room(YX, 8, TILE),
            dma((11,)),
            dma((2, 4)),
            dma((2, 2)),
            dma((2, 4)),
            dma((2, CREW)),
            dma((2, 2)),
            dma((2, YX)),
            dma((2, ROLES)),
            dma((2, ROLES)),
            dma((2, ROLES)),
            dma((2, YX)),
            dma((2, YX)),
            dma((2, CREW)),
            dma((2, CREW)),
            dma((2, YX)),
        ],
        compiler_params=pltpu.CompilerParams(
            collective_id=0, has_side_effects=True, vmem_limit_bytes=63 * 2**20
        ),
    )(anchors, velocity, spectral, lift, mix, proj, *tables())


def finish_kernel(
    second, raw, tile, lift, mix, table, second_out, loss_out, lift_out, mix_out, proj_out, spec_out, held, copy_sem
):
    fetches = [pltpu.make_async_copy(second.at[c], held.at[c], copy_sem.at[0, c]) for c in range(3)]
    stores = [pltpu.make_async_copy(held.at[c], second_out.at[c], copy_sem.at[1, c]) for c in range(3)]
    for copy in fetches:
        copy.start()

    for get, put in zip(fetches, stores):
        get.wait()
        put.start()

    def normal(total):
        mean = jnp.sum(total * total, keepdims=True) / total.size
        return total / jnp.sqrt(mean + tiny_eps)

    cross = tile[0:3, :WIDTH]
    proj_out[...] = normal(tile[0:3, WIDTH:])
    lift_out[...] = normal(tile[3:6, :WIDTH] + dot(cross, mix[...], NT))
    mix_out[...] = normal(dot(lift[...], cross, TN))
    scale = 1.0 / jnp.sqrt(tile[7:8, 0:1] / (MODES**3 * WIDTH * WIDTH) + tiny_eps)
    for k in range(8):
        value = raw[k] * scale
        spec_out[k] = value[:, :WIDTH]
        spec_out[8 + k] = value[:, WIDTH:]
    losses = tile[6:7, :] / (3.0 * PATCH**3)
    lanes = lax.broadcasted_iota(jnp.int32, (1, TILE), 1)
    found = [jnp.sum(jnp.where(lanes == table[0:1, k : k + 1], losses, 0.0), axis=1, keepdims=True) for k in range(2)]
    loss_out[...] = jnp.concatenate(found, axis=1)
    for copy in stores:
        copy.wait()


def finish(second, raw, tile, lift, mix, table):
    vmem = pl.BlockSpec(memory_space=pltpu.VMEM)
    anywhere = pl.BlockSpec(memory_space=pltpu.HBM)
    return pl.pallas_call(
        finish_kernel,
        out_shape=(
            result(3, PLANES, 64, TILE),
            result(1, 2),
            result(3, WIDTH),
            result(WIDTH, WIDTH),
            result(3, WIDTH),
            result(MODES, WIDTH, WIDTH),
        ),
        in_specs=[anywhere] + [vmem] * 5,
        out_specs=(anywhere,) + (vmem,) * 5,
        scratch_shapes=[pltpu.VMEM((3, PLANES, 64, TILE), jnp.float32), pltpu.SemaphoreType.DMA((2, 3))],
    )(second, raw, tile, lift, mix, table)


def on_device(velocity, anchors, slot_table, lift, mix, proj, spectral):
    second, raw, tile = step(anchors, velocity, spectral, lift, mix, proj)
    return finish(second, raw, tile, lift, mix, slot_table)


def solution(mesh):
    return jax.shard_map(
        on_device,
        mesh=mesh,
        in_specs=(
            P(None, "role", "slab", None),
            P("slab", None),
            P("slab", None),
            P(),
            P(),
            P(),
            P(("role", "slab"), None, None),
        ),
        out_specs=(
            P(None, "role", "slab", None),
            P("slab", None),
            P(),
            P(),
            P(),
            P(("role", "slab"), None, None),
        ),
        check_vma=False,
    )
```

```python
import math

import jax
import jax.numpy as jnp
import numpy as np
from jax import lax
from jax.experimental import pallas as pl
from jax.experimental.pallas import tpu as pltpu
from jax.sharding import PartitionSpec as P

MODES = 16
PATCH = 32
AREA = PATCH * PATCH
ROLES = 4
SLABS = 64
YX = 16
CREW = 16
PLANES = 8
WIDTH = 64
PART = WIDTH // ROLES
SH = 4
TILE = 128
PAIRS = 3 * PLANES

time_step = 0.1
viscosity = 1.5
tiny_eps = 1e-06
exact = lax.Precision.HIGHEST
MESH = pl.DeviceIdType.MESH
root = math.sqrt(2.0 / math.pi)
NN = (((1,), (0,)), ((), ()))
NT = (((1,), (1,)), ((), ()))
TN = (((0,), (0,)), ((), ()))


def dot(a, b, dims=NN):
    return lax.dot_general(a, b, dims, precision=exact, preferred_element_type=jnp.float32)


def split(value):
    high = value.astype(jnp.bfloat16)
    return high, (value - high.astype(jnp.float32)).astype(jnp.bfloat16)


def pass_(a, b, dims):
    return lax.dot_general(a, b, dims, preferred_element_type=jnp.float32)


def dot3(a, b, dims=NN):
    return pass_(a[0], b[0], dims) + (pass_(a[0], b[1], dims) + pass_(a[1], b[0], dims))


def dot2(a, exact_b, dims=NN):
    return pass_(a[0], exact_b, dims) + pass_(a[1], exact_b, dims)


def fourier_table():
    order = np.arange(MODES)[:, None]
    points = np.arange(PATCH)[None, :]
    angles = 2.0 * math.pi * ((order + 1) // 2) * points / PATCH
    waves = np.where((order % 2 == 1) | (order == 0), np.cos(angles), np.sin(angles))
    return waves * np.where(order == 0, math.sqrt(1.0 / PATCH), math.sqrt(2.0 / PATCH))


def pair(table):
    table = table.astype(np.float32)
    high = table.astype(jnp.bfloat16)
    return jnp.asarray(np.stack([high, (table - high.astype(np.float32)).astype(jnp.bfloat16)]))


def tables():
    phi = fourier_table()
    over_x = phi.reshape(2, 4, 2, 4, 8)
    over_y = phi.reshape(2, 8, PATCH)
    plane = np.einsum("axchl,gky->gcaxklhy", over_x, over_y).reshape(256, AREA)
    phi_z = phi.reshape(ROLES, SH, ROLES, PLANES)
    eye2, eye3, eye4, eye16 = np.eye(2), np.eye(3), np.eye(ROLES), np.eye(PART)
    ones = np.ones(PART)
    spread = np.einsum("hg,rsbz,ij,c->hbzijsgrc", eye2, phi_z, eye3, ones).reshape(2 * ROLES * PAIRS, 3 * SH * TILE)
    short = np.einsum("hg,rsbz,ij->hbzisjgr", eye2, phi_z, eye3).reshape(2 * ROLES * PAIRS, SH, 24)
    short = np.pad(short, ((0, 0), (0, 0), (0, TILE - 24))).reshape(-1, SH * TILE)
    inverse = np.einsum("hg,rsbz,cd->bhzcsgrd", eye2, phi_z, eye16).reshape(ROLES * 256, SH * TILE)
    expand = np.einsum("ij,hg,rs,c->ihrjgsc", eye3, eye2, eye4, ones).reshape(24, 3 * TILE)
    expand = np.pad(expand, ((0, TILE - 24), (0, 0)))
    sort = np.einsum("ij,hg,rs,cd->ihrcsjgd", eye3, eye2, eye4, eye16).reshape(3 * TILE, ROLES, 96)
    sort = np.pad(sort, ((0, 0), (0, 0), (0, TILE - 96))).reshape(3 * TILE, ROLES * TILE)
    return [pair(plane), pair(plane.T), pair(np.concatenate([spread, short], axis=1)), pair(inverse), jnp.asarray(expand, jnp.bfloat16), jnp.asarray(sort, jnp.bfloat16)]


def place(team, slab):
    return team // 2 * 32 + slab % 32 // 2 * 2 + team % 2


ROWS = 96


def step_kernel(
    anchors, vel, spectral_in, lift_in, mix_in, proj_in, plane_in, across_in, spread_in, inverse_in, expand_in, sort_in,
    second_out, raw_out, tile_out,
    ext, mid, after_two, spectral, lift, mix, proj, plane, across, spread, inverse, expand, sort,
    w_send, w_in, w_all, cut_out, cut_in, a_rows, t_rows, band, bands, a_send, a_got, a_wide, y_send, y_got,
    seen_wide, proj_wide, act, slope, g_high, g_low, out_sum, twice, g_send, g_got, m_send, m_got, r_send, r_got, raw,
    s_crew, s_yx,
    local_sem, z_sem, x_sem, c_sem, cross_sem, swap_sem, wy_sem, band_sem, y_sem, g_sem, a_sem, m_sem, back_sem,
    sc_sem, sy_sem,
):
    role, slab = lax.axis_index("role"), lax.axis_index("slab")
    yx = slab % 32 // 2
    team = slab // 32 * 2 + slab % 2
    patch = role // 2 * 32 + yx * 2 + role % 2
    after, before = (slab + 1) % SLABS, (slab + SLABS - 1) % SLABS
    teams = {1: team + 1 - 2 * (team % 2), 2: (team + 2) % ROLES, 3: ROLES - 1 - team}
    crew = [(d, (role * ROLES + team + d) % CREW) for d in range(1, CREW)]
    spots = [(d, (yx + d) % YX) for d in range(1, YX)]
    home = role == team
    pending = []

    def remote(src, dst, send_sem, recv_sem, to_role, to_slab):
        return pltpu.make_async_remote_copy(
            src_ref=src, dst_ref=dst, send_sem=send_sem, recv_sem=recv_sem,
            device_id=(to_role, to_slab), device_id_type=MESH,
        )

    def to_spot(at):
        return slab // 32 * 32 + at * 2 + slab % 2

    def send(src, dst, sems, d, to_role, to_slab):
        copy = remote(src, dst, sems.at[0, d], sems.at[1, d], to_role, to_slab)
        copy.start()
        pending.append(copy)
        return copy

    def fetch(at, src, dst):
        copy = pltpu.make_async_copy(src, dst, local_sem.at[at])
        copy.start()
        return copy

    own = fetch(0, vel, ext.at[:, pl.ds(2, PLANES), pl.ds(16, 64)])
    fetched = [
        fetch(1, spectral_in, spectral), fetch(2, lift_in, lift), fetch(3, mix_in, mix), fetch(4, proj_in, proj),
        fetch(9, sort_in, sort),
    ]
    later = [
        fetch(5, plane_in, plane), fetch(10, across_in, across), fetch(6, spread_in, spread), fetch(7, inverse_in, inverse), fetch(8, expand_in, expand)
    ]

    barrier = pltpu.get_barrier_semaphore()

    def greet(to_role, to_slab):
        pl.semaphore_signal(barrier, inc=1, device_id=(to_role, to_slab), device_id_type=MESH)

    greet(role, after)
    greet(role, before)

    @pl.when(role > 0)
    def _():
        greet(role - 1, after)
        greet(role - 1, before)

    @pl.when(role < ROLES - 1)
    def _():
        greet(role + 1, after)
        greet(role + 1, before)

    for _, to in crew:
        greet(to // ROLES, place(to % ROLES, slab))
    for _, to in spots:
        greet(role, to_spot(to))

    for copy in fetched:
        copy.wait()
    row_ky = lax.broadcasted_iota(jnp.int32, (MODES, MODES * WIDTH), 0)
    lane_ky = lax.broadcasted_iota(jnp.int32, (MODES, MODES * WIDTH), 1) // WIDTH
    twin = jnp.concatenate([lift[...], lift[...]], axis=1)
    long = jnp.concatenate([twin] * (MODES // 2), axis=1)
    blocks = [jnp.where(row_ky == lane_ky, long[i : i + 1], 0.0) for i in range(3)]
    lifted = dot3(
        split(jnp.concatenate(blocks, axis=0)), split(spectral[...].reshape(MODES * WIDTH, WIDTH))
    )
    lifted = lifted.reshape(3, 2, 8, WIDTH)
    lifted = jnp.concatenate([lifted[i, h] for i in range(3) for h in range(2)], axis=1)
    lifted = dot2(split(lifted), sort[...])
    for k in range(ROLES):
        w_send[k] = lifted[:, k * TILE : (k + 1) * TILE]

    pl.semaphore_wait(barrier, 34 + 2 * ((role + 1) // 2 % 2))

    o_copies = [
        send(w_send.at[to % ROLES], w_in.at[team, role], cross_sem, d, to // ROLES, place(to % ROLES, slab))
        for d, to in crew
    ]
    w_in[team, role] = w_send[team]

    def to_below(k):
        return remote(
            vel.at[:, pl.ds(k, 1)], ext.at[:, pl.ds(10 + k, 1), pl.ds(16, 64)],
            z_sem.at[0, k], z_sem.at[1, k], role - 1, slab,
        )

    def to_above(k):
        return remote(
            vel.at[:, pl.ds(7 - k, 1)], ext.at[:, pl.ds(1 - k, 1), pl.ds(16, 64)],
            z_sem.at[0, 2 + k], z_sem.at[1, 2 + k], role + 1, slab,
        )

    def corner(up, right, at):
        plane_at, slot = (7, 1) if up else (0, 10)
        row, spot = (56, 8) if right else (0, 80)
        return remote(
            vel.at[:, pl.ds(plane_at, 1), pl.ds(row, 8)], ext.at[:, pl.ds(slot, 1), pl.ds(spot, 8)],
            c_sem.at[0, at], c_sem.at[1, at], role + 1 if up else role - 1, after if right else before,
        )

    to_after = remote(
        vel.at[:, :, pl.ds(56, 8)], ext.at[:, pl.ds(2, PLANES), pl.ds(8, 8)],
        x_sem.at[0, 0], x_sem.at[1, 0], role, after,
    )
    to_before = remote(
        vel.at[:, :, pl.ds(0, 8)], ext.at[:, pl.ds(2, PLANES), pl.ds(80, 8)],
        x_sem.at[0, 1], x_sem.at[1, 1], role, before,
    )

    @pl.when(role > 0)
    def _():
        to_below(0).start()

    @pl.when(role < ROLES - 1)
    def _():
        to_above(0).start()

    to_after.start()
    to_before.start()

    @pl.when(role > 0)
    def _():
        to_below(1).start()
        corner(False, True, 0).start()
        corner(False, False, 1).start()

    @pl.when(role < ROLES - 1)
    def _():
        to_above(1).start()
        corner(True, True, 2).start()
        corner(True, False, 3).start()

    @pl.when(role == 0)
    def _():
        ext[:, pl.ds(0, 2)] = jnp.zeros((3, 2, ROWS, TILE), jnp.float32)

    @pl.when(role == ROLES - 1)
    def _():
        ext[:, pl.ds(10, 2)] = jnp.zeros((3, 2, ROWS, TILE), jnp.float32)

    seen = dot(mix[...], lift[...], (((0,), (1,)), ((), ())))
    unit = jnp.where(
        lax.broadcasted_iota(jnp.int32, (3, 3), 0) == lax.broadcasted_iota(jnp.int32, (3, 3), 1), 1.0, 0.0
    )
    proj_t = dot(proj[...], unit, TN)
    lift_t = dot(lift[...], unit, TN)
    for i in range(3):
        seen_wide[i] = jnp.broadcast_to(seen[:, i : i + 1], (WIDTH, TILE))
        proj_wide[i] = jnp.broadcast_to(proj_t[:, i : i + 1], (WIDTH, TILE))

    lane_80 = lax.broadcasted_iota(jnp.int32, (80, TILE), 1)
    lane_64 = lax.broadcasted_iota(jnp.int32, (64, TILE), 1)
    lane_8 = lax.broadcasted_iota(jnp.int32, (8, TILE), 1)

    def advance(field, z, row, count, lane):
        centre = [field[c, z, pl.ds(row, count)] for c in range(3)]
        out = []
        for c in range(3):
            here = centre[c]
            z_next, z_prev = field[c, z + 1, pl.ds(row, count)], field[c, z - 1, pl.ds(row, count)]
            x_next, x_prev = field[c, z, pl.ds(row + 1, count)], field[c, z, pl.ds(row - 1, count)]
            y_next = jnp.where(lane == TILE - 1, 0.0, pltpu.roll(here, TILE - 1, 1))
            y_prev = jnp.where(lane == 0, 0.0, pltpu.roll(here, 1, 1))
            laplace = z_next + z_prev + x_next + x_prev + y_next + y_prev - 6.0 * here
            carried = 0.5 * (
                centre[0] * (z_next - z_prev) + centre[1] * (x_next - x_prev) + centre[2] * (y_next - y_prev)
            )
            out.append(here + time_step * (viscosity * laplace - carried))
        return out

    own.wait()
    to_after.wait_recv()
    to_before.wait_recv()

    def inner(z, carry):
        out = advance(ext, z, 8, 80, lane_80)
        for c in range(3):
            mid[c, z, pl.ds(8, 80)] = out[c]
        return carry

    lax.fori_loop(3, 9, inner, 0)

    for copy in o_copies:
        copy.wait_recv()
    lifted = [jnp.concatenate([w_in[k, r] for r in range(ROLES)], axis=1) for k in range(ROLES)]
    lifted = dot2(split(jnp.concatenate(lifted, axis=0)), sort[...], NT)
    for k in range(ROLES):
        for i in range(3):
            w_all[k, yx, i] = lifted[k * 8 : k * 8 + 8, i * TILE : (i + 1) * TILE]
    w_copies = [send(w_all.at[:, yx], w_all.at[:, yx], wy_sem, d, role, to_spot(to)) for d, to in spots]

    @pl.when(role > 0)
    def _():
        to_above(0).wait_recv()

    @pl.when(role < ROLES - 1)
    def _():
        to_below(0).wait_recv()

    for z in (2, 9):
        out = advance(ext, z, 16, 64, lane_64)
        for c in range(3):
            mid[c, z, pl.ds(16, 64)] = out[c]


    x_at, y_at = anchors[0, 0], anchors[0, 1]
    from_lane = lax.broadcasted_iota(jnp.int32, (TILE, TILE), 0)
    to_lane = lax.broadcasted_iota(jnp.int32, (TILE, TILE), 1)
    chosen = [
        jnp.where((from_lane == to_lane % PATCH + y_at) & (to_lane // PATCH == k), 1.0, 0.0).astype(jnp.bfloat16)
        for k in range(4)
    ]

    def cut(field, first_row, first_plane, at):
        total = None
        for k in range(4):
            rows = [
                field[c, z + first_plane, pl.ds(first_row + x_at + 8 * k, 8), :]
                for z in range(PLANES)
                for c in range(3)
            ]
            part = pass_(jnp.concatenate(rows, axis=0).astype(jnp.bfloat16), chosen[k], NN)
            total = part if total is None else total + part
        cut_out[at] = total.astype(jnp.bfloat16).reshape(12, 16, TILE)

    def swap(at):
        return remote(
            cut_out.at[at], cut_in.at[at], swap_sem.at[0, at], swap_sem.at[1, at], team, place(role, slab)
        )

    def swap_start(at):
        @pl.when(jnp.logical_not(home))
        def _():
            swap(at).start()

        @pl.when(home)
        def _():
            cut_in[at] = cut_out[at]

    def swap_arrival(at, rows):
        @pl.when(jnp.logical_not(home))
        def _():
            swap(at).wait_recv()

        rows[...] = cut_in[at].astype(jnp.float32).reshape(PAIRS, 8, TILE)
        return jnp.concatenate([rows[:, k] for k in range(8)], axis=1)

    cut(mid, 16, 2, 0)

    t_rows[...] = cut_out[0].astype(jnp.float32).reshape(PAIRS, 8, TILE)
    cells_here = jnp.concatenate([t_rows[:, k] for k in range(8)], axis=1).astype(jnp.bfloat16)
    for copy in later:
        copy.wait()
    band[...] = pass_(cells_here, across[0], NN) + pass_(cells_here, across[1], NN)

    def band_copy(k):
        return remote(band, bands.at[role], band_sem.at[0, k], band_sem.at[1, role], team, place(k, slab))

    def band_arrival(k):
        return remote(band, bands.at[k], band_sem.at[0, k], band_sem.at[1, k], team, place(k, slab))

    for k in range(ROLES):

        @pl.when(jnp.logical_not(home & (k == role)))
        def _():
            band_copy(k).start()

    @pl.when(home)
    def _():
        bands[role] = band[...]

    swap_start(0)

    @pl.when(role > 0)
    def _():
        to_above(1).wait_recv()
        corner(True, True, 2).wait_recv()
        corner(True, False, 3).wait_recv()
        out = advance(ext, 1, 16, 64, lane_64)
        for c in range(3):
            mid[c, 1, pl.ds(16, 64)] = out[c]

    @pl.when(role < ROLES - 1)
    def _():
        to_below(1).wait_recv()
        corner(False, True, 0).wait_recv()
        corner(False, False, 1).wait_recv()
        out = advance(ext, 10, 16, 64, lane_64)
        for c in range(3):
            mid[c, 10, pl.ds(16, 64)] = out[c]

    for z in (2, 9):
        for row in (8, 80):
            out = advance(ext, z, row, 8, lane_8)
            for c in range(3):
                mid[c, z, pl.ds(row, 8)] = out[c]

    @pl.when(role == 0)
    def _():
        mid[:, 1, pl.ds(16, 64)] = jnp.zeros((3, 64, TILE), jnp.float32)

    @pl.when(role == ROLES - 1)
    def _():
        mid[:, 10, pl.ds(16, 64)] = jnp.zeros((3, 64, TILE), jnp.float32)

    def outer(z, carry):
        out = advance(mid, z, 16, 64, lane_64)
        for c in range(3):
            after_two[c, z - 2] = out[c]
        return carry

    lax.fori_loop(2, 6, outer, 0)
    lax.fori_loop(6, 10, outer, 0)
    second_copy = fetch(0, after_two, second_out)
    cut(after_two, 0, 0, 1)
    swap_start(1)

    for k in range(ROLES):

        @pl.when(jnp.logical_not(home & (k == role)))
        def _():
            band_arrival(k).wait_recv()

    every = jnp.concatenate([bands[b] for b in range(ROLES)], axis=0)
    halves = jnp.concatenate([every[:, :TILE], every[:, TILE:]], axis=0)
    coef = dot3(split(halves), (spread[0], spread[1]), TN)
    for copy in w_copies:
        copy.wait_recv()

    def blocks_out(ref, s, part):
        part = part.reshape(2, 8, 8, TILE)
        for core in range(2):
            ref[s // 2 * 2 + core, pl.ds(s % 2 * 8, 8)] = part[core]

    mixed = []
    for s in range(SH):
        at = (3 * SH + s) * TILE
        blocks_out(a_send, s, coef[:, at : at + TILE])
        total = None
        for i in range(3):
            at = (i * SH + s) * TILE
            weights = jnp.concatenate(
                [w_all[s // 2 * 2 + core, pl.ds(s % 2 * 8, 8), i].reshape(64, TILE) for core in range(2)], axis=0
            )
            term = coef[:, at : at + TILE] * weights
            total = term if total is None else total + term
        mixed.append(total)
    mixed = split(jnp.concatenate([part.T for part in mixed], axis=0))

    def back(to):
        rows = pl.ds(pl.multiple_of(to * 256, 256), 256)
        y_send[to] = dot3((inverse[0, rows], inverse[1, rows]), mixed)

    y_copies = {}
    for d in (2, 3, 1):
        to = teams[d]
        back(to)
        y_copies[d] = send(y_send.at[to], y_got.at[team], y_sem, d, role, place(to, slab))
    back(team)
    y_got[team] = y_send[team]
    a = swap_arrival(0, a_rows)
    for k in range(PAIRS):
        out_sum[k] = jnp.zeros((8, AREA), jnp.float32)

    def forward(q):
        rows = jnp.concatenate([y_got[q, :TILE], y_got[q, TILE:]], axis=1)
        slope[q] = dot3(split(rows), (plane[0], plane[1]))
        channels = pl.ds(pl.multiple_of(q * PART, PART), PART)
        by_seen = [seen_wide[i, channels] for i in range(3)]
        by_proj = [proj_wide[j, channels] for j in range(3)]

        def gelu(z, carry):
            at = pl.ds(pl.multiple_of(z * PART, PART), PART)
            for k in range(8):
                lanes = slice(k * TILE, (k + 1) * TILE)
                x = slope[q, at, lanes]
                for i in range(3):
                    x = x + by_seen[i] * a_rows[z * 3 + i, k : k + 1]
                square = x * x
                t = jnp.tanh(x * (root + (root * 0.044715) * square))
                half = 0.5 + 0.5 * t
                value = x * half
                act[q, at, lanes] = value
                slope[q, at, lanes] = half + value * (1.0 - t) * (root + (root * 3.0 * 0.044715) * square)
                for j in range(3):
                    term = by_proj[j] * value
                    out_sum[z * 3 + j, :, lanes] += term[:8] + term[8:]
            return carry

        lax.fori_loop(0, PLANES, gelu, 0)

    forward(team)
    for d in (1, 2, 3):
        y_copies[d].wait_recv()
        if d == 2:
            a_copies = [send(a_send.at[:, to], a_got.at[yx], a_sem, d, role, to_spot(to)) for d, to in spots]
            a_got[yx] = a_send[:, yx]
        forward(teams[d])

    wanted = swap_arrival(1, t_rows)
    out = jnp.concatenate([jnp.sum(out_sum[k], axis=0, keepdims=True) for k in range(PAIRS)], axis=0)
    error = a + out - wanted
    doubled = 2.0 * error
    for k in range(8):
        twice[:, k] = doubled[:, k * TILE : (k + 1) * TILE]

    def backward(q):
        channels = pl.ds(pl.multiple_of(q * PART, PART), PART)
        by_proj = [proj_wide[j, channels] for j in range(3)]

        def chain(z, carry):
            at = pl.ds(pl.multiple_of(z * PART, PART), PART)
            for k in range(8):
                lanes = slice(k * TILE, (k + 1) * TILE)
                g = by_proj[0] * twice[z * 3, k : k + 1]
                for j in range(1, 3):
                    g = g + by_proj[j] * twice[z * 3 + j, k : k + 1]
                g = g * slope[q, at, lanes]
                slope[q, at, lanes] = g
                g_high[at, lanes], g_low[at, lanes] = split(g)
            return carry

        lax.fori_loop(0, PLANES, chain, 0)
        g_send[q] = dot3((g_high[...], g_low[...]), (across[0], across[1]))

    g_copies = []
    for d in (2, 3, 1):
        to = teams[d]
        backward(to)
        g_copies.append(send(g_send.at[to], g_got.at[team], g_sem, d, role, place(to, slab)))
    backward(team)
    g_got[team] = g_send[team]

    row_8 = lax.broadcasted_iota(jnp.int32, (8, TILE), 0)
    lane = lax.broadcasted_iota(jnp.int32, (8, TILE), 1)
    zero = jnp.zeros((8, TILE), jnp.float32)
    wide = jnp.zeros((PART, TILE), jnp.float32)

    def cells(q, carry):
        def over(z, sums):
            at = pl.ds(pl.multiple_of(z * PART, PART), PART)
            sums = list(sums)
            for k in range(8):
                lanes = slice(k * TILE, (k + 1) * TILE)
                g, value = slope[q, at, lanes], act[q, at, lanes]
                for i in range(3):
                    sums[i] = sums[i] + g * a_rows[z * 3 + i, k : k + 1]
                    sums[3 + i] = sums[3 + i] + value * twice[z * 3 + i, k : k + 1]
            return tuple(sums)

        return lax.fori_loop(0, PLANES, over, (wide,) * 6)

    by_quarter = [cells(q, 0) for q in range(ROLES)]

    def channel_rows(k, row):
        column = jnp.concatenate([sums[k] for sums in by_quarter], axis=0)
        return dot(jnp.where(row_8 == row, 1.0, 0.0), column, NT)

    cross_rows = sum(channel_rows(i, i) for i in range(3))
    proj_rows = sum(channel_rows(3 + j, j) for j in range(3))
    sse = jnp.sum(error * error, keepdims=True)

    for copy in g_copies:
        copy.wait_recv()
    stacked = jnp.concatenate([g_got[b][:, h * TILE : (h + 1) * TILE] for b in range(ROLES) for h in range(2)], axis=0)
    grad = dot3(split(stacked), (inverse[0], inverse[1]), TN)
    for s in range(SH):
        blocks_out(m_send, s, grad[:, s * TILE : (s + 1) * TILE])
    m_copies = [send(m_send.at[:, to], m_got.at[yx], m_sem, d, role, to_spot(to)) for d, to in spots]
    m_got[yx] = m_send[:, yx]
    for copy in a_copies:
        copy.wait_recv()
    a_all = split(a_got[...].reshape(SLABS * 8, TILE))
    a_all = dot2(a_all, expand[...])
    for i in range(3):
        a_wide[i] = a_all[:, i * TILE : (i + 1) * TILE].reshape(YX, ROLES, 8, TILE)
    for copy in m_copies:
        copy.wait_recv()

    crossed = []
    for b in range(ROLES):
        sums = [zero, zero, zero]
        for k in range(YX):
            g = m_got[k, b]
            sums = [sums[i] + a_wide[i, k, b] * g for i in range(3)]
        crossed.append(jnp.concatenate(sums, axis=1))
    crossed = dot2(split(jnp.concatenate(crossed, axis=0)), sort[...])
    for b in range(ROLES):
        for k in range(ROLES):
            r_send[k, b] = crossed[b * 8 : b * 8 + 8, k * TILE : (k + 1) * TILE]
    r_copies = [
        send(r_send.at[to // ROLES, to % ROLES], r_got.at[role, team], back_sem, d, to // ROLES, place(to % ROLES, slab))
        for d, to in crew
    ]
    r_got[role, team] = r_send[role, team]
    for copy in r_copies:
        copy.wait_recv()
    joined = [(r_got[0, q] + r_got[1, q]) + (r_got[2, q] + r_got[3, q]) for q in range(ROLES)]
    joined = dot2(split(jnp.concatenate(joined, axis=1)), sort[...], NT)
    squares = jnp.zeros((WIDTH, TILE), jnp.float32)
    lift_sum = [jnp.zeros((WIDTH, WIDTH), jnp.float32)] * 3
    for k in range(8):
        rows = [joined[k : k + 1, i * TILE : (i + 1) * TILE] for i in range(3)]
        value = lift_t[:, 0:1] * rows[0] + lift_t[:, 1:2] * rows[1] + lift_t[:, 2:3] * rows[2]
        raw[k] = value
        squares = squares + value * value
        for i in range(3):
            lift_sum[i] = lift_sum[i] + (
                spectral[k] * rows[i][:, :WIDTH] + spectral[8 + k] * rows[i][:, WIDTH:]
            )
    raw_copy = fetch(1, raw, raw_out)
    left = cross_rows
    for i in range(3):
        left = left + dot(jnp.where(row_8[:, :WIDTH] == 3 + i, 1.0, 0.0), lift_sum[i], NT)
    tile = jnp.concatenate([left, proj_rows], axis=1)
    tile = tile + jnp.where((row_8 == 6) & (lane == patch), sse, 0.0)
    tile = tile + jnp.where(row_8 == 7, jnp.sum(squares, keepdims=True), 0.0)

    s_crew[role, team] = tile
    copies = [
        send(s_crew.at[role, team], s_crew.at[role, team], sc_sem, d, to // ROLES, place(to % ROLES, slab))
        for d, to in crew
    ]
    for copy in copies:
        copy.wait_recv()
    s_yx[yx] = jnp.sum(s_crew[...], axis=(0, 1))
    copies = [send(s_yx.at[yx], s_yx.at[yx], sy_sem, d, role, to_spot(to)) for d, to in spots]
    for copy in copies:
        copy.wait_recv()
    tile_out[...] = jnp.sum(s_yx[...], axis=0)

    for copy in pending:
        copy.wait_send()
    second_copy.wait()
    raw_copy.wait()
    to_after.wait_send()
    to_before.wait_send()

    @pl.when(role > 0)
    def _():
        to_below(0).wait_send()
        to_below(1).wait_send()
        corner(False, True, 0).wait_send()
        corner(False, False, 1).wait_send()

    @pl.when(role < ROLES - 1)
    def _():
        to_above(0).wait_send()
        to_above(1).wait_send()
        corner(True, True, 2).wait_send()
        corner(True, False, 3).wait_send()

    for k in range(ROLES):

        @pl.when(jnp.logical_not(home & (k == role)))
        def _():
            band_copy(k).wait_send()

    @pl.when(jnp.logical_not(home))
    def _():
        swap(0).wait_send()
        swap(1).wait_send()


def result(*shape):
    return jax.ShapeDtypeStruct(shape, jnp.float32)


def step(anchors, velocity, spectral, lift, mix, proj):
    vmem = pl.BlockSpec(memory_space=pltpu.VMEM)
    anywhere = pl.BlockSpec(memory_space=pltpu.HBM)
    dma = pltpu.SemaphoreType.DMA

    def room(*shape):
        return pltpu.VMEM(shape, jnp.float32)

    def narrow(*shape):
        return pltpu.VMEM(shape, jnp.bfloat16)

    return pl.pallas_call(
        step_kernel,
        out_shape=(result(3, PLANES, 64, TILE), result(8, WIDTH, TILE), result(8, TILE)),
        in_specs=[pl.BlockSpec(memory_space=pltpu.SMEM)] + [anywhere] * 11,
        out_specs=(anywhere, anywhere, vmem),
        scratch_shapes=[
            room(3, 12, ROWS, TILE),
            room(3, 12, ROWS, TILE),
            room(3, PLANES, 64, TILE),
            room(MODES, WIDTH, WIDTH),
            room(3, WIDTH),
            room(WIDTH, WIDTH),
            room(3, WIDTH),
            narrow(2, 256, AREA),
            narrow(2, AREA, 256),
            narrow(2, 2 * ROLES * PAIRS, 4 * SH * TILE),
            narrow(2, ROLES * 256, SH * TILE),
            narrow(TILE, 3 * TILE),
            narrow(3 * TILE, ROLES * TILE),
            room(ROLES, 8, TILE),
            room(ROLES, ROLES, 8, TILE),
            room(ROLES, YX, 3, 8, TILE),
            narrow(2, 12, 16, TILE),
            narrow(2, 12, 16, TILE),
            room(PAIRS, 8, TILE),
            room(PAIRS, 8, TILE),
            room(PAIRS, 256),
            room(ROLES, PAIRS, 256),
            room(ROLES, YX, 8, TILE),
            room(YX, ROLES, 8, TILE),
            room(3, YX, ROLES, 8, TILE),
            room(ROLES, 256, TILE),
            room(ROLES, 256, TILE),
            room(3, WIDTH, TILE),
            room(3, WIDTH, TILE),
            room(ROLES, TILE, AREA),
            room(ROLES, TILE, AREA),
            narrow(TILE, AREA),
            narrow(TILE, AREA),
            room(PAIRS, 8, AREA),
            room(PAIRS, 8, TILE),
            room(ROLES, TILE, 256),
            room(ROLES, TILE, 256),
            room(ROLES, YX, 8, TILE),
            room(YX, ROLES, 8, TILE),
            room(ROLES, ROLES, 8, TILE),
            room(ROLES, ROLES, 8, TILE),
            room(8, WIDTH, TILE),
            room(ROLES, ROLES, 8, TILE),
            room(YX, 8, TILE),
            dma((11,)),
            dma((2, 4)),
            dma((2, 2)),
            dma((2, 4)),
            dma((2, CREW)),
            dma((2, 2)),
            dma((2, YX)),
            dma((2, ROLES)),
            dma((2, ROLES)),
            dma((2, ROLES)),
            dma((2, YX)),
            dma((2, YX)),
            dma((2, CREW)),
            dma((2, CREW)),
            dma((2, YX)),
        ],
        compiler_params=pltpu.CompilerParams(
            collective_id=0, has_side_effects=True, vmem_limit_bytes=63 * 2**20
        ),
    )(anchors, velocity, spectral, lift, mix, proj, *tables())


def finish_kernel(
    second, raw, tile, lift, mix, table, second_out, loss_out, lift_out, mix_out, proj_out, spec_out, held, copy_sem
):
    fetches = [pltpu.make_async_copy(second.at[c], held.at[c], copy_sem.at[0, c]) for c in range(3)]
    stores = [pltpu.make_async_copy(held.at[c], second_out.at[c], copy_sem.at[1, c]) for c in range(3)]
    for copy in fetches:
        copy.start()

    for get, put in zip(fetches, stores):
        get.wait()
        put.start()

    def normal(total):
        mean = jnp.sum(total * total, keepdims=True) / total.size
        return total / jnp.sqrt(mean + tiny_eps)

    cross = tile[0:3, :WIDTH]
    proj_out[...] = normal(tile[0:3, WIDTH:])
    lift_out[...] = normal(tile[3:6, :WIDTH] + dot(cross, mix[...], NT))
    mix_out[...] = normal(dot(lift[...], cross, TN))
    scale = 1.0 / jnp.sqrt(tile[7:8, 0:1] / (MODES**3 * WIDTH * WIDTH) + tiny_eps)
    for k in range(8):
        value = raw[k] * scale
        spec_out[k] = value[:, :WIDTH]
        spec_out[8 + k] = value[:, WIDTH:]
    losses = tile[6:7, :] / (3.0 * PATCH**3)
    lanes = lax.broadcasted_iota(jnp.int32, (1, TILE), 1)
    found = [jnp.sum(jnp.where(lanes == table[0:1, k : k + 1], losses, 0.0), axis=1, keepdims=True) for k in range(2)]
    loss_out[...] = jnp.concatenate(found, axis=1)
    for copy in stores:
        copy.wait()


def finish(second, raw, tile, lift, mix, table):
    vmem = pl.BlockSpec(memory_space=pltpu.VMEM)
    anywhere = pl.BlockSpec(memory_space=pltpu.HBM)
    return pl.pallas_call(
        finish_kernel,
        out_shape=(
            result(3, PLANES, 64, TILE),
            result(1, 2),
            result(3, WIDTH),
            result(WIDTH, WIDTH),
            result(3, WIDTH),
            result(MODES, WIDTH, WIDTH),
        ),
        in_specs=[anywhere] + [vmem] * 5,
        out_specs=(anywhere,) + (vmem,) * 5,
        scratch_shapes=[pltpu.VMEM((3, PLANES, 64, TILE), jnp.float32), pltpu.SemaphoreType.DMA((2, 3))],
    )(second, raw, tile, lift, mix, table)


def on_device(velocity, anchors, slot_table, lift, mix, proj, spectral):
    second, raw, tile = step(anchors, velocity, spectral, lift, mix, proj)
    return finish(second, raw, tile, lift, mix, slot_table)


def solution(mesh):
    return jax.shard_map(
        on_device,
        mesh=mesh,
        in_specs=(
            P(None, "role", "slab", None),
            P("slab", None),
            P("slab", None),
            P(),
            P(),
            P(),
            P(("role", "slab"), None, None),
        ),
        out_specs=(
            P(None, "role", "slab", None),
            P("slab", None),
            P(),
            P(),
            P(),
            P(("role", "slab"), None, None),
        ),
        check_vma=False,
    )
```

```python
import math

import jax
import jax.numpy as jnp
import numpy as np
from jax import lax
from jax.experimental import pallas as pl
from jax.experimental.pallas import tpu as pltpu
from jax.sharding import PartitionSpec as P

MODES = 16
PATCH = 32
AREA = PATCH * PATCH
ROLES = 4
SLABS = 64
YX = 16
CREW = 16
PLANES = 8
WIDTH = 64
PART = WIDTH // ROLES
SH = 4
TILE = 128
PAIRS = 3 * PLANES

time_step = 0.1
viscosity = 1.5
tiny_eps = 1e-06
exact = lax.Precision.HIGHEST
MESH = pl.DeviceIdType.MESH
root = math.sqrt(2.0 / math.pi)
NN = (((1,), (0,)), ((), ()))
NT = (((1,), (1,)), ((), ()))
TN = (((0,), (0,)), ((), ()))


def dot(a, b, dims=NN):
    return lax.dot_general(a, b, dims, precision=exact, preferred_element_type=jnp.float32)


def split(value):
    high = value.astype(jnp.bfloat16)
    return high, (value - high.astype(jnp.float32)).astype(jnp.bfloat16)


def pass_(a, b, dims):
    return lax.dot_general(a, b, dims, preferred_element_type=jnp.float32)


def dot3(a, b, dims=NN):
    return pass_(a[0], b[0], dims) + (pass_(a[0], b[1], dims) + pass_(a[1], b[0], dims))


def dot2(a, exact_b, dims=NN):
    return pass_(a[0], exact_b, dims) + pass_(a[1], exact_b, dims)


def fourier_table():
    order = np.arange(MODES)[:, None]
    points = np.arange(PATCH)[None, :]
    angles = 2.0 * math.pi * ((order + 1) // 2) * points / PATCH
    waves = np.where((order % 2 == 1) | (order == 0), np.cos(angles), np.sin(angles))
    return waves * np.where(order == 0, math.sqrt(1.0 / PATCH), math.sqrt(2.0 / PATCH))


def pair(table):
    table = table.astype(np.float32)
    high = table.astype(jnp.bfloat16)
    return jnp.asarray(np.stack([high, (table - high.astype(np.float32)).astype(jnp.bfloat16)]))


def tables():
    phi = fourier_table()
    over_x = phi.reshape(2, 4, 2, 4, 8)
    over_y = phi.reshape(2, 8, PATCH)
    plane = np.einsum("axchl,gky->gcaxklhy", over_x, over_y).reshape(256, AREA)
    phi_z = phi.reshape(ROLES, SH, ROLES, PLANES)
    eye2, eye3, eye4, eye16 = np.eye(2), np.eye(3), np.eye(ROLES), np.eye(PART)
    ones = np.ones(PART)
    spread = np.einsum("hg,rsbz,ij,c->hbzijsgrc", eye2, phi_z, eye3, ones).reshape(2 * ROLES * PAIRS, 3 * SH * TILE)
    short = np.einsum("hg,rsbz,ij->hbzisjgr", eye2, phi_z, eye3).reshape(2 * ROLES * PAIRS, SH, 24)
    short = np.pad(short, ((0, 0), (0, 0), (0, TILE - 24))).reshape(-1, SH * TILE)
    inverse = np.einsum("hg,rsbz,cd->bhzcsgrd", eye2, phi_z, eye16).reshape(ROLES * 256, SH * TILE)
    expand = np.einsum("ij,hg,rs,c->ihrjgsc", eye3, eye2, eye4, ones).reshape(24, 3 * TILE)
    expand = np.pad(expand, ((0, TILE - 24), (0, 0)))
    sort = np.einsum("ij,hg,rs,cd->ihrcsjgd", eye3, eye2, eye4, eye16).reshape(3 * TILE, ROLES, 96)
    sort = np.pad(sort, ((0, 0), (0, 0), (0, TILE - 96))).reshape(3 * TILE, ROLES * TILE)
    return [pair(plane), pair(plane.T), pair(np.concatenate([spread, short], axis=1)), pair(inverse), jnp.asarray(expand, jnp.bfloat16), jnp.asarray(sort, jnp.bfloat16)]


def place(team, slab):
    return team // 2 * 32 + slab % 32 // 2 * 2 + team % 2


ROWS = 96


def step_kernel(
    anchors, vel, spectral_in, lift_in, mix_in, proj_in, plane_in, across_in, spread_in, inverse_in, expand_in, sort_in,
    second_out, raw_out, tile_out,
    ext, mid, after_two, spectral, lift, mix, proj, plane, across, spread, inverse, expand, sort,
    w_send, w_in, w_all, cut_out, cut_in, a_rows, t_rows, band, bands, a_send, a_got, a_wide, y_send, y_got,
    seen_wide, proj_wide, act, slope, g_high, g_low, out_sum, twice, g_send, g_got, m_send, m_got, r_send, r_got, raw,
    s_crew, s_yx,
    local_sem, z_sem, x_sem, c_sem, cross_sem, swap_sem, wy_sem, band_sem, y_sem, g_sem, a_sem, m_sem, back_sem,
    sc_sem, sy_sem,
):
    role, slab = lax.axis_index("role"), lax.axis_index("slab")
    yx = slab % 32 // 2
    team = slab // 32 * 2 + slab % 2
    patch = role // 2 * 32 + yx * 2 + role % 2
    after, before = (slab + 1) % SLABS, (slab + SLABS - 1) % SLABS
    teams = [(d, (team + d) % ROLES) for d in range(1, ROLES)]
    crew = [(d, (role * ROLES + team + d) % CREW) for d in range(1, CREW)]
    spots = [(d, (yx + d) % YX) for d in range(1, YX)]
    home = role == team
    pending = []

    def remote(src, dst, send_sem, recv_sem, to_role, to_slab):
        return pltpu.make_async_remote_copy(
            src_ref=src, dst_ref=dst, send_sem=send_sem, recv_sem=recv_sem,
            device_id=(to_role, to_slab), device_id_type=MESH,
        )

    def to_spot(at):
        return slab // 32 * 32 + at * 2 + slab % 2

    def send(src, dst, sems, d, to_role, to_slab):
        copy = remote(src, dst, sems.at[0, d], sems.at[1, d], to_role, to_slab)
        copy.start()
        pending.append(copy)
        return copy

    def fetch(at, src, dst):
        copy = pltpu.make_async_copy(src, dst, local_sem.at[at])
        copy.start()
        return copy

    own = fetch(0, vel, ext.at[:, pl.ds(2, PLANES), pl.ds(16, 64)])
    fetched = [
        fetch(1, spectral_in, spectral), fetch(2, lift_in, lift), fetch(3, mix_in, mix), fetch(4, proj_in, proj),
        fetch(9, sort_in, sort),
    ]
    later = [
        fetch(5, plane_in, plane), fetch(10, across_in, across), fetch(6, spread_in, spread), fetch(7, inverse_in, inverse), fetch(8, expand_in, expand)
    ]

    barrier = pltpu.get_barrier_semaphore()

    def greet(to_role, to_slab):
        pl.semaphore_signal(barrier, inc=1, device_id=(to_role, to_slab), device_id_type=MESH)

    greet(role, after)
    greet(role, before)

    @pl.when(role > 0)
    def _():
        greet(role - 1, after)
        greet(role - 1, before)

    @pl.when(role < ROLES - 1)
    def _():
        greet(role + 1, after)
        greet(role + 1, before)

    for _, to in crew:
        greet(to // ROLES, place(to % ROLES, slab))
    for _, to in spots:
        greet(role, to_spot(to))

    for copy in fetched:
        copy.wait()
    row_ky = lax.broadcasted_iota(jnp.int32, (MODES, MODES * WIDTH), 0)
    lane_ky = lax.broadcasted_iota(jnp.int32, (MODES, MODES * WIDTH), 1) // WIDTH
    twin = jnp.concatenate([lift[...], lift[...]], axis=1)
    long = jnp.concatenate([twin] * (MODES // 2), axis=1)
    blocks = [jnp.where(row_ky == lane_ky, long[i : i + 1], 0.0) for i in range(3)]
    lifted = dot3(
        split(jnp.concatenate(blocks, axis=0)), split(spectral[...].reshape(MODES * WIDTH, WIDTH))
    )
    lifted = lifted.reshape(3, 2, 8, WIDTH)
    lifted = jnp.concatenate([lifted[i, h] for i in range(3) for h in range(2)], axis=1)
    lifted = dot2(split(lifted), sort[...])
    for k in range(ROLES):
        w_send[k] = lifted[:, k * TILE : (k + 1) * TILE]

    pl.semaphore_wait(barrier, 34 + 2 * ((role + 1) // 2 % 2))

    o_copies = [
        send(w_send.at[to % ROLES], w_in.at[team, role], cross_sem, d, to // ROLES, place(to % ROLES, slab))
        for d, to in crew
    ]
    w_in[team, role] = w_send[team]

    def to_below(k):
        return remote(
            vel.at[:, pl.ds(k, 1)], ext.at[:, pl.ds(10 + k, 1), pl.ds(16, 64)],
            z_sem.at[0, k], z_sem.at[1, k], role - 1, slab,
        )

    def to_above(k):
        return remote(
            vel.at[:, pl.ds(7 - k, 1)], ext.at[:, pl.ds(1 - k, 1), pl.ds(16, 64)],
            z_sem.at[0, 2 + k], z_sem.at[1, 2 + k], role + 1, slab,
        )

    def corner(up, right, at):
        plane_at, slot = (7, 1) if up else (0, 10)
        row, spot = (56, 8) if right else (0, 80)
        return remote(
            vel.at[:, pl.ds(plane_at, 1), pl.ds(row, 8)], ext.at[:, pl.ds(slot, 1), pl.ds(spot, 8)],
            c_sem.at[0, at], c_sem.at[1, at], role + 1 if up else role - 1, after if right else before,
        )

    to_after = remote(
        vel.at[:, :, pl.ds(56, 8)], ext.at[:, pl.ds(2, PLANES), pl.ds(8, 8)],
        x_sem.at[0, 0], x_sem.at[1, 0], role, after,
    )
    to_before = remote(
        vel.at[:, :, pl.ds(0, 8)], ext.at[:, pl.ds(2, PLANES), pl.ds(80, 8)],
        x_sem.at[0, 1], x_sem.at[1, 1], role, before,
    )

    @pl.when(role > 0)
    def _():
        to_below(0).start()

    @pl.when(role < ROLES - 1)
    def _():
        to_above(0).start()

    to_after.start()
    to_before.start()

    @pl.when(role > 0)
    def _():
        to_below(1).start()
        corner(False, True, 0).start()
        corner(False, False, 1).start()

    @pl.when(role < ROLES - 1)
    def _():
        to_above(1).start()
        corner(True, True, 2).start()
        corner(True, False, 3).start()

    @pl.when(role == 0)
    def _():
        ext[:, pl.ds(0, 2)] = jnp.zeros((3, 2, ROWS, TILE), jnp.float32)

    @pl.when(role == ROLES - 1)
    def _():
        ext[:, pl.ds(10, 2)] = jnp.zeros((3, 2, ROWS, TILE), jnp.float32)

    seen = dot(mix[...], lift[...], (((0,), (1,)), ((), ())))
    unit = jnp.where(
        lax.broadcasted_iota(jnp.int32, (3, 3), 0) == lax.broadcasted_iota(jnp.int32, (3, 3), 1), 1.0, 0.0
    )
    proj_t = dot(proj[...], unit, TN)
    lift_t = dot(lift[...], unit, TN)
    for i in range(3):
        seen_wide[i] = jnp.broadcast_to(seen[:, i : i + 1], (WIDTH, TILE))
        proj_wide[i] = jnp.broadcast_to(proj_t[:, i : i + 1], (WIDTH, TILE))

    lane_80 = lax.broadcasted_iota(jnp.int32, (80, TILE), 1)
    lane_64 = lax.broadcasted_iota(jnp.int32, (64, TILE), 1)
    lane_8 = lax.broadcasted_iota(jnp.int32, (8, TILE), 1)

    def advance(field, z, row, count, lane):
        centre = [field[c, z, pl.ds(row, count)] for c in range(3)]
        out = []
        for c in range(3):
            here = centre[c]
            z_next, z_prev = field[c, z + 1, pl.ds(row, count)], field[c, z - 1, pl.ds(row, count)]
            x_next, x_prev = field[c, z, pl.ds(row + 1, count)], field[c, z, pl.ds(row - 1, count)]
            y_next = jnp.where(lane == TILE - 1, 0.0, pltpu.roll(here, TILE - 1, 1))
            y_prev = jnp.where(lane == 0, 0.0, pltpu.roll(here, 1, 1))
            laplace = z_next + z_prev + x_next + x_prev + y_next + y_prev - 6.0 * here
            carried = 0.5 * (
                centre[0] * (z_next - z_prev) + centre[1] * (x_next - x_prev) + centre[2] * (y_next - y_prev)
            )
            out.append(here + time_step * (viscosity * laplace - carried))
        return out

    own.wait()
    to_after.wait_recv()
    to_before.wait_recv()

    def inner(z, carry):
        out = advance(ext, z, 8, 80, lane_80)
        for c in range(3):
            mid[c, z, pl.ds(8, 80)] = out[c]
        return carry

    lax.fori_loop(3, 9, inner, 0)

    for copy in o_copies:
        copy.wait_recv()
    lifted = [jnp.concatenate([w_in[k, r] for r in range(ROLES)], axis=1) for k in range(ROLES)]
    lifted = dot2(split(jnp.concatenate(lifted, axis=0)), sort[...], NT)
    for k in range(ROLES):
        for i in range(3):
            w_all[k, yx, i] = lifted[k * 8 : k * 8 + 8, i * TILE : (i + 1) * TILE]
    w_copies = [send(w_all.at[:, yx], w_all.at[:, yx], wy_sem, d, role, to_spot(to)) for d, to in spots]

    @pl.when(role > 0)
    def _():
        to_above(0).wait_recv()

    @pl.when(role < ROLES - 1)
    def _():
        to_below(0).wait_recv()

    for z in (2, 9):
        out = advance(ext, z, 16, 64, lane_64)
        for c in range(3):
            mid[c, z, pl.ds(16, 64)] = out[c]


    x_at, y_at = anchors[0, 0], anchors[0, 1]
    from_lane = lax.broadcasted_iota(jnp.int32, (TILE, TILE), 0)
    to_lane = lax.broadcasted_iota(jnp.int32, (TILE, TILE), 1)
    chosen = [
        jnp.where((from_lane == to_lane % PATCH + y_at) & (to_lane // PATCH == k), 1.0, 0.0).astype(jnp.bfloat16)
        for k in range(4)
    ]

    def cut(field, first_row, first_plane, at):
        total = None
        for k in range(4):
            rows = [
                field[c, z + first_plane, pl.ds(first_row + x_at + 8 * k, 8), :]
                for z in range(PLANES)
                for c in range(3)
            ]
            part = pass_(jnp.concatenate(rows, axis=0).astype(jnp.bfloat16), chosen[k], NN)
            total = part if total is None else total + part
        cut_out[at] = total.astype(jnp.bfloat16).reshape(12, 16, TILE)

    def swap(at):
        return remote(
            cut_out.at[at], cut_in.at[at], swap_sem.at[0, at], swap_sem.at[1, at], team, place(role, slab)
        )

    def swap_start(at):
        @pl.when(jnp.logical_not(home))
        def _():
            swap(at).start()

        @pl.when(home)
        def _():
            cut_in[at] = cut_out[at]

    def swap_arrival(at, rows):
        @pl.when(jnp.logical_not(home))
        def _():
            swap(at).wait_recv()

        rows[...] = cut_in[at].astype(jnp.float32).reshape(PAIRS, 8, TILE)
        return jnp.concatenate([rows[:, k] for k in range(8)], axis=1)

    cut(mid, 16, 2, 0)

    t_rows[...] = cut_out[0].astype(jnp.float32).reshape(PAIRS, 8, TILE)
    cells_here = jnp.concatenate([t_rows[:, k] for k in range(8)], axis=1).astype(jnp.bfloat16)
    for copy in later:
        copy.wait()
    band[...] = pass_(cells_here, across[0], NN) + pass_(cells_here, across[1], NN)

    def band_copy(k):
        return remote(band, bands.at[role], band_sem.at[0, k], band_sem.at[1, role], team, place(k, slab))

    def band_arrival(k):
        return remote(band, bands.at[k], band_sem.at[0, k], band_sem.at[1, k], team, place(k, slab))

    for k in range(ROLES):

        @pl.when(jnp.logical_not(home & (k == role)))
        def _():
            band_copy(k).start()

    @pl.when(home)
    def _():
        bands[role] = band[...]

    swap_start(0)

    @pl.when(role > 0)
    def _():
        to_above(1).wait_recv()
        corner(True, True, 2).wait_recv()
        corner(True, False, 3).wait_recv()
        out = advance(ext, 1, 16, 64, lane_64)
        for c in range(3):
            mid[c, 1, pl.ds(16, 64)] = out[c]

    @pl.when(role < ROLES - 1)
    def _():
        to_below(1).wait_recv()
        corner(False, True, 0).wait_recv()
        corner(False, False, 1).wait_recv()
        out = advance(ext, 10, 16, 64, lane_64)
        for c in range(3):
            mid[c, 10, pl.ds(16, 64)] = out[c]

    for z in (2, 9):
        for row in (8, 80):
            out = advance(ext, z, row, 8, lane_8)
            for c in range(3):
                mid[c, z, pl.ds(row, 8)] = out[c]

    @pl.when(role == 0)
    def _():
        mid[:, 1, pl.ds(16, 64)] = jnp.zeros((3, 64, TILE), jnp.float32)

    @pl.when(role == ROLES - 1)
    def _():
        mid[:, 10, pl.ds(16, 64)] = jnp.zeros((3, 64, TILE), jnp.float32)

    def outer(z, carry):
        out = advance(mid, z, 16, 64, lane_64)
        for c in range(3):
            after_two[c, z - 2] = out[c]
        return carry

    lax.fori_loop(2, 6, outer, 0)
    lax.fori_loop(6, 10, outer, 0)
    second_copy = fetch(0, after_two, second_out)
    cut(after_two, 0, 0, 1)
    swap_start(1)

    for k in range(ROLES):

        @pl.when(jnp.logical_not(home & (k == role)))
        def _():
            band_arrival(k).wait_recv()

    every = jnp.concatenate([bands[b] for b in range(ROLES)], axis=0)
    halves = jnp.concatenate([every[:, :TILE], every[:, TILE:]], axis=0)
    coef = dot3(split(halves), (spread[0], spread[1]), TN)
    for copy in w_copies:
        copy.wait_recv()

    def blocks_out(ref, s, part):
        part = part.reshape(2, 8, 8, TILE)
        for core in range(2):
            ref[s // 2 * 2 + core, pl.ds(s % 2 * 8, 8)] = part[core]

    mixed = []
    for s in range(SH):
        at = (3 * SH + s) * TILE
        blocks_out(a_send, s, coef[:, at : at + TILE])
        total = None
        for i in range(3):
            at = (i * SH + s) * TILE
            weights = jnp.concatenate(
                [w_all[s // 2 * 2 + core, pl.ds(s % 2 * 8, 8), i].reshape(64, TILE) for core in range(2)], axis=0
            )
            term = coef[:, at : at + TILE] * weights
            total = term if total is None else total + term
        mixed.append(total)
    mixed = split(jnp.concatenate([part.T for part in mixed], axis=0))

    def back(to):
        rows = pl.ds(pl.multiple_of(to * 256, 256), 256)
        y_send[to] = dot3((inverse[0, rows], inverse[1, rows]), mixed)

    y_copies = []
    for d, to in (teams[1], teams[0], teams[2]):
        back(to)
        y_copies.append((d, send(y_send.at[to], y_got.at[team], y_sem, d, role, place(to, slab))))
    back(team)
    y_got[team] = y_send[team]
    a = swap_arrival(0, a_rows)
    for k in range(PAIRS):
        out_sum[k] = jnp.zeros((8, AREA), jnp.float32)

    def forward(q):
        rows = jnp.concatenate([y_got[q, :TILE], y_got[q, TILE:]], axis=1)
        slope[q] = dot3(split(rows), (plane[0], plane[1]))
        channels = pl.ds(pl.multiple_of(q * PART, PART), PART)
        by_seen = [seen_wide[i, channels] for i in range(3)]
        by_proj = [proj_wide[j, channels] for j in range(3)]

        def gelu(z, carry):
            at = pl.ds(pl.multiple_of(z * PART, PART), PART)
            for k in range(8):
                lanes = slice(k * TILE, (k + 1) * TILE)
                x = slope[q, at, lanes]
                for i in range(3):
                    x = x + by_seen[i] * a_rows[z * 3 + i, k : k + 1]
                square = x * x
                t = jnp.tanh(x * (root + (root * 0.044715) * square))
                half = 0.5 + 0.5 * t
                value = x * half
                act[q, at, lanes] = value
                slope[q, at, lanes] = half + value * (1.0 - t) * (root + (root * 3.0 * 0.044715) * square)
                for j in range(3):
                    term = by_proj[j] * value
                    out_sum[z * 3 + j, :, lanes] += term[:8] + term[8:]
            return carry

        lax.fori_loop(0, PLANES, gelu, 0)

    forward(team)
    a_copies = [send(a_send.at[:, to], a_got.at[yx], a_sem, d, role, to_spot(to)) for d, to in spots]
    a_got[yx] = a_send[:, yx]
    for d, copy in y_copies:
        copy.wait_recv()
        forward((team + ROLES - d) % ROLES)

    wanted = swap_arrival(1, t_rows)
    out = jnp.concatenate([jnp.sum(out_sum[k], axis=0, keepdims=True) for k in range(PAIRS)], axis=0)
    error = a + out - wanted
    doubled = 2.0 * error
    for k in range(8):
        twice[:, k] = doubled[:, k * TILE : (k + 1) * TILE]

    def backward(q):
        channels = pl.ds(pl.multiple_of(q * PART, PART), PART)
        by_proj = [proj_wide[j, channels] for j in range(3)]

        def chain(z, carry):
            at = pl.ds(pl.multiple_of(z * PART, PART), PART)
            for k in range(8):
                lanes = slice(k * TILE, (k + 1) * TILE)
                g = by_proj[0] * twice[z * 3, k : k + 1]
                for j in range(1, 3):
                    g = g + by_proj[j] * twice[z * 3 + j, k : k + 1]
                g = g * slope[q, at, lanes]
                slope[q, at, lanes] = g
                g_high[at, lanes], g_low[at, lanes] = split(g)
            return carry

        lax.fori_loop(0, PLANES, chain, 0)
        g_send[q] = dot3((g_high[...], g_low[...]), (across[0], across[1]))

    g_copies = []
    for d, to in (teams[1], teams[0], teams[2]):
        backward(to)
        g_copies.append(send(g_send.at[to], g_got.at[team], g_sem, d, role, place(to, slab)))
    backward(team)
    g_got[team] = g_send[team]

    row_8 = lax.broadcasted_iota(jnp.int32, (8, TILE), 0)
    lane = lax.broadcasted_iota(jnp.int32, (8, TILE), 1)
    zero = jnp.zeros((8, TILE), jnp.float32)
    wide = jnp.zeros((PART, TILE), jnp.float32)

    def cells(q, carry):
        def over(z, sums):
            at = pl.ds(pl.multiple_of(z * PART, PART), PART)
            sums = list(sums)
            for k in range(8):
                lanes = slice(k * TILE, (k + 1) * TILE)
                g, value = slope[q, at, lanes], act[q, at, lanes]
                for i in range(3):
                    sums[i] = sums[i] + g * a_rows[z * 3 + i, k : k + 1]
                    sums[3 + i] = sums[3 + i] + value * twice[z * 3 + i, k : k + 1]
            return tuple(sums)

        return lax.fori_loop(0, PLANES, over, (wide,) * 6)

    by_quarter = [cells(q, 0) for q in range(ROLES)]

    def channel_rows(k, row):
        column = jnp.concatenate([sums[k] for sums in by_quarter], axis=0)
        return dot(jnp.where(row_8 == row, 1.0, 0.0), column, NT)

    cross_rows = sum(channel_rows(i, i) for i in range(3))
    proj_rows = sum(channel_rows(3 + j, j) for j in range(3))
    sse = jnp.sum(error * error, keepdims=True)

    for copy in g_copies:
        copy.wait_recv()
    stacked = jnp.concatenate([g_got[b][:, h * TILE : (h + 1) * TILE] for b in range(ROLES) for h in range(2)], axis=0)
    grad = dot3(split(stacked), (inverse[0], inverse[1]), TN)
    for s in range(SH):
        blocks_out(m_send, s, grad[:, s * TILE : (s + 1) * TILE])
    m_copies = [send(m_send.at[:, to], m_got.at[yx], m_sem, d, role, to_spot(to)) for d, to in spots]
    m_got[yx] = m_send[:, yx]
    for copy in a_copies:
        copy.wait_recv()
    a_all = split(a_got[...].reshape(SLABS * 8, TILE))
    a_all = dot2(a_all, expand[...])
    for i in range(3):
        a_wide[i] = a_all[:, i * TILE : (i + 1) * TILE].reshape(YX, ROLES, 8, TILE)
    for copy in m_copies:
        copy.wait_recv()

    crossed = []
    for b in range(ROLES):
        sums = [zero, zero, zero]
        for k in range(YX):
            g = m_got[k, b]
            sums = [sums[i] + a_wide[i, k, b] * g for i in range(3)]
        crossed.append(jnp.concatenate(sums, axis=1))
    crossed = dot2(split(jnp.concatenate(crossed, axis=0)), sort[...])
    for b in range(ROLES):
        for k in range(ROLES):
            r_send[k, b] = crossed[b * 8 : b * 8 + 8, k * TILE : (k + 1) * TILE]
    r_copies = [
        send(r_send.at[to // ROLES, to % ROLES], r_got.at[role, team], back_sem, d, to // ROLES, place(to % ROLES, slab))
        for d, to in crew
    ]
    r_got[role, team] = r_send[role, team]
    for copy in r_copies:
        copy.wait_recv()
    joined = [(r_got[0, q] + r_got[1, q]) + (r_got[2, q] + r_got[3, q]) for q in range(ROLES)]
    joined = dot2(split(jnp.concatenate(joined, axis=1)), sort[...], NT)
    squares = jnp.zeros((WIDTH, TILE), jnp.float32)
    lift_sum = [jnp.zeros((WIDTH, WIDTH), jnp.float32)] * 3
    for k in range(8):
        rows = [joined[k : k + 1, i * TILE : (i + 1) * TILE] for i in range(3)]
        value = lift_t[:, 0:1] * rows[0] + lift_t[:, 1:2] * rows[1] + lift_t[:, 2:3] * rows[2]
        raw[k] = value
        squares = squares + value * value
        for i in range(3):
            lift_sum[i] = lift_sum[i] + (
                spectral[k] * rows[i][:, :WIDTH] + spectral[8 + k] * rows[i][:, WIDTH:]
            )
    raw_copy = fetch(1, raw, raw_out)
    left = cross_rows
    for i in range(3):
        left = left + dot(jnp.where(row_8[:, :WIDTH] == 3 + i, 1.0, 0.0), lift_sum[i], NT)
    tile = jnp.concatenate([left, proj_rows], axis=1)
    tile = tile + jnp.where((row_8 == 6) & (lane == patch), sse, 0.0)
    tile = tile + jnp.where(row_8 == 7, jnp.sum(squares, keepdims=True), 0.0)

    s_crew[role, team] = tile
    copies = [
        send(s_crew.at[role, team], s_crew.at[role, team], sc_sem, d, to // ROLES, place(to % ROLES, slab))
        for d, to in crew
    ]
    for copy in copies:
        copy.wait_recv()
    s_yx[yx] = jnp.sum(s_crew[...], axis=(0, 1))
    copies = [send(s_yx.at[yx], s_yx.at[yx], sy_sem, d, role, to_spot(to)) for d, to in spots]
    for copy in copies:
        copy.wait_recv()
    tile_out[...] = jnp.sum(s_yx[...], axis=0)

    for copy in pending:
        copy.wait_send()
    second_copy.wait()
    raw_copy.wait()
    to_after.wait_send()
    to_before.wait_send()

    @pl.when(role > 0)
    def _():
        to_below(0).wait_send()
        to_below(1).wait_send()
        corner(False, True, 0).wait_send()
        corner(False, False, 1).wait_send()

    @pl.when(role < ROLES - 1)
    def _():
        to_above(0).wait_send()
        to_above(1).wait_send()
        corner(True, True, 2).wait_send()
        corner(True, False, 3).wait_send()

    for k in range(ROLES):

        @pl.when(jnp.logical_not(home & (k == role)))
        def _():
            band_copy(k).wait_send()

    @pl.when(jnp.logical_not(home))
    def _():
        swap(0).wait_send()
        swap(1).wait_send()


def result(*shape):
    return jax.ShapeDtypeStruct(shape, jnp.float32)


def step(anchors, velocity, spectral, lift, mix, proj):
    vmem = pl.BlockSpec(memory_space=pltpu.VMEM)
    anywhere = pl.BlockSpec(memory_space=pltpu.HBM)
    dma = pltpu.SemaphoreType.DMA

    def room(*shape):
        return pltpu.VMEM(shape, jnp.float32)

    def narrow(*shape):
        return pltpu.VMEM(shape, jnp.bfloat16)

    return pl.pallas_call(
        step_kernel,
        out_shape=(result(3, PLANES, 64, TILE), result(8, WIDTH, TILE), result(8, TILE)),
        in_specs=[pl.BlockSpec(memory_space=pltpu.SMEM)] + [anywhere] * 11,
        out_specs=(anywhere, anywhere, vmem),
        scratch_shapes=[
            room(3, 12, ROWS, TILE),
            room(3, 12, ROWS, TILE),
            room(3, PLANES, 64, TILE),
            room(MODES, WIDTH, WIDTH),
            room(3, WIDTH),
            room(WIDTH, WIDTH),
            room(3, WIDTH),
            narrow(2, 256, AREA),
            narrow(2, AREA, 256),
            narrow(2, 2 * ROLES * PAIRS, 4 * SH * TILE),
            narrow(2, ROLES * 256, SH * TILE),
            narrow(TILE, 3 * TILE),
            narrow(3 * TILE, ROLES * TILE),
            room(ROLES, 8, TILE),
            room(ROLES, ROLES, 8, TILE),
            room(ROLES, YX, 3, 8, TILE),
            narrow(2, 12, 16, TILE),
            narrow(2, 12, 16, TILE),
            room(PAIRS, 8, TILE),
            room(PAIRS, 8, TILE),
            room(PAIRS, 256),
            room(ROLES, PAIRS, 256),
            room(ROLES, YX, 8, TILE),
            room(YX, ROLES, 8, TILE),
            room(3, YX, ROLES, 8, TILE),
            room(ROLES, 256, TILE),
            room(ROLES, 256, TILE),
            room(3, WIDTH, TILE),
            room(3, WIDTH, TILE),
            room(ROLES, TILE, AREA),
            room(ROLES, TILE, AREA),
            narrow(TILE, AREA),
            narrow(TILE, AREA),
            room(PAIRS, 8, AREA),
            room(PAIRS, 8, TILE),
            room(ROLES, TILE, 256),
            room(ROLES, TILE, 256),
            room(ROLES, YX, 8, TILE),
            room(YX, ROLES, 8, TILE),
            room(ROLES, ROLES, 8, TILE),
            room(ROLES, ROLES, 8, TILE),
            room(8, WIDTH, TILE),
            room(ROLES, ROLES, 8, TILE),
            room(YX, 8, TILE),
            dma((11,)),
            dma((2, 4)),
            dma((2, 2)),
            dma((2, 4)),
            dma((2, CREW)),
            dma((2, 2)),
            dma((2, YX)),
            dma((2, ROLES)),
            dma((2, ROLES)),
            dma((2, ROLES)),
            dma((2, YX)),
            dma((2, YX)),
            dma((2, CREW)),
            dma((2, CREW)),
            dma((2, YX)),
        ],
        compiler_params=pltpu.CompilerParams(
            collective_id=0, has_side_effects=True, vmem_limit_bytes=63 * 2**20
        ),
    )(anchors, velocity, spectral, lift, mix, proj, *tables())


def finish_kernel(
    second, raw, tile, lift, mix, table, second_out, loss_out, lift_out, mix_out, proj_out, spec_out, held, copy_sem
):
    fetches = [pltpu.make_async_copy(second.at[c], held.at[c], copy_sem.at[0, c]) for c in range(3)]
    stores = [pltpu.make_async_copy(held.at[c], second_out.at[c], copy_sem.at[1, c]) for c in range(3)]
    for copy in fetches:
        copy.start()

    for get, put in zip(fetches, stores):
        get.wait()
        put.start()

    def normal(total):
        mean = jnp.sum(total * total, keepdims=True) / total.size
        return total / jnp.sqrt(mean + tiny_eps)

    cross = tile[0:3, :WIDTH]
    proj_out[...] = normal(tile[0:3, WIDTH:])
    lift_out[...] = normal(tile[3:6, :WIDTH] + dot(cross, mix[...], NT))
    mix_out[...] = normal(dot(lift[...], cross, TN))
    scale = 1.0 / jnp.sqrt(tile[7:8, 0:1] / (MODES**3 * WIDTH * WIDTH) + tiny_eps)
    for k in range(8):
        value = raw[k] * scale
        spec_out[k] = value[:, :WIDTH]
        spec_out[8 + k] = value[:, WIDTH:]
    losses = tile[6:7, :] / (3.0 * PATCH**3)
    lanes = lax.broadcasted_iota(jnp.int32, (1, TILE), 1)
    found = [jnp.sum(jnp.where(lanes == table[0:1, k : k + 1], losses, 0.0), axis=1, keepdims=True) for k in range(2)]
    loss_out[...] = jnp.concatenate(found, axis=1)
    for copy in stores:
        copy.wait()


def finish(second, raw, tile, lift, mix, table):
    vmem = pl.BlockSpec(memory_space=pltpu.VMEM)
    anywhere = pl.BlockSpec(memory_space=pltpu.HBM)
    return pl.pallas_call(
        finish_kernel,
        out_shape=(
            result(3, PLANES, 64, TILE),
            result(1, 2),
            result(3, WIDTH),
            result(WIDTH, WIDTH),
            result(3, WIDTH),
            result(MODES, WIDTH, WIDTH),
        ),
        in_specs=[anywhere] + [vmem] * 5,
        out_specs=(anywhere,) + (vmem,) * 5,
        scratch_shapes=[pltpu.VMEM((3, PLANES, 64, TILE), jnp.float32), pltpu.SemaphoreType.DMA((2, 3))],
    )(second, raw, tile, lift, mix, table)


def on_device(velocity, anchors, slot_table, lift, mix, proj, spectral):
    second, raw, tile = step(anchors, velocity, spectral, lift, mix, proj)
    return finish(second, raw, tile, lift, mix, slot_table)


def solution(mesh):
    return jax.shard_map(
        on_device,
        mesh=mesh,
        in_specs=(
            P(None, "role", "slab", None),
            P("slab", None),
            P("slab", None),
            P(),
            P(),
            P(),
            P(("role", "slab"), None, None),
        ),
        out_specs=(
            P(None, "role", "slab", None),
            P("slab", None),
            P(),
            P(),
            P(),
            P(("role", "slab"), None, None),
        ),
        check_vma=False,
    )
```
